32 devices in a mesh: groups: 2 (over x), seq: 2 (over core), mp: 8 (over z, y).
Axes of the slice: x: 2, y: 2, z: 4, core: 2. Of those that a mesh axis runs over, the one named last changes fastest.
Arguments:
- tokens_in: bfloat16 [3072, 4096], P(('groups', 'seq', 'mp')), parts along dimension 0, may hold values from -6 to 6
- out_grad: bfloat16 [3072, 14336], P('groups', ('seq', 'mp')), parts along dimension 0, may hold values from -6 to 6
- w_gate: bfloat16 [4096, 14336], P(None, ('seq', 'mp')), may hold values from -0.09375 to 0.09375
- w_up: bfloat16 [4096, 14336], P(None, ('seq', 'mp')), may hold values from -0.09375 to 0.09375
- proj_in: bfloat16 [4096, 64], replicated, may hold values from -0.09375 to 0.09375
- proj_out: bfloat16 [14336, 128], P(('seq', 'mp')), may hold values from -0.046875 to 0.046875
- lengths: int32 [16], P('groups'), parts along dimension 0, may hold values from 1 to 768, 1536 in all
- val_sketch: bfloat16 [1024, 8192], P('mp', 'seq'), may hold values from -0.0625 to 0.0625
Outputs:
- scores: float32 [16, 1024], P(('groups', 'seq'), 'mp'), parts along dimension 0
The draws below stay inside these ranges and needn't reach their ends.
There are 2 independent parts, one for each index of `groups`. The reference program is written for one: setup_inputs(seed, part) draws one part's arguments, and reference() takes and returns one part's arrays. A program takes and returns all parts, laid end to end along the dimension named above; an argument that names none is the same for every part. Nothing has to cross between parts.
Inputs may be any that keep to these rules, and one draw needn't show every extreme that they name: Sequences lie end to end in token order, sequence s starting where sequence s - 1 ends; the lengths add up to 1536 and one of them is exactly 768.
All inputs are finite; a program needn't handle non-finite values.
Results may differ from the reference program's by a relative error of at most 0.003.
Values may be sent and summed in bfloat16 or wider, within the bound.
No kernel may reach another device: no remote copies, remote signals or barrier semaphores. Data moves between devices by JAX's collectives and lax.ppermute only.
A program may use at most 128 MiB of HBM per device.

```python
import math
import jax
import jax.numpy as jnp
import numpy as np
from jax import lax

D = 4096
FF = 14336
R = 64
NVAL = 1024
TOKENS = 1536
MAXLEN = 768
SEQS = 8


def levels(rng, extent, split, least, top_value):
    loudness, own = 1.0, jax.random.fold_in(rng, 6)
    for axis_at, blocks in split:
        draws = jnp.exp(jax.random.uniform(jax.random.fold_in(own, axis_at), (blocks,), jnp.float32, least / len(split), top_value / len(split)))
        loudness = loudness * jnp.repeat(draws, extent[axis_at] // blocks).reshape([-1 if axis == axis_at else 1 for axis in range(len(extent))])
    return loudness


def profile(count, total, limit, lean):
    weights = [(1 << 20) // math.isqrt(standing ** lean) + 1 for standing in range(2, count + 1)]
    surplus, holding = total - limit - (count - 1), [1] * (count - 1)
    while surplus > 0:
        movable = [i for i in range(count - 1) if holding[i] < limit]
        pool, budget = sum([weights[i] for i in movable]), surplus
        for i in movable:
            extra = min(limit - holding[i], max(1, budget * weights[i] // pool), surplus)
            holding[i] = holding[i] + extra
            surplus = surplus - extra
    return np.array([limit] + holding)


def ragged_sizes(own_key, number_of, total, bound, lean):
    if number_of == 2:
        one = jax.random.randint(own_key, (), max(1, total - bound), min(bound, total - 1) + 1)
        return jnp.stack([one, total - one])
    sizes = jnp.asarray(profile(number_of, total, bound, lean), jnp.int32)
    twos = (number_of - 1) // 2
    donor, taker = sizes[1:1 + 2 * twos:2], sizes[2:2 + 2 * twos:2]
    room = jnp.minimum(donor - 1, bound - taker)
    moved = jax.random.randint(jax.random.fold_in(own_key, 1), (twos,), 0, 1 << 20) % (room + 1)
    sizes = sizes.at[1:1 + 2 * twos:2].set(donor - moved).at[2:2 + 2 * twos:2].set(taker + moved)
    return sizes[jax.random.permutation(jax.random.fold_in(own_key, 2), number_of)]


def centred(stream_key, dims, spread, limit, cuts=(), kind=jnp.bfloat16):
    drawn = spread * jax.random.normal(stream_key, dims, jnp.float32)
    if cuts:
        drawn = drawn * levels(stream_key, dims, cuts, -0.22, 0.18)
    return jnp.clip(drawn, -limit, limit).astype(kind)


def setup_inputs(seed: int = 0, part: int = 0) -> dict:
    streams_of = jax.random.split(jax.random.key(seed), 9)
    part_splits = jax.random.split(jax.random.fold_in(streams_of[8], part), 9)
    return {
        "tokens_in": centred(part_splits[0], (TOKENS, D), 1.0, 6.0, ((0, 16),)),
        "out_grad": centred(part_splits[1], (TOKENS, FF), 1.0, 6.0, ((1, 16),)),
        "w_gate": centred(streams_of[2], (D, FF), D ** -0.5, 0.09375, ((1, 16),)),
        "w_up": centred(streams_of[3], (D, FF), D ** -0.5, 0.09375, ((1, 16),)),
        "proj_in": centred(streams_of[4], (D, R), D ** -0.5, 0.09375),
        "proj_out": centred(streams_of[5], (FF, 2 * R), FF ** -0.5, 0.046875, ((0, 16),)),
        "lengths": ragged_sizes(part_splits[6], SEQS, TOKENS, MAXLEN, 1).astype(jnp.int32),
        "val_sketch": centred(streams_of[7], (NVAL, 2 * R * R), (2 * R * R) ** -0.5, 0.0625, ((0, 8), (1, 2))),
    }


eps_scale = 1e-06

def grad_rows(block_rows, row_start, w_gate, w_up, proj_out, out_grad):
    half_cols = proj_out.shape[1] // 2
    gate_pre = jnp.dot(block_rows, w_gate, preferred_element_type=jnp.float32)
    up_pre = jnp.dot(block_rows, w_up, preferred_element_type=jnp.float32)
    cotangent = lax.dynamic_slice_in_dim(out_grad, row_start, block_rows.shape[0], 0).astype(jnp.float32)
    sigmoid_gate = jax.nn.sigmoid(gate_pre)
    grad_up = (cotangent * gate_pre * sigmoid_gate).astype(jnp.bfloat16)
    grad_gate = (cotangent * up_pre * sigmoid_gate * (1.0 + gate_pre * (1.0 - sigmoid_gate))).astype(jnp.bfloat16)
    proj_gate = jnp.dot(grad_gate, proj_out[:, :half_cols], preferred_element_type=jnp.float32)
    proj_up = jnp.dot(grad_up, proj_out[:, half_cols:], preferred_element_type=jnp.float32)
    return jnp.concatenate([proj_gate, proj_up], axis=1)

def reference(tokens_in, out_grad, w_gate, w_up, proj_in, proj_out, lengths, val_sketch):
    block_size = math.gcd(TOKENS, 512)
    num_blocks = TOKENS // block_size

    def block_grads(block_index):
        row_start = block_index * block_size
        block_rows = lax.dynamic_slice_in_dim(tokens_in, row_start, block_size, 0)
        return grad_rows(block_rows, row_start, w_gate, w_up, proj_out, out_grad)
    proj_grads = lax.map(block_grads, jnp.arange(num_blocks, dtype=jnp.int32)).reshape(TOKENS, 2 * R)
    proj_acts = jnp.dot(tokens_in, proj_in, preferred_element_type=jnp.float32)
    seq_ends = jnp.cumsum(lengths).astype(jnp.int32)
    seq_starts = (seq_ends - lengths).astype(jnp.int32)
    position = lax.iota(jnp.int32, TOKENS)
    member = ((position[:, None] >= seq_starts[None, :]) & (position[:, None] < seq_ends[None, :])).astype(jnp.float32)
    weighted = (member[:, :, None] * proj_acts[:, None, :]).reshape(TOKENS, SEQS * R)
    sketch = lax.dot_general(weighted, proj_grads, (((0,), (0,)), ((), ())), precision=lax.Precision.HIGHEST)
    layered = sketch.reshape(SEQS, R, 2, R)
    norm_scale = jnp.sqrt(lax.optimization_barrier(jnp.mean(layered * layered, axis=(1, 3))) + eps_scale)
    normed = (layered / norm_scale[:, None, :, None]).reshape(SEQS, 2 * R * R)
    return lax.dot_general(normed, val_sketch.astype(jnp.float32), (((1,), (1,)), ((), ())), precision=lax.Precision.HIGHEST)
```

```python
import functools

import jax
import jax.numpy as jnp
import numpy as np
from jax import lax
from jax.sharding import PartitionSpec as P

eps_scale = 1e-06


def ring_order(mesh):
    n = mesh.shape["mp"]
    line = list(mesh.devices[0, 0, :])
    natural = list(range(n))
    if n < 4 or not hasattr(line[0], "coords"):
        return natural
    first, third = line[0].coords, line[2].coords
    if sum(abs(a - b) for a, b in zip(first, third)) == 1:
        return natural[0::2] + natural[1::2][::-1]
    return natural


def grad_rows(rows, cotangent, w_gate, w_up, proj_out):
    half_cols = proj_out.shape[1] // 2
    gate_pre = jnp.dot(rows, w_gate, preferred_element_type=jnp.float32)
    up_pre = jnp.dot(rows, w_up, preferred_element_type=jnp.float32)
    cotangent = cotangent.astype(jnp.float32)
    sigmoid_gate = jax.nn.sigmoid(gate_pre)
    grad_up = (cotangent * gate_pre * sigmoid_gate).astype(jnp.bfloat16)
    grad_gate = (
        cotangent * up_pre * sigmoid_gate * (1.0 + gate_pre * (1.0 - sigmoid_gate))
    ).astype(jnp.bfloat16)
    proj_gate = jnp.dot(grad_gate, proj_out[:, :half_cols], preferred_element_type=jnp.float32)
    proj_up = jnp.dot(grad_up, proj_out[:, half_cols:], preferred_element_type=jnp.float32)
    return jnp.concatenate([proj_gate, proj_up], axis=1)


def shards(order, tokens_in, out_grad, w_gate, w_up, proj_in, proj_out, lengths, val_sketch):
    n = len(order)
    rows = tokens_in.shape[0]
    seq_count = lengths.shape[0]
    rank = proj_in.shape[1]
    place = np.argsort(np.array(order)).astype(np.int32)
    at = jnp.asarray(place)[lax.axis_index("mp")]
    ring = jnp.asarray(np.array(order, np.int32))
    core = lax.axis_index("seq")
    forward = [(order[i], order[(i + 1) % n]) for i in range(n)]
    backward = [(b, a) for a, b in forward]
    send_on = functools.partial(lax.ppermute, axis_name="mp", perm=forward)
    send_back = functools.partial(lax.ppermute, axis_name="mp", perm=backward)
    swap = functools.partial(lax.ppermute, axis_name="seq", perm=[(0, 1), (1, 0)])

    seq_ends = jnp.cumsum(lengths)
    seq_starts = seq_ends - lengths

    def first_row(step, of_core):
        return (of_core * n + ring[(at + step + n) % n]) * rows

    def sketch_of(blocks, starts):
        x = jnp.concatenate(blocks, axis=0) if len(blocks) > 1 else blocks[0]
        cot, position = [], []
        for b, s in zip(blocks, starts):
            cot.append(lax.dynamic_slice_in_dim(out_grad, s, b.shape[0], 0))
            position.append(s + lax.iota(jnp.int32, b.shape[0]))
        cot = jnp.concatenate(cot, axis=0)
        position = jnp.concatenate(position, axis=0)
        grads = grad_rows(x, cot, w_gate, w_up, proj_out)
        acts = jnp.dot(x, proj_in, preferred_element_type=jnp.float32)
        member = (
            (position[:, None] >= seq_starts[None, :]) & (position[:, None] < seq_ends[None, :])
        ).astype(jnp.float32)
        weighted = (member[:, :, None] * acts[:, None, :]).reshape(-1, seq_count * rank)
        return lax.dot_general(
            weighted, grads, (((0,), (0,)), ((), ())), precision=lax.Precision.HIGHEST
        )

    other_val = swap(val_sketch)
    other = swap(tokens_in)
    on, back = tokens_in, tokens_in
    total = sketch_of([tokens_in, other], [first_row(0, core), first_row(0, 1 - core)])
    for step in range(1, n // 2):
        on, back = send_on(on), send_back(back)
        blocks = [on, back, swap(on), swap(back)]
        starts = [first_row(d, c) for c in (core, 1 - core) for d in (-step, step)]
        total = total + sketch_of(blocks, starts)
    half = rows // 2
    on, back = send_on(on[:half]), send_back(back[half:])
    blocks = [on, back, swap(on), swap(back)]
    starts = [
        first_row(n // 2, c) + d for c in (core, 1 - core) for d in (0, half)
    ]
    total = total + sketch_of(blocks, starts)

    own = seq_count // 2
    total = total.reshape(2, own, rank, 2 * rank)
    kept = lax.dynamic_index_in_dim(total, core, 0, keepdims=False)
    sent = lax.dynamic_index_in_dim(total, 1 - core, 0, keepdims=False)
    sketch = kept + swap(sent)
    bit = 1
    while bit < n:
        sketch = sketch + lax.ppermute(sketch, "mp", [(i, i ^ bit) for i in range(n)])
        bit *= 2
    layered = sketch.reshape(own, rank, 2, rank)
    norm_scale = jnp.sqrt(jnp.mean(layered * layered, axis=(1, 3)) + eps_scale)
    normed = (layered / norm_scale[:, None, :, None]).reshape(own, 2 * rank * rank)
    low = jnp.where(core == 0, val_sketch, other_val)
    high = jnp.where(core == 0, other_val, val_sketch)
    full_val = jnp.concatenate([low, high], axis=1)
    return lax.dot_general(
        normed,
        full_val.astype(jnp.float32),
        (((1,), (1,)), ((), ())),
        precision=lax.Precision.HIGHEST,
    )


def solution(mesh):
    in_specs = (
        P(("groups", "seq", "mp"), None),
        P("groups", ("seq", "mp")),
        P(None, ("seq", "mp")),
        P(None, ("seq", "mp")),
        P(),
        P(("seq", "mp"), None),
        P("groups"),
        P("mp", "seq"),
    )
    out_specs = P(("groups", "seq"), "mp")
    return jax.shard_map(
        functools.partial(shards, ring_order(mesh)),
        mesh=mesh,
        in_specs=in_specs,
        out_specs=out_specs,
        check_vma=False,
    )
```

```python
import functools

import jax
import jax.numpy as jnp
import numpy as np
from jax import lax
from jax.experimental import pallas as pl
from jax.experimental.pallas import tpu as pltpu
from jax.sharding import PartitionSpec as P

eps_scale = 1e-06
LANES = 128


def ring_order(mesh):
    n = mesh.shape["mp"]
    line = list(mesh.devices[0, 0, :])
    natural = list(range(n))
    if n < 4 or not hasattr(line[0], "coords"):
        return natural
    first, third = line[0].coords, line[2].coords
    if sum(abs(a - b) for a, b in zip(first, third)) == 1:
        return natural[0::2] + natural[1::2][::-1]
    return natural


def grad_rows(rows, cotangent, w_gate, w_up, proj_out):
    half_cols = proj_out.shape[1] // 2
    gate_pre = jnp.dot(rows, w_gate, preferred_element_type=jnp.float32)
    up_pre = jnp.dot(rows, w_up, preferred_element_type=jnp.float32)
    cotangent = cotangent.astype(jnp.float32)
    sigmoid_gate = jax.nn.sigmoid(gate_pre)
    grad_up = (cotangent * gate_pre * sigmoid_gate).astype(jnp.bfloat16)
    grad_gate = (
        cotangent * up_pre * sigmoid_gate * (1.0 + gate_pre * (1.0 - sigmoid_gate))
    ).astype(jnp.bfloat16)
    proj_gate = jnp.dot(grad_gate, proj_out[:, :half_cols], preferred_element_type=jnp.float32)
    proj_up = jnp.dot(grad_up, proj_out[:, half_cols:], preferred_element_type=jnp.float32)
    return jnp.concatenate([proj_gate, proj_up], axis=1)


def plain_sketch(blocks, starts, out_grad, w_gate, w_up, proj_in, proj_out, seq_starts, seq_ends):
    x = jnp.concatenate(blocks, axis=0)
    cot, position = [], []
    for b, s in zip(blocks, starts):
        cot.append(lax.dynamic_slice_in_dim(out_grad, s, b.shape[0], 0))
        position.append(s + lax.iota(jnp.int32, b.shape[0]))
    position = jnp.concatenate(position, axis=0)
    grads = grad_rows(x, jnp.concatenate(cot, axis=0), w_gate, w_up, proj_out)
    acts = jnp.dot(x, proj_in, preferred_element_type=jnp.float32)
    member = (
        (position[:, None] >= seq_starts[None, :]) & (position[:, None] < seq_ends[None, :])
    ).astype(jnp.float32)
    weighted = (member[:, :, None] * acts[:, None, :]).reshape(x.shape[0], -1)
    return lax.dot_general(
        weighted, grads, (((0,), (0,)), ((), ())), precision=lax.Precision.HIGHEST
    )


def step_kernel(block_rows, first, starts, bounds, *refs):
    count = len(block_rows)
    blocks = refs[:count]
    w_gate, w_up, out_grad, proj_in, proj_out = refs[count : count + 5]
    at = count + 5
    before = None if first else refs[at]
    at += 0 if first else 1
    after, x, w, cot, w_sem, x_sem, cot_sem = refs[at:]
    tiles = w.shape[0]
    seq_count = bounds.shape[1]

    row, x_copies, cot_copies, rows_at = 0, [], [], []
    for i, r in enumerate(block_rows):
        x_copies.append(
            pltpu.make_async_copy(blocks[i], x.at[pl.ds(row, r)], x_sem.at[i])
        )
        source = out_grad.at[pl.ds(pl.multiple_of(starts[i], 16), r)]
        cot_copies.append(pltpu.make_async_copy(source, cot.at[pl.ds(row, r)], cot_sem.at[i]))
        rows_at.append(row)
        row += r
    w_copies = []
    for t in range(tiles):
        columns = pl.ds(t * LANES, LANES)
        w_copies.append(
            (
                pltpu.make_async_copy(
                    w_gate.at[:, columns], w.at[t, :, pl.ds(0, LANES)], w_sem.at[t, 0]
                ),
                pltpu.make_async_copy(
                    w_up.at[:, columns], w.at[t, :, pl.ds(LANES, LANES)], w_sem.at[t, 1]
                ),
            )
        )
    for copy in x_copies:
        copy.start()
    for copy in w_copies[0]:
        copy.start()
    for copy in cot_copies:
        copy.start()
    for pair in w_copies[1:]:
        for copy in pair:
            copy.start()

    for copy in x_copies:
        copy.wait()
    acts = jnp.dot(x[...], proj_in[...], preferred_element_type=jnp.float32)

    grads = jnp.zeros((row, LANES), jnp.float32)
    for t in range(tiles):
        for copy in w_copies[t]:
            copy.wait()
        if t == 0:
            for copy in cot_copies:
                copy.wait()
        pre = jnp.dot(x[...], w[t], preferred_element_type=jnp.float32)
        gate, up = pre[:, :LANES], pre[:, LANES:]
        cotangent = cot[:, t * LANES : (t + 1) * LANES].astype(jnp.float32)
        sig = 1.0 / (1.0 + jnp.exp(-gate))
        scaled = cotangent * sig
        grad_up = (scaled * gate).astype(jnp.bfloat16)
        grad_gate = (scaled * up * (1.0 + gate * (1.0 - sig))).astype(jnp.bfloat16)
        both = jnp.concatenate([grad_gate, grad_up], axis=1)
        grads += jnp.dot(both, proj_out[t], preferred_element_type=jnp.float32)

    position = []
    for i, r in enumerate(block_rows):
        position.append(starts[i] + lax.broadcasted_iota(jnp.int32, (r, LANES), 0))
    position = jnp.concatenate(position, axis=0)
    low = lax.broadcasted_iota(jnp.int32, (1, LANES), 1) < LANES // 2
    for g in range(seq_count // 2):
        begin = jnp.where(low, bounds[0, 2 * g], bounds[0, 2 * g + 1])
        end = jnp.where(low, bounds[1, 2 * g], bounds[1, 2 * g + 1])
        weighted = jnp.where((position >= begin) & (position < end), acts, 0.0)
        part = lax.dot_general(
            weighted,
            grads,
            (((0,), (0,)), ((), ())),
            precision=lax.Precision.HIGHEST,
            preferred_element_type=jnp.float32,
        )
        here = slice(g * LANES, (g + 1) * LANES)
        after[here, :] = part if first else before[here, :] + part


def kernel_sketch(blocks, starts, bounds, total, out_grad, w_gate, w_up, proj_in, proj_out):
    block_rows = [b.shape[0] for b in blocks]
    rows, width = sum(block_rows), blocks[0].shape[1]
    hidden = w_gate.shape[1]
    tiles = hidden // LANES
    first = total is None
    out_rows = bounds.shape[1] * LANES // 2
    anywhere = pl.BlockSpec(memory_space=pl.ANY)
    vmem = pl.BlockSpec(memory_space=pltpu.VMEM)
    smem = pl.BlockSpec(memory_space=pltpu.SMEM)
    operands = [jnp.stack(starts), bounds, *blocks, w_gate, w_up, out_grad, proj_in, proj_out]
    specs = [smem, smem] + [anywhere] * (len(blocks) + 3) + [vmem, vmem]
    if not first:
        operands.append(total)
        specs.append(vmem)
    return pl.pallas_call(
        functools.partial(step_kernel, block_rows, first),
        out_shape=jax.ShapeDtypeStruct((out_rows, LANES), jnp.float32),
        in_specs=specs,
        out_specs=vmem,
        scratch_shapes=[
            pltpu.VMEM((rows, width), jnp.bfloat16),
            pltpu.VMEM((tiles, width, 2 * LANES), jnp.bfloat16),
            pltpu.VMEM((rows, hidden), jnp.bfloat16),
            pltpu.SemaphoreType.DMA((tiles, 2)),
            pltpu.SemaphoreType.DMA((len(blocks),)),
            pltpu.SemaphoreType.DMA((len(blocks),)),
        ],
        compiler_params=pltpu.CompilerParams(vmem_limit_bytes=40 * 2**20),
        cost_estimate=pl.CostEstimate(
            flops=2 * rows * width * (2 * hidden + 2 * LANES),
            bytes_accessed=2 * (rows + 2 * hidden) * width,
            transcendentals=0,
        ),
    )(*operands)


def shards(order, tokens_in, out_grad, w_gate, w_up, proj_in, proj_out, lengths, val_sketch):
    n = len(order)
    rows, width = tokens_in.shape
    hidden = w_gate.shape[1]
    seq_count = lengths.shape[0]
    rank = proj_in.shape[1]
    place = np.argsort(np.array(order)).astype(np.int32)
    at = jnp.asarray(place)[lax.axis_index("mp")]
    ring = jnp.asarray(np.array(order, np.int32))
    core = lax.axis_index("seq")
    forward = [(order[i], order[(i + 1) % n]) for i in range(n)]
    backward = [(b, a) for a, b in forward]
    send_on = functools.partial(lax.ppermute, axis_name="mp", perm=forward)
    send_back = functools.partial(lax.ppermute, axis_name="mp", perm=backward)
    swap = functools.partial(lax.ppermute, axis_name="seq", perm=[(0, 1), (1, 0)])

    seq_ends = jnp.cumsum(lengths)
    seq_starts = seq_ends - lengths

    def first_row(step, of_core):
        return (of_core * n + ring[(at + step + n) % n]) * rows

    in_kernel = (
        rows % 32 == 0
        and hidden % LANES == 0
        and width % LANES == 0
        and 2 * rank == LANES
        and seq_count % 2 == 0
    )
    if in_kernel:
        bounds = jnp.stack([seq_starts, seq_ends])
        twice = jnp.concatenate([proj_in, proj_in], axis=1)
        tiled = proj_out.reshape(hidden // LANES, LANES, 2 * rank)
        left = lax.broadcasted_iota(jnp.int32, tiled.shape, 2) < rank
        none = jnp.zeros((), tiled.dtype)
        diagonal = jnp.concatenate(
            [jnp.where(left, tiled, none), jnp.where(left, none, tiled)], axis=1
        )

    def add_sketch(total, blocks, starts):
        if in_kernel:
            return kernel_sketch(
                blocks, starts, bounds, total, out_grad, w_gate, w_up, twice, diagonal
            )
        part = plain_sketch(
            blocks, starts, out_grad, w_gate, w_up, proj_in, proj_out, seq_starts, seq_ends
        )
        return part if total is None else total + part

    half = rows // 2
    other_val = swap(val_sketch)
    other = swap(tokens_in)
    on_a, on_b = tokens_in[:half], tokens_in[half:]
    back_a, back_b = on_a, on_b
    total = add_sketch(None, [tokens_in, other], [first_row(0, core), first_row(0, 1 - core)])
    for step in range(1, n // 2 + 1):
        last = step == n // 2
        on_a, back_b = send_on(on_a), send_back(back_b)
        blocks = [on_a, back_b]
        where = [(-step, 0), (step, half)]
        if not last:
            on_b, back_a = send_on(on_b), send_back(back_a)
            blocks += [on_b, back_a]
            where += [(-step, half), (step, 0)]
        blocks += [swap(b) for b in blocks]
        starts = [first_row(d, c) + h for c in (core, 1 - core) for d, h in where]
        total = add_sketch(total, blocks, starts)

    own = seq_count // 2
    total = total.reshape(2, own, rank, 2 * rank)
    kept = lax.dynamic_index_in_dim(total, core, 0, keepdims=False)
    sent = lax.dynamic_index_in_dim(total, 1 - core, 0, keepdims=False)
    sketch = kept + swap(sent)
    bit = 1
    while bit < n:
        sketch = sketch + lax.ppermute(sketch, "mp", [(i, i ^ bit) for i in range(n)])
        bit *= 2
    layered = sketch.reshape(own, rank, 2, rank)
    norm_scale = jnp.sqrt(jnp.mean(layered * layered, axis=(1, 3)) + eps_scale)
    normed = (layered / norm_scale[:, None, :, None]).reshape(own, 2 * rank * rank)
    low = jnp.where(core == 0, val_sketch, other_val)
    high = jnp.where(core == 0, other_val, val_sketch)
    full_val = jnp.concatenate([low, high], axis=1)
    return lax.dot_general(
        normed,
        full_val.astype(jnp.float32),
        (((1,), (1,)), ((), ())),
        precision=lax.Precision.HIGHEST,
    )


def solution(mesh):
    in_specs = (
        P(("groups", "seq", "mp"), None),
        P("groups", ("seq", "mp")),
        P(None, ("seq", "mp")),
        P(None, ("seq", "mp")),
        P(),
        P(("seq", "mp"), None),
        P("groups"),
        P("mp", "seq"),
    )
    out_specs = P(("groups", "seq"), "mp")
    return jax.shard_map(
        functools.partial(shards, ring_order(mesh)),
        mesh=mesh,
        in_specs=in_specs,
        out_specs=out_specs,
        check_vma=False,
    )
```

```python
import functools

import jax
import jax.numpy as jnp
import numpy as np
from jax import lax
from jax.experimental import pallas as pl
from jax.experimental.pallas import tpu as pltpu
from jax.sharding import PartitionSpec as P

eps_scale = 1e-06
LANES = 128
CHUNK = 32
ANY = pl.BlockSpec(memory_space=pl.ANY)
VMEM = pl.BlockSpec(memory_space=pltpu.VMEM)
SMEM = pl.BlockSpec(memory_space=pltpu.SMEM)


def ring_order(mesh):
    n = mesh.shape["mp"]
    line = list(mesh.devices[0, 0, :])
    natural = list(range(n))
    if n < 4 or not hasattr(line[0], "coords"):
        return natural
    first, third = line[0].coords, line[2].coords
    if sum(abs(a - b) for a, b in zip(first, third)) == 1:
        return natural[0::2] + natural[1::2][::-1]
    return natural


def ring_table(order, rows):
    n = len(order)
    table = []
    for core in range(2):
        for m in range(n):
            p, sign = order.index(m), 1 - 2 * core

            def row(c, shift):
                return (c * n + order[(p + shift) % n]) * rows

            line = [row(core, 0), row(1 - core, 0)]
            for k in range(1, n // 2):
                line += [row(core, -sign * k), row(core, sign * k)]
                line += [row(1 - core, sign * k), row(1 - core, -sign * k)]
            line += [row(core, n // 2), row(1 - core, n // 2), core]
            table.append(line)
    return np.array(table, np.int32)


def fill_weights(w_gate, w_up, proj_in, proj_out, w, diagonal, sems):
    hidden = w_gate.shape[1]
    copies = [
        pltpu.make_async_copy(w_gate, w.at[:, pl.ds(0, hidden)], sems.at[0]),
        pltpu.make_async_copy(w_up, w.at[:, pl.ds(hidden, hidden)], sems.at[1]),
    ]
    for copy in copies:
        copy.start()
    w[:, 2 * hidden :] = jnp.concatenate([proj_in[...], proj_in[...]], axis=1)
    values = proj_out[...]
    left = lax.broadcasted_iota(jnp.int32, values.shape, 1) < LANES // 2
    none = jnp.zeros_like(values)
    diagonal[:hidden, :] = jnp.where(left, values, none)
    diagonal[hidden:, :] = jnp.where(left, none, values)
    return copies


def split(value):
    high = value.astype(jnp.bfloat16)
    return high, (value - high.astype(jnp.float32)).astype(jnp.bfloat16)


def step_kernel(count, place, first, last, table, lengths, *refs):
    blocks = refs[:count]
    out_grad, at = refs[count], count + 1
    if first:
        weights, at = refs[at : at + 4], at + 4
    else:
        (before, w, diagonal), at = refs[at : at + 3], at + 3
    outs, at = (refs[at : at + 2], at + 2) if last else (refs[at : at + 1], at + 1)
    if first:
        (w, diagonal), at = refs[at : at + 2], at + 2
    x, cot, pre, both, x_sem, cot_sem, w_sem = refs[at:]
    rows = blocks[0].shape[0]
    total_rows = rows * count
    hidden = out_grad.shape[1]
    seq_count = lengths.shape[0]

    x_copies, cot_copies, starts = [], [], []
    for i in range(count):
        here = pl.ds(i * rows, rows)
        starts.append(table[place + i])
        source = out_grad.at[pl.ds(pl.multiple_of(starts[i], 16), rows)]
        x_copies.append(pltpu.make_async_copy(blocks[i], x.at[here], x_sem.at[i]))
        cot_copies.append(pltpu.make_async_copy(source, cot.at[here], cot_sem.at[i]))
    for copy in x_copies + cot_copies:
        copy.start()
    if first:
        for copy in fill_weights(*weights, w, diagonal, w_sem):
            copy.wait()
    for copy in x_copies:
        copy.wait()
    pre[...] = jnp.dot(x[...], w[...], preferred_element_type=jnp.float32)
    for copy in cot_copies:
        copy.wait()

    def chunk(i, _):
        here = pl.ds(pl.multiple_of(i * CHUNK, CHUNK), CHUNK)
        gate = pre[here, :hidden]
        up = pre[here, hidden : 2 * hidden]
        cotangent = cot[here, :].astype(jnp.float32)
        sig = 0.5 * (1.0 + jnp.tanh(0.5 * gate))
        scaled = cotangent * sig
        both[here, hidden:] = (scaled * gate).astype(jnp.bfloat16)
        both[here, :hidden] = (scaled * up * (1.0 + gate * (1.0 - sig))).astype(jnp.bfloat16)
        return 0

    lax.fori_loop(0, total_rows // CHUNK, chunk, 0)
    grads = jnp.dot(both[...], diagonal[...], preferred_element_type=jnp.float32)
    grads_high, grads_low = split(grads)
    grads_both = jnp.concatenate([grads_high, grads_low], axis=1)

    acts = pre[:, 2 * hidden :]
    position = []
    for i in range(count):
        position.append(starts[i] + lax.broadcasted_iota(jnp.int32, (rows, LANES), 0))
    position = jnp.concatenate(position, axis=0)
    low = lax.broadcasted_iota(jnp.int32, (1, LANES), 1) < LANES // 2
    ends = []
    for s in range(seq_count):
        ends.append(lengths[s] + (ends[-1] if s else 0))
    groups = seq_count // 2
    highs, lows = [], []
    for g in range(groups):
        begin = jnp.where(low, ends[2 * g - 1] if g else 0, ends[2 * g])
        end = jnp.where(low, ends[2 * g], ends[2 * g + 1])
        weighted = jnp.where((position >= begin) & (position < end), acts, 0.0)
        high, rest = split(weighted)
        highs.append(high)
        lows.append(rest)
    over_rows = (((0,), (0,)), ((), ()))
    main = lax.dot_general(
        jnp.concatenate(highs, axis=1),
        grads_both,
        over_rows,
        preferred_element_type=jnp.float32,
    )
    rest = lax.dot_general(
        jnp.concatenate(lows, axis=1), grads_high, over_rows, preferred_element_type=jnp.float32
    )
    part = main[:, :LANES] + main[:, LANES:] + rest
    if not first:
        part += before[...]
    if not last:
        outs[0][...] = part
        return
    kept, sent = outs
    core = table[table.shape[0] - 1]
    half = part.shape[0] // 2
    upper, lower = part[:half, :], part[half:, :]
    kept[...] = jnp.where(core == 0, upper, lower)
    sent[...] = jnp.where(core == 0, lower, upper)


def step_sketch(blocks, place, state, table, lengths, out_grad, weights, last=False):
    count = len(blocks)
    rows, width = blocks[0].shape
    total_rows = count * rows
    hidden = out_grad.shape[1]
    columns = 2 * hidden + LANES
    first = state is None
    out_rows = lengths.shape[0] * LANES // 2
    operands = [table, lengths, *blocks, out_grad]
    specs = [SMEM, SMEM] + [ANY] * (count + 1)
    if first:
        operands += weights
        specs += [ANY, ANY, VMEM, VMEM]
    else:
        operands += state
        specs += [VMEM, VMEM, VMEM]
    out_shape = [jax.ShapeDtypeStruct((out_rows, LANES), jnp.float32)]
    if last:
        out_shape = [jax.ShapeDtypeStruct((out_rows // 2, LANES), jnp.float32)] * 2
    if first:
        out_shape += [
            pltpu.VMEM((width, columns), jnp.bfloat16),
            jax.ShapeDtypeStruct((2 * hidden, LANES), jnp.bfloat16),
        ]
    outs = pl.pallas_call(
        functools.partial(step_kernel, count, place, first, last),
        out_shape=out_shape,
        in_specs=specs,
        out_specs=[VMEM] * len(out_shape),
        scratch_shapes=[
            pltpu.VMEM((total_rows, width), jnp.bfloat16),
            pltpu.VMEM((total_rows, hidden), jnp.bfloat16),
            pltpu.VMEM((total_rows, columns), jnp.float32),
            pltpu.VMEM((total_rows, 2 * hidden), jnp.bfloat16),
            pltpu.SemaphoreType.DMA((count,)),
            pltpu.SemaphoreType.DMA((count,)),
            pltpu.SemaphoreType.DMA((2,)),
        ],
        compiler_params=pltpu.CompilerParams(vmem_limit_bytes=32 * 2**20),
        cost_estimate=pl.CostEstimate(
            flops=4 * total_rows * width * columns,
            bytes_accessed=2 * total_rows * width,
            transcendentals=0,
        ),
    )(*operands)
    return outs if first or last else [*outs, *state[1:]]


def score_kernel(table, mine, theirs, val_own, val_other, scores, sketch):
    core = table[table.shape[0] - 1]
    sketch[...] = mine[...] + theirs[...]
    own, rank = scores.shape[0], sketch.shape[0] // scores.shape[0]
    half = rank // 2
    left = lax.broadcasted_iota(jnp.int32, (own, LANES), 1) < LANES // 2
    squares = jnp.zeros((own, LANES), jnp.float32)
    found = jnp.zeros((4 * own, scores.shape[1]), jnp.float32)
    for side, val in ((core, val_own), (1 - core, val_other)):
        gates, ups = [], []
        for a in range(half):
            slab = sketch[pl.ds(side * half + a, own, stride=rank), :]
            squares += slab * slab
            gates.append(jnp.where(left, slab, 0.0))
            ups.append(jnp.where(left, 0.0, slab))
        gate_high, gate_low = split(jnp.concatenate(gates, axis=1))
        up_high, up_low = split(jnp.concatenate(ups, axis=1))
        found += lax.dot_general(
            jnp.concatenate([gate_high, gate_low, up_high, up_low], axis=0),
            val[...],
            (((1,), (1,)), ((), ())),
            preferred_element_type=jnp.float32,
        )
    count = rank * LANES // 2
    gate_mean = jnp.sum(jnp.where(left, squares, 0.0), axis=1, keepdims=True) / count
    up_mean = jnp.sum(jnp.where(left, 0.0, squares), axis=1, keepdims=True) / count
    gate_part = found[:own] + found[own : 2 * own]
    up_part = found[2 * own : 3 * own] + found[3 * own :]
    scores[...] = gate_part / jnp.sqrt(gate_mean + eps_scale) + up_part / jnp.sqrt(
        up_mean + eps_scale
    )


def score(table, mine, theirs, val_own, val_other, own):
    return pl.pallas_call(
        score_kernel,
        out_shape=jax.ShapeDtypeStruct((own, val_own.shape[0]), jnp.float32),
        in_specs=[SMEM, VMEM, VMEM, VMEM, VMEM],
        out_specs=VMEM,
        scratch_shapes=[pltpu.VMEM(mine.shape, jnp.float32)],
        compiler_params=pltpu.CompilerParams(vmem_limit_bytes=16 * 2**20),
    )(table, mine, theirs, val_own, val_other)


def fast(order, tokens_in, out_grad, w_gate, w_up, proj_in, proj_out, lengths, val_sketch):
    n = len(order)
    rows = tokens_in.shape[0]
    seq_count = lengths.shape[0]
    table = ring_table(order, rows)
    device = lax.axis_index("seq") * n + lax.axis_index("mp")
    table = lax.dynamic_index_in_dim(jnp.asarray(table), device, 0, keepdims=False)
    ahead = [(order[i], order[(i + 1) % n]) for i in range(n)]
    one = ahead + [(n + b, n + a) for a, b in ahead]
    send_one = functools.partial(lax.ppermute, axis_name=("seq", "mp"), perm=one)
    send_two = functools.partial(
        lax.ppermute, axis_name=("seq", "mp"), perm=[(b, a) for a, b in one]
    )
    swap = functools.partial(lax.ppermute, axis_name="seq", perm=[(0, 1), (1, 0)])

    add = functools.partial(
        step_sketch,
        table=table,
        lengths=lengths,
        out_grad=out_grad,
        weights=[w_gate, w_up, proj_in, proj_out],
    )
    one_way, two_way = send_one(tokens_in), send_two(tokens_in)
    other = swap(tokens_in)
    other_val = swap(val_sketch)
    total, *weights = add([tokens_in, other], 0, None)
    place = 2
    for k in range(1, n // 2):
        one_way, two_way, total, other_val = lax.optimization_barrier(
            (one_way, two_way, total, other_val)
        )
        next_one = send_one(one_way)
        next_two = send_two(two_way) if k + 1 < n // 2 else None
        blocks = [one_way, two_way, swap(one_way), swap(two_way)]
        total = add(blocks, place, [total, *weights])[0]
        place += 4
        one_way, two_way = next_one, next_two
    one_way, total = lax.optimization_barrier((one_way, total))
    kept, sent = add([one_way, swap(one_way)], place, [total, *weights], last=True)

    mine, theirs = kept, swap(sent)
    bit = 1
    while bit < n:
        mine = mine + theirs
        pairs = [(i, i ^ bit) for i in range(n)]
        theirs = lax.ppermute(mine.astype(jnp.bfloat16), "mp", pairs).astype(jnp.float32)
        bit *= 2
    return score(table, mine, theirs, val_sketch, other_val, seq_count // 2)


def grad_rows(rows, cotangent, w_gate, w_up, proj_out):
    half_cols = proj_out.shape[1] // 2
    gate_pre = jnp.dot(rows, w_gate, preferred_element_type=jnp.float32)
    up_pre = jnp.dot(rows, w_up, preferred_element_type=jnp.float32)
    cotangent = cotangent.astype(jnp.float32)
    sigmoid_gate = jax.nn.sigmoid(gate_pre)
    grad_up = (cotangent * gate_pre * sigmoid_gate).astype(jnp.bfloat16)
    grad_gate = (
        cotangent * up_pre * sigmoid_gate * (1.0 + gate_pre * (1.0 - sigmoid_gate))
    ).astype(jnp.bfloat16)
    proj_gate = jnp.dot(grad_gate, proj_out[:, :half_cols], preferred_element_type=jnp.float32)
    proj_up = jnp.dot(grad_up, proj_out[:, half_cols:], preferred_element_type=jnp.float32)
    return jnp.concatenate([proj_gate, proj_up], axis=1)


def plain(order, tokens_in, out_grad, w_gate, w_up, proj_in, proj_out, lengths, val_sketch):
    n = len(order)
    rows = tokens_in.shape[0]
    seq_count = lengths.shape[0]
    rank = proj_in.shape[1]
    x = lax.all_gather(tokens_in, ("seq", "mp"), axis=0, tiled=True)
    grads = grad_rows(x, out_grad, w_gate, w_up, proj_out)
    acts = jnp.dot(x, proj_in, preferred_element_type=jnp.float32)
    ends = jnp.cumsum(lengths)
    position = lax.iota(jnp.int32, x.shape[0])[:, None]
    member = ((position >= (ends - lengths)[None, :]) & (position < ends[None, :])).astype(
        jnp.float32
    )
    weighted = (member[:, :, None] * acts[:, None, :]).reshape(x.shape[0], seq_count * rank)
    sketch = lax.dot_general(
        weighted, grads, (((0,), (0,)), ((), ())), precision=lax.Precision.HIGHEST
    )
    sketch = lax.psum(sketch, ("seq", "mp"))
    own = seq_count // lax.axis_size("seq")
    layered = sketch.reshape(seq_count, rank, 2, rank)
    layered = lax.dynamic_slice_in_dim(layered, lax.axis_index("seq") * own, own, 0)
    norm_scale = jnp.sqrt(jnp.mean(layered * layered, axis=(1, 3)) + eps_scale)
    normed = (layered / norm_scale[:, None, :, None]).reshape(own, 2 * rank * rank)
    full_val = lax.all_gather(val_sketch, "seq", axis=1, tiled=True)
    return lax.dot_general(
        normed,
        full_val.astype(jnp.float32),
        (((1,), (1,)), ((), ())),
        precision=lax.Precision.HIGHEST,
    )


def shards(order, tokens_in, out_grad, w_gate, w_up, proj_in, proj_out, lengths, val_sketch):
    n = len(order)
    rows, width = tokens_in.shape
    fits = (
        n >= 2
        and n & (n - 1) == 0
        and lax.axis_size("seq") == 2
        and rows % CHUNK == 0
        and w_gate.shape[1] % LANES == 0
        and width % LANES == 0
        and 2 * proj_in.shape[1] == LANES
        and lengths.shape[0] % 4 == 0
        and val_sketch.shape[1] == proj_in.shape[1] * LANES // 2
    )
    work = fast if fits else plain
    return work(
        order, tokens_in, out_grad, w_gate, w_up, proj_in, proj_out, lengths, val_sketch
    )


def solution(mesh):
    in_specs = (
        P(("groups", "seq", "mp"), None),
        P("groups", ("seq", "mp")),
        P(None, ("seq", "mp")),
        P(None, ("seq", "mp")),
        P(),
        P(("seq", "mp"), None),
        P("groups"),
        P("mp", "seq"),
    )
    out_specs = P(("groups", "seq"), "mp")
    return jax.shard_map(
        functools.partial(shards, ring_order(mesh)),
        mesh=mesh,
        in_specs=in_specs,
        out_specs=out_specs,
        check_vma=False,
    )
```

```python
import functools

import jax
import jax.numpy as jnp
import numpy as np
from jax import lax
from jax.experimental import pallas as pl
from jax.experimental.pallas import tpu as pltpu
from jax.sharding import PartitionSpec as P

eps_scale = 1e-06
LANES = 128
CHUNK = 32
ANY = pl.BlockSpec(memory_space=pl.ANY)
VMEM = pl.BlockSpec(memory_space=pltpu.VMEM)
SMEM = pl.BlockSpec(memory_space=pltpu.SMEM)


def ring_order(mesh):
    n = mesh.shape["mp"]
    line = list(mesh.devices[0, 0, :])
    natural = list(range(n))
    if n < 4 or not hasattr(line[0], "coords"):
        return natural
    first, third = line[0].coords, line[2].coords
    if sum(abs(a - b) for a, b in zip(first, third)) == 1:
        return natural[0::2] + natural[1::2][::-1]
    return natural


def ring_table(order, rows):
    n = len(order)
    table = []
    for core in range(2):
        for m in range(n):
            p, sign = order.index(m), 1 - 2 * core

            def row(c, shift):
                return (c * n + order[(p + shift) % n]) * rows

            line = [row(core, 0), row(1 - core, 0)]
            for k in range(1, n // 2):
                line += [row(core, -sign * k), row(1 - core, sign * k)]
                line += [row(core, sign * k), row(1 - core, -sign * k)]
            line += [row(core, n // 2), row(1 - core, n // 2), core]
            table.append(line)
    return np.array(table, np.int32)


def prepare_kernel(w_gate, w_up, out_grad, proj_in, proj_out, twice, diagonal):
    twice[...] = jnp.concatenate([proj_in[...], proj_in[...]], axis=1)
    values = proj_out[...]
    hidden = values.shape[0]
    left = lax.broadcasted_iota(jnp.int32, values.shape, 1) < LANES // 2
    none = jnp.zeros_like(values)
    diagonal[:hidden, :] = jnp.where(left, values, none)
    diagonal[hidden:, :] = jnp.where(left, none, values)


def prepare(w_gate, w_up, out_grad, proj_in, proj_out):
    width, hidden = w_gate.shape
    return pl.pallas_call(
        prepare_kernel,
        out_shape=[
            jax.ShapeDtypeStruct((width, LANES), proj_in.dtype),
            jax.ShapeDtypeStruct((2 * hidden, LANES), proj_out.dtype),
        ],
        in_specs=[VMEM] * 5,
        out_specs=[VMEM] * 2,
        compiler_params=pltpu.CompilerParams(vmem_limit_bytes=16 * 2**20),
    )(w_gate, w_up, out_grad, proj_in, proj_out)


def split(value):
    high = value.astype(jnp.bfloat16)
    return high, (value - high.astype(jnp.float32)).astype(jnp.bfloat16)


def step_kernel(count, entry, first, last, table, lengths, *refs):
    blocks = refs[:count]
    out_grad, w_gate, w_up, twice, diagonal = refs[count : count + 5]
    at = count + 5
    if not first:
        before, at = refs[at], at + 1
    outs, (pre, both) = refs[at:-2], refs[-2:]
    rows = blocks[0].shape[0]
    total_rows = rows * count
    hidden = out_grad.shape[1]
    seq_count = lengths.shape[0]
    starts = [table[entry + i] for i in range(count)]

    for place, w in ((0, w_gate), (hidden, w_up), (2 * hidden, twice)):
        x = jnp.concatenate([block[...] for block in blocks], axis=0)
        pre[:, place : place + w.shape[1]] = jnp.dot(
            x, w[...], preferred_element_type=jnp.float32
        )
    for i in range(total_rows // CHUNK):
        here = slice(i * CHUNK, (i + 1) * CHUNK)
        block, row = divmod(i * CHUNK, rows)
        source = pl.ds(pl.multiple_of(starts[block] + row, CHUNK), CHUNK)
        gate = pre[here, :hidden]
        up = pre[here, hidden : 2 * hidden]
        cotangent = out_grad[source, :].astype(jnp.float32)
        sig = 0.5 * (1.0 + jnp.tanh(0.5 * gate))
        scaled = cotangent * sig
        both[here, hidden:] = (scaled * gate).astype(jnp.bfloat16)
        both[here, :hidden] = (scaled * up * (1.0 + gate * (1.0 - sig))).astype(jnp.bfloat16)
    grads = jnp.dot(both[...], diagonal[...], preferred_element_type=jnp.float32)
    grads_high, grads_low = split(grads)
    grads_both = jnp.concatenate([grads_high, grads_low], axis=1)

    acts = pre[:, 2 * hidden :]
    position = []
    for i in range(count):
        position.append(starts[i] + lax.broadcasted_iota(jnp.int32, (rows, LANES), 0))
    position = jnp.concatenate(position, axis=0)
    low = lax.broadcasted_iota(jnp.int32, (1, LANES), 1) < LANES // 2
    ends = []
    for s in range(seq_count):
        ends.append(lengths[s] + (ends[-1] if s else 0))
    highs, lows = [], []
    for g in range(seq_count // 2):
        begin = jnp.where(low, ends[2 * g - 1] if g else 0, ends[2 * g])
        end = jnp.where(low, ends[2 * g], ends[2 * g + 1])
        weighted = jnp.where((position >= begin) & (position < end), acts, 0.0)
        high, rest = split(weighted)
        highs.append(high)
        lows.append(rest)
    over_rows = (((0,), (0,)), ((), ()))
    main = lax.dot_general(
        jnp.concatenate(highs, axis=1),
        grads_both,
        over_rows,
        preferred_element_type=jnp.float32,
    )
    rest = lax.dot_general(
        jnp.concatenate(lows, axis=1), grads_high, over_rows, preferred_element_type=jnp.float32
    )
    part = main[:, :LANES] + main[:, LANES:] + rest
    if not first:
        part += before[...]
    if not last:
        outs[0][...] = part
        return
    kept, sent = outs
    core = table[table.shape[0] - 1]
    half = part.shape[0] // 2
    upper, lower = part[:half, :], part[half:, :]
    kept[...] = jnp.where(core == 0, upper, lower)
    sent[...] = jnp.where(core == 0, lower, upper)


def step_sketch(blocks, entry, total, table, lengths, weights, last=False):
    count = len(blocks)
    rows, width = blocks[0].shape
    total_rows = count * rows
    hidden = weights[0].shape[1]
    columns = 2 * hidden + LANES
    first = total is None
    out_rows = lengths.shape[0] * LANES // 2
    operands = [*blocks, *weights] + ([] if first else [total])
    out_shape = [jax.ShapeDtypeStruct((out_rows, LANES), jnp.float32)]
    if last:
        out_shape = [jax.ShapeDtypeStruct((out_rows // 2, LANES), jnp.float32)] * 2
    outs = pl.pallas_call(
        functools.partial(step_kernel, count, entry, first, last),
        out_shape=out_shape,
        in_specs=[SMEM, SMEM] + [VMEM] * len(operands),
        out_specs=[VMEM] * len(out_shape),
        scratch_shapes=[
            pltpu.VMEM((total_rows, columns), jnp.float32),
            pltpu.VMEM((total_rows, 2 * hidden), jnp.bfloat16),
        ],
        compiler_params=pltpu.CompilerParams(vmem_limit_bytes=16 * 2**20),
        cost_estimate=pl.CostEstimate(
            flops=4 * total_rows * width * columns,
            bytes_accessed=2 * total_rows * width,
            transcendentals=0,
        ),
    )(table, lengths, *operands)
    return outs if last else outs[0]


def score_kernel(table, mine, theirs, val_own, val_other, scores, sketch):
    core = table[table.shape[0] - 1]
    sketch[...] = mine[...] + theirs[...].astype(jnp.float32)
    own, rank = scores.shape[0], sketch.shape[0] // scores.shape[0]
    half = rank // 2
    left = lax.broadcasted_iota(jnp.int32, (own, LANES), 1) < LANES // 2
    squares = jnp.zeros((own, LANES), jnp.float32)
    found = jnp.zeros((4 * own, scores.shape[1]), jnp.float32)
    for side, val in ((core, val_own), (1 - core, val_other)):
        gates, ups = [], []
        for a in range(half):
            slab = sketch[pl.ds(side * half + a, own, stride=rank), :]
            squares += slab * slab
            gates.append(jnp.where(left, slab, 0.0))
            ups.append(jnp.where(left, 0.0, slab))
        gate_high, gate_low = split(jnp.concatenate(gates, axis=1))
        up_high, up_low = split(jnp.concatenate(ups, axis=1))
        found += lax.dot_general(
            jnp.concatenate([gate_high, gate_low, up_high, up_low], axis=0),
            val[...],
            (((1,), (1,)), ((), ())),
            preferred_element_type=jnp.float32,
        )
    count = rank * LANES // 2
    gate_mean = jnp.sum(jnp.where(left, squares, 0.0), axis=1, keepdims=True) / count
    up_mean = jnp.sum(jnp.where(left, 0.0, squares), axis=1, keepdims=True) / count
    gate_part = found[:own] + found[own : 2 * own]
    up_part = found[2 * own : 3 * own] + found[3 * own :]
    scores[...] = gate_part / jnp.sqrt(gate_mean + eps_scale) + up_part / jnp.sqrt(
        up_mean + eps_scale
    )


def score(table, mine, theirs, val_own, val_other, own):
    return pl.pallas_call(
        score_kernel,
        out_shape=jax.ShapeDtypeStruct((own, val_own.shape[0]), jnp.float32),
        in_specs=[SMEM, VMEM, VMEM, VMEM, VMEM],
        out_specs=VMEM,
        scratch_shapes=[pltpu.VMEM(mine.shape, jnp.float32)],
        compiler_params=pltpu.CompilerParams(vmem_limit_bytes=16 * 2**20),
    )(table, mine, theirs, val_own, val_other)


def fast(order, tokens_in, out_grad, w_gate, w_up, proj_in, proj_out, lengths, val_sketch):
    n = len(order)
    rows = tokens_in.shape[0]
    seq_count = lengths.shape[0]
    table = ring_table(order, rows)
    device = lax.axis_index("seq") * n + lax.axis_index("mp")
    table = lax.dynamic_index_in_dim(jnp.asarray(table), device, 0, keepdims=False)
    ahead = [(order[i], order[(i + 1) % n]) for i in range(n)]
    one = ahead + [(n + b, n + a) for a, b in ahead]
    send_one = functools.partial(lax.ppermute, axis_name=("seq", "mp"), perm=one)
    send_two = functools.partial(
        lax.ppermute, axis_name=("seq", "mp"), perm=[(b, a) for a, b in one]
    )
    swap = functools.partial(lax.ppermute, axis_name="seq", perm=[(0, 1), (1, 0)])

    after = lax.optimization_barrier
    one_way = send_one(tokens_in)
    other, other_val = swap(tokens_in), swap(val_sketch)
    twice, diagonal = prepare(w_gate, w_up, out_grad, proj_in, proj_out)
    later_tokens, twice = after((tokens_in, twice))
    two_way = send_two(later_tokens)
    add = functools.partial(
        step_sketch,
        table=table,
        lengths=lengths,
        weights=[out_grad, w_gate, w_up, twice, diagonal],
    )

    waiting = (tokens_in, other)
    total, entry = None, 0
    for k in range(1, n // 2):
        one_way, other_half = after((one_way, waiting[1]))
        next_one = send_one(one_way)
        swapped_one = swap(one_way)
        total = add([waiting[0], other_half], entry, total)
        entry += 2
        two_way, total, other_val = after((two_way, total, other_val))
        next_two = send_two(two_way) if k + 1 < n // 2 else None
        swapped_two = swap(two_way)
        _, swapped_one = after((two_way, swapped_one))
        total = add([one_way, swapped_one], entry, total)
        entry += 2
        next_one, total = after((next_one, total))
        waiting = (two_way, swapped_two)
        one_way, two_way = next_one, next_two
    total = add(waiting, entry, total)
    entry += 2
    kept, sent = add([one_way, swap(one_way)], entry, total, last=True)

    mine, theirs = kept, swap(sent)
    bit = 1
    while bit < n:
        mine = mine + theirs
        sent = mine.astype(jnp.bfloat16)
        exchange = [bit]
        if bit == 1 and n >= 8:
            exchange = [1, 2, 3]
        got = [
            lax.ppermute(sent, "mp", [(i, i ^ flip) for i in range(n)]) for flip in exchange
        ]
        for part in got[:-1]:
            mine = mine + part.astype(jnp.float32)
        theirs = got[-1]
        bit = exchange[-1] + 1 if len(exchange) > 1 else 2 * bit
        if bit < n:
            theirs = theirs.astype(jnp.float32)
    return score(table, mine, theirs, val_sketch, other_val, seq_count // 2)


def grad_rows(rows, cotangent, w_gate, w_up, proj_out):
    half_cols = proj_out.shape[1] // 2
    gate_pre = jnp.dot(rows, w_gate, preferred_element_type=jnp.float32)
    up_pre = jnp.dot(rows, w_up, preferred_element_type=jnp.float32)
    cotangent = cotangent.astype(jnp.float32)
    sigmoid_gate = jax.nn.sigmoid(gate_pre)
    grad_up = (cotangent * gate_pre * sigmoid_gate).astype(jnp.bfloat16)
    grad_gate = (
        cotangent * up_pre * sigmoid_gate * (1.0 + gate_pre * (1.0 - sigmoid_gate))
    ).astype(jnp.bfloat16)
    proj_gate = jnp.dot(grad_gate, proj_out[:, :half_cols], preferred_element_type=jnp.float32)
    proj_up = jnp.dot(grad_up, proj_out[:, half_cols:], preferred_element_type=jnp.float32)
    return jnp.concatenate([proj_gate, proj_up], axis=1)


def plain(order, tokens_in, out_grad, w_gate, w_up, proj_in, proj_out, lengths, val_sketch):
    n = len(order)
    rows = tokens_in.shape[0]
    seq_count = lengths.shape[0]
    rank = proj_in.shape[1]
    x = lax.all_gather(tokens_in, ("seq", "mp"), axis=0, tiled=True)
    grads = grad_rows(x, out_grad, w_gate, w_up, proj_out)
    acts = jnp.dot(x, proj_in, preferred_element_type=jnp.float32)
    ends = jnp.cumsum(lengths)
    position = lax.iota(jnp.int32, x.shape[0])[:, None]
    member = ((position >= (ends - lengths)[None, :]) & (position < ends[None, :])).astype(
        jnp.float32
    )
    weighted = (member[:, :, None] * acts[:, None, :]).reshape(x.shape[0], seq_count * rank)
    sketch = lax.dot_general(
        weighted, grads, (((0,), (0,)), ((), ())), precision=lax.Precision.HIGHEST
    )
    sketch = lax.psum(sketch, ("seq", "mp"))
    own = seq_count // lax.axis_size("seq")
    layered = sketch.reshape(seq_count, rank, 2, rank)
    layered = lax.dynamic_slice_in_dim(layered, lax.axis_index("seq") * own, own, 0)
    norm_scale = jnp.sqrt(jnp.mean(layered * layered, axis=(1, 3)) + eps_scale)
    normed = (layered / norm_scale[:, None, :, None]).reshape(own, 2 * rank * rank)
    full_val = lax.all_gather(val_sketch, "seq", axis=1, tiled=True)
    return lax.dot_general(
        normed,
        full_val.astype(jnp.float32),
        (((1,), (1,)), ((), ())),
        precision=lax.Precision.HIGHEST,
    )


def shards(order, tokens_in, out_grad, w_gate, w_up, proj_in, proj_out, lengths, val_sketch):
    n = len(order)
    rows, width = tokens_in.shape
    fits = (
        n >= 2
        and n & (n - 1) == 0
        and lax.axis_size("seq") == 2
        and rows % CHUNK == 0
        and w_gate.shape[1] % LANES == 0
        and width % LANES == 0
        and 2 * proj_in.shape[1] == LANES
        and lengths.shape[0] % 4 == 0
        and val_sketch.shape[1] == proj_in.shape[1] * LANES // 2
    )
    work = fast if fits else plain
    return work(
        order, tokens_in, out_grad, w_gate, w_up, proj_in, proj_out, lengths, val_sketch
    )


def solution(mesh):
    in_specs = (
        P(("groups", "seq", "mp"), None),
        P("groups", ("seq", "mp")),
        P(None, ("seq", "mp")),
        P(None, ("seq", "mp")),
        P(),
        P(("seq", "mp"), None),
        P("groups"),
        P("mp", "seq"),
    )
    out_specs = P(("groups", "seq"), "mp")
    return jax.shard_map(
        functools.partial(shards, ring_order(mesh)),
        mesh=mesh,
        in_specs=in_specs,
        out_specs=out_specs,
        check_vma=False,
    )
```

```python
import functools

import jax
import jax.numpy as jnp
import numpy as np
from jax import lax
from jax.experimental import pallas as pl
from jax.experimental.pallas import tpu as pltpu
from jax.sharding import PartitionSpec as P

eps_scale = 1e-06
LANES = 128
CHUNK = 32
ANY = pl.BlockSpec(memory_space=pl.ANY)
VMEM = pl.BlockSpec(memory_space=pltpu.VMEM)
SMEM = pl.BlockSpec(memory_space=pltpu.SMEM)


def ring_order(mesh):
    n = mesh.shape["mp"]
    line = list(mesh.devices[0, 0, :])
    natural = list(range(n))
    if n < 4 or not hasattr(line[0], "coords"):
        return natural
    first, third = line[0].coords, line[2].coords
    if sum(abs(a - b) for a, b in zip(first, third)) == 1:
        return natural[0::2] + natural[1::2][::-1]
    return natural


def ring_table(order, rows):
    n = len(order)
    table = []
    for core in range(2):
        for m in range(n):
            p, sign = order.index(m), 1 - 2 * core

            def row(c, shift):
                return (c * n + order[(p + shift) % n]) * rows

            line = [row(core, 0), row(1 - core, 0)]
            for k in range(1, n // 2):
                line += [row(core, -sign * k), row(1 - core, sign * k)]
                line += [row(core, sign * k), row(1 - core, -sign * k)]
            line += [row(core, n // 2), row(1 - core, n // 2), core]
            table.append(line)
    return np.array(table, np.int32)


def prepare_kernel(table, lengths, w_gate, w_up, out_grad, proj_in, proj_out, twice, diagonal):
    twice[...] = jnp.concatenate([proj_in[...], proj_in[...]], axis=1)
    values = proj_out[...]
    hidden = values.shape[0]
    left = lax.broadcasted_iota(jnp.int32, values.shape, 1) < LANES // 2
    none = jnp.zeros_like(values)
    diagonal[:hidden, :] = jnp.where(left, values, none)
    diagonal[hidden:, :] = jnp.where(left, none, values)


def prepare(table, lengths, w_gate, w_up, out_grad, proj_in, proj_out):
    width, hidden = w_gate.shape
    return pl.pallas_call(
        prepare_kernel,
        out_shape=[
            jax.ShapeDtypeStruct((width, LANES), proj_in.dtype),
            jax.ShapeDtypeStruct((2 * hidden, LANES), proj_out.dtype),
        ],
        in_specs=[SMEM, SMEM] + [VMEM] * 5,
        out_specs=[VMEM] * 2,
        compiler_params=pltpu.CompilerParams(vmem_limit_bytes=16 * 2**20),
    )(table, lengths, w_gate, w_up, out_grad, proj_in, proj_out)


def split(value):
    high = value.astype(jnp.bfloat16)
    return high, (value - high.astype(jnp.float32)).astype(jnp.bfloat16)


def step_kernel(count, entry, first, last, table, lengths, *refs):
    blocks = refs[:count]
    out_grad, w_gate, w_up, twice, diagonal = refs[count : count + 5]
    at = count + 5
    if not first:
        before, at = refs[at], at + 1
    outs, (pre, both) = refs[at:-2], refs[-2:]
    rows = blocks[0].shape[0]
    total_rows = rows * count
    hidden = out_grad.shape[1]
    seq_count = lengths.shape[0]
    starts = [table[entry + i] for i in range(count)]

    for place, w in ((0, w_gate), (hidden, w_up), (2 * hidden, twice)):
        x = jnp.concatenate([block[...] for block in blocks], axis=0)
        pre[:, place : place + w.shape[1]] = jnp.dot(
            x, w[...], preferred_element_type=jnp.float32
        )
    for i in range(total_rows // CHUNK):
        here = slice(i * CHUNK, (i + 1) * CHUNK)
        block, row = divmod(i * CHUNK, rows)
        source = pl.ds(pl.multiple_of(starts[block] + row, CHUNK), CHUNK)
        gate = pre[here, :hidden]
        up = pre[here, hidden : 2 * hidden]
        cotangent = out_grad[source, :].astype(jnp.float32)
        sig = 0.5 * (1.0 + jnp.tanh(0.5 * gate))
        scaled = cotangent * sig
        both[here, hidden:] = (scaled * gate).astype(jnp.bfloat16)
        both[here, :hidden] = (scaled * up * (1.0 + gate * (1.0 - sig))).astype(jnp.bfloat16)
    grads = jnp.dot(both[...], diagonal[...], preferred_element_type=jnp.float32)
    grads_high, grads_low = split(grads)
    grads_both = jnp.concatenate([grads_high, grads_low], axis=1)

    acts = pre[:, 2 * hidden :]
    position = []
    for i in range(count):
        position.append(starts[i] + lax.broadcasted_iota(jnp.int32, (rows, LANES), 0))
    position = jnp.concatenate(position, axis=0)
    low = lax.broadcasted_iota(jnp.int32, (1, LANES), 1) < LANES // 2
    ends = []
    for s in range(seq_count):
        ends.append(lengths[s] + (ends[-1] if s else 0))
    highs, lows = [], []
    for g in range(seq_count // 2):
        begin = jnp.where(low, ends[2 * g - 1] if g else 0, ends[2 * g])
        end = jnp.where(low, ends[2 * g], ends[2 * g + 1])
        weighted = jnp.where((position >= begin) & (position < end), acts, 0.0)
        high, rest = split(weighted)
        highs.append(high)
        lows.append(rest)
    over_rows = (((0,), (0,)), ((), ()))
    main = lax.dot_general(
        jnp.concatenate(highs, axis=1),
        grads_both,
        over_rows,
        preferred_element_type=jnp.float32,
    )
    rest = lax.dot_general(
        jnp.concatenate(lows, axis=1), grads_high, over_rows, preferred_element_type=jnp.float32
    )
    part = main[:, :LANES] + main[:, LANES:] + rest
    if not first:
        part += before[...]
    if not last:
        outs[0][...] = part
        return
    kept, sent = outs
    core = table[table.shape[0] - 1]
    half = part.shape[0] // 2
    upper, lower = part[:half, :], part[half:, :]
    kept[...] = jnp.where(core == 0, upper, lower)
    sent[...] = jnp.where(core == 0, lower, upper)


def step_sketch(blocks, entry, total, table, lengths, weights, last=False):
    count = len(blocks)
    rows, width = blocks[0].shape
    total_rows = count * rows
    hidden = weights[0].shape[1]
    columns = 2 * hidden + LANES
    first = total is None
    out_rows = lengths.shape[0] * LANES // 2
    operands = [*blocks, *weights] + ([] if first else [total])
    out_shape = [jax.ShapeDtypeStruct((out_rows, LANES), jnp.float32)]
    if last:
        out_shape = [jax.ShapeDtypeStruct((out_rows // 2, LANES), jnp.float32)] * 2
    outs = pl.pallas_call(
        functools.partial(step_kernel, count, entry, first, last),
        out_shape=out_shape,
        in_specs=[SMEM, SMEM] + [VMEM] * len(operands),
        out_specs=[VMEM] * len(out_shape),
        scratch_shapes=[
            pltpu.VMEM((total_rows, columns), jnp.float32),
            pltpu.VMEM((total_rows, 2 * hidden), jnp.bfloat16),
        ],
        compiler_params=pltpu.CompilerParams(vmem_limit_bytes=16 * 2**20),
        cost_estimate=pl.CostEstimate(
            flops=4 * total_rows * width * columns,
            bytes_accessed=2 * total_rows * width,
            transcendentals=0,
        ),
    )(table, lengths, *operands)
    return outs if last else outs[0]


def score_kernel(table, mine, theirs, val_own, val_other, scores, sketch):
    core = table[table.shape[0] - 1]
    sketch[...] = mine[...] + theirs[...].astype(jnp.float32)
    own, rank = scores.shape[0], sketch.shape[0] // scores.shape[0]
    half = rank // 2
    left = lax.broadcasted_iota(jnp.int32, (own, LANES), 1) < LANES // 2
    squares = jnp.zeros((own, LANES), jnp.float32)
    found = jnp.zeros((4 * own, scores.shape[1]), jnp.float32)
    for side, val in ((core, val_own), (1 - core, val_other)):
        gates, ups = [], []
        for a in range(half):
            slab = sketch[pl.ds(side * half + a, own, stride=rank), :]
            squares += slab * slab
            gates.append(jnp.where(left, slab, 0.0))
            ups.append(jnp.where(left, 0.0, slab))
        gate_high, gate_low = split(jnp.concatenate(gates, axis=1))
        up_high, up_low = split(jnp.concatenate(ups, axis=1))
        found += lax.dot_general(
            jnp.concatenate([gate_high, gate_low, up_high, up_low], axis=0),
            val[...],
            (((1,), (1,)), ((), ())),
            preferred_element_type=jnp.float32,
        )
    count = rank * LANES // 2
    gate_mean = jnp.sum(jnp.where(left, squares, 0.0), axis=1, keepdims=True) / count
    up_mean = jnp.sum(jnp.where(left, 0.0, squares), axis=1, keepdims=True) / count
    gate_part = found[:own] + found[own : 2 * own]
    up_part = found[2 * own : 3 * own] + found[3 * own :]
    scores[...] = gate_part / jnp.sqrt(gate_mean + eps_scale) + up_part / jnp.sqrt(
        up_mean + eps_scale
    )


def score(table, mine, theirs, val_own, val_other, own):
    return pl.pallas_call(
        score_kernel,
        out_shape=jax.ShapeDtypeStruct((own, val_own.shape[0]), jnp.float32),
        in_specs=[SMEM, VMEM, VMEM, VMEM, VMEM],
        out_specs=VMEM,
        scratch_shapes=[pltpu.VMEM(mine.shape, jnp.float32)],
        compiler_params=pltpu.CompilerParams(vmem_limit_bytes=16 * 2**20),
    )(table, mine, theirs, val_own, val_other)


def fast(order, tokens_in, out_grad, w_gate, w_up, proj_in, proj_out, lengths, val_sketch):
    n = len(order)
    rows = tokens_in.shape[0]
    seq_count = lengths.shape[0]
    table = ring_table(order, rows)
    device = lax.axis_index("seq") * n + lax.axis_index("mp")
    table = lax.dynamic_index_in_dim(jnp.asarray(table), device, 0, keepdims=False)
    ahead = [(order[i], order[(i + 1) % n]) for i in range(n)]
    one = ahead + [(n + b, n + a) for a, b in ahead]
    send_one = functools.partial(lax.ppermute, axis_name=("seq", "mp"), perm=one)
    send_two = functools.partial(
        lax.ppermute, axis_name=("seq", "mp"), perm=[(b, a) for a, b in one]
    )
    swap = functools.partial(lax.ppermute, axis_name="seq", perm=[(0, 1), (1, 0)])

    after = lax.optimization_barrier
    one_way = send_one(tokens_in)
    other, other_val = swap(tokens_in), swap(val_sketch)
    later_tokens, table = after((tokens_in, table))
    two_way = send_two(later_tokens)
    twice, diagonal = prepare(table, lengths, w_gate, w_up, out_grad, proj_in, proj_out)
    add = functools.partial(
        step_sketch,
        table=table,
        lengths=lengths,
        weights=[out_grad, w_gate, w_up, twice, diagonal],
    )

    waiting = (tokens_in, other)
    total, entry = None, 0
    for k in range(1, n // 2):
        one_way, other_half = after((one_way, waiting[1]))
        next_one = send_one(one_way)
        swapped_one = swap(one_way)
        total = add([waiting[0], other_half], entry, total)
        entry += 2
        two_way, total, other_val = after((two_way, total, other_val))
        next_two = send_two(two_way) if k + 1 < n // 2 else None
        swapped_two = swap(two_way)
        _, swapped_one = after((two_way, swapped_one))
        total = add([one_way, swapped_one], entry, total)
        entry += 2
        next_one, total = after((next_one, total))
        waiting = (two_way, swapped_two)
        one_way, two_way = next_one, next_two
    total = add(waiting, entry, total)
    entry += 2
    kept, sent = add([one_way, swap(one_way)], entry, total, last=True)

    mine, theirs = kept, swap(sent)
    bit = 1
    while bit < n:
        mine = mine + theirs
        sent = mine.astype(jnp.bfloat16)
        exchange = [bit]
        if bit == 1 and n >= 8:
            exchange = [1, 2, 3]
        got = [
            lax.ppermute(sent, "mp", [(i, i ^ flip) for i in range(n)]) for flip in exchange
        ]
        for part in got[:-1]:
            mine = mine + part.astype(jnp.float32)
        theirs = got[-1]
        bit = exchange[-1] + 1 if len(exchange) > 1 else 2 * bit
        if bit < n:
            theirs = theirs.astype(jnp.float32)
    return score(table, mine, theirs, val_sketch, other_val, seq_count // 2)


def grad_rows(rows, cotangent, w_gate, w_up, proj_out):
    half_cols = proj_out.shape[1] // 2
    gate_pre = jnp.dot(rows, w_gate, preferred_element_type=jnp.float32)
    up_pre = jnp.dot(rows, w_up, preferred_element_type=jnp.float32)
    cotangent = cotangent.astype(jnp.float32)
    sigmoid_gate = jax.nn.sigmoid(gate_pre)
    grad_up = (cotangent * gate_pre * sigmoid_gate).astype(jnp.bfloat16)
    grad_gate = (
        cotangent * up_pre * sigmoid_gate * (1.0 + gate_pre * (1.0 - sigmoid_gate))
    ).astype(jnp.bfloat16)
    proj_gate = jnp.dot(grad_gate, proj_out[:, :half_cols], preferred_element_type=jnp.float32)
    proj_up = jnp.dot(grad_up, proj_out[:, half_cols:], preferred_element_type=jnp.float32)
    return jnp.concatenate([proj_gate, proj_up], axis=1)


def plain(order, tokens_in, out_grad, w_gate, w_up, proj_in, proj_out, lengths, val_sketch):
    n = len(order)
    rows = tokens_in.shape[0]
    seq_count = lengths.shape[0]
    rank = proj_in.shape[1]
    x = lax.all_gather(tokens_in, ("seq", "mp"), axis=0, tiled=True)
    grads = grad_rows(x, out_grad, w_gate, w_up, proj_out)
    acts = jnp.dot(x, proj_in, preferred_element_type=jnp.float32)
    ends = jnp.cumsum(lengths)
    position = lax.iota(jnp.int32, x.shape[0])[:, None]
    member = ((position >= (ends - lengths)[None, :]) & (position < ends[None, :])).astype(
        jnp.float32
    )
    weighted = (member[:, :, None] * acts[:, None, :]).reshape(x.shape[0], seq_count * rank)
    sketch = lax.dot_general(
        weighted, grads, (((0,), (0,)), ((), ())), precision=lax.Precision.HIGHEST
    )
    sketch = lax.psum(sketch, ("seq", "mp"))
    own = seq_count // lax.axis_size("seq")
    layered = sketch.reshape(seq_count, rank, 2, rank)
    layered = lax.dynamic_slice_in_dim(layered, lax.axis_index("seq") * own, own, 0)
    norm_scale = jnp.sqrt(jnp.mean(layered * layered, axis=(1, 3)) + eps_scale)
    normed = (layered / norm_scale[:, None, :, None]).reshape(own, 2 * rank * rank)
    full_val = lax.all_gather(val_sketch, "seq", axis=1, tiled=True)
    return lax.dot_general(
        normed,
        full_val.astype(jnp.float32),
        (((1,), (1,)), ((), ())),
        precision=lax.Precision.HIGHEST,
    )


def shards(order, tokens_in, out_grad, w_gate, w_up, proj_in, proj_out, lengths, val_sketch):
    n = len(order)
    rows, width = tokens_in.shape
    fits = (
        n >= 2
        and n & (n - 1) == 0
        and lax.axis_size("seq") == 2
        and rows % CHUNK == 0
        and w_gate.shape[1] % LANES == 0
        and width % LANES == 0
        and 2 * proj_in.shape[1] == LANES
        and lengths.shape[0] % 4 == 0
        and val_sketch.shape[1] == proj_in.shape[1] * LANES // 2
    )
    work = fast if fits else plain
    return work(
        order, tokens_in, out_grad, w_gate, w_up, proj_in, proj_out, lengths, val_sketch
    )


def solution(mesh):
    in_specs = (
        P(("groups", "seq", "mp"), None),
        P("groups", ("seq", "mp")),
        P(None, ("seq", "mp")),
        P(None, ("seq", "mp")),
        P(),
        P(("seq", "mp"), None),
        P("groups"),
        P("mp", "seq"),
    )
    out_specs = P(("groups", "seq"), "mp")
    return jax.shard_map(
        functools.partial(shards, ring_order(mesh)),
        mesh=mesh,
        in_specs=in_specs,
        out_specs=out_specs,
        check_vma=False,
    )
```

```python
import functools

import jax
import jax.numpy as jnp
import numpy as np
from jax import lax
from jax.experimental import pallas as pl
from jax.experimental.pallas import tpu as pltpu
from jax.sharding import PartitionSpec as P

eps_scale = 1e-06
LANES = 128
CHUNK = 32
ANY = pl.BlockSpec(memory_space=pl.ANY)
VMEM = pl.BlockSpec(memory_space=pltpu.VMEM)
SMEM = pl.BlockSpec(memory_space=pltpu.SMEM)


def ring_order(mesh):
    n = mesh.shape["mp"]
    line = list(mesh.devices[0, 0, :])
    natural = list(range(n))
    if n < 4 or not hasattr(line[0], "coords"):
        return natural
    first, third = line[0].coords, line[2].coords
    if sum(abs(a - b) for a, b in zip(first, third)) == 1:
        return natural[0::2] + natural[1::2][::-1]
    return natural


def ring_table(order, rows):
    n = len(order)
    table = []
    for core in range(2):
        for m in range(n):
            p, sign = order.index(m), 1 - 2 * core

            def row(c, shift):
                return (c * n + order[(p + shift) % n]) * rows

            line = [row(core, 0), row(1 - core, 0)]
            for k in range(1, n // 2):
                line += [row(core, -sign * k), row(1 - core, sign * k)]
                line += [row(core, sign * k), row(1 - core, -sign * k)]
            line += [row(core, n // 2), row(1 - core, n // 2), core]
            table.append(line)
    return np.array(table, np.int32)


def split(value):
    high = value.astype(jnp.bfloat16)
    return high, (value - high.astype(jnp.float32)).astype(jnp.bfloat16)


def gradients(pre, cotangents, both):
    hidden = both.shape[1] // 2
    for i, cotangent in enumerate(cotangents):
        here = slice(i * CHUNK, (i + 1) * CHUNK)
        gate = pre[here, :hidden]
        up = pre[here, hidden : 2 * hidden]
        sig = 0.5 * (1.0 + jnp.tanh(0.5 * gate))
        scaled = cotangent().astype(jnp.float32) * sig
        both[here, hidden:] = (scaled * gate).astype(jnp.bfloat16)
        both[here, :hidden] = (scaled * up * (1.0 + gate * (1.0 - sig))).astype(jnp.bfloat16)


def sketch_of(starts, rows, lengths, pre, both, diagonal):
    grads = jnp.dot(both[...], diagonal[...], preferred_element_type=jnp.float32)
    grads_high, grads_low = split(grads)
    grads_both = jnp.concatenate([grads_high, grads_low], axis=1)
    seq_count = lengths.shape[0]
    acts = pre[:, both.shape[1] :]
    position = []
    for start in starts:
        position.append(start + lax.broadcasted_iota(jnp.int32, (rows, LANES), 0))
    position = jnp.concatenate(position, axis=0)
    low = lax.broadcasted_iota(jnp.int32, (1, LANES), 1) < LANES // 2
    ends = []
    for s in range(seq_count):
        ends.append(lengths[s] + (ends[-1] if s else 0))
    highs, lows = [], []
    for g in range(seq_count // 2):
        begin = jnp.where(low, ends[2 * g - 1] if g else 0, ends[2 * g])
        end = jnp.where(low, ends[2 * g], ends[2 * g + 1])
        weighted = jnp.where((position >= begin) & (position < end), acts, 0.0)
        high, rest = split(weighted)
        highs.append(high)
        lows.append(rest)
    over_rows = (((0,), (0,)), ((), ()))
    main = lax.dot_general(
        jnp.concatenate(highs, axis=1),
        grads_both,
        over_rows,
        preferred_element_type=jnp.float32,
    )
    rest = lax.dot_general(
        jnp.concatenate(lows, axis=1), grads_high, over_rows, preferred_element_type=jnp.float32
    )
    return main[:, :LANES] + main[:, LANES:] + rest


def first_kernel(
    table, lengths, own, other, gate_hbm, up_hbm, out_grad_hbm, proj_out_hbm, proj_in,
    total, w, out_grad, diagonal, x, pre, both, sems, w_sems,
):
    rows = own.shape[0]
    width, hidden = gate_hbm.shape
    depth = width // w_sems.shape[0]
    parts = []
    for k in range(w_sems.shape[0]):
        here = pl.ds(k * depth, depth)
        parts.append(
            (
                pltpu.make_async_copy(
                    gate_hbm.at[here], w.at[here, pl.ds(0, hidden)], w_sems.at[k, 0]
                ),
                pltpu.make_async_copy(
                    up_hbm.at[here], w.at[here, pl.ds(hidden, hidden)], w_sems.at[k, 1]
                ),
            )
        )
    blocks = [
        pltpu.make_async_copy(own, x.at[pl.ds(0, rows)], sems.at[0]),
        pltpu.make_async_copy(other, x.at[pl.ds(rows, rows)], sems.at[1]),
    ]
    upper = pltpu.make_async_copy(proj_out_hbm, diagonal.at[pl.ds(0, hidden)], sems.at[2])
    whole = pltpu.make_async_copy(out_grad_hbm, out_grad, sems.at[3])
    for copy in blocks + [upper]:
        copy.start()
    for pair in parts:
        for copy in pair:
            copy.start()
    whole.start()

    w[:, 2 * hidden :] = jnp.concatenate([proj_in[...], proj_in[...]], axis=1)
    upper.wait()
    values = diagonal[:hidden, :]
    left = lax.broadcasted_iota(jnp.int32, values.shape, 1) < LANES // 2
    none = jnp.zeros_like(values)
    diagonal[hidden:, :] = jnp.where(left, none, values)
    diagonal[:hidden, :] = jnp.where(left, values, none)
    for copy in blocks:
        copy.wait()
    for k, pair in enumerate(parts):
        for copy in pair:
            copy.wait()
        here = slice(k * depth, (k + 1) * depth)
        product = jnp.dot(x[:, here], w[here, :], preferred_element_type=jnp.float32)
        pre[...] = product if k == 0 else pre[...] + product
    whole.wait()
    starts = [table[0], table[1]]
    gradients(pre, cotangent_chunks(out_grad, starts, rows), both)
    total[...] = sketch_of(starts, rows, lengths, pre, both, diagonal)


def cotangent_chunks(out_grad, starts, rows):
    chunks = []
    for start in starts:
        for row in range(0, rows, CHUNK):
            here = pl.ds(pl.multiple_of(start + row, CHUNK), CHUNK)
            chunks.append(lambda here=here: out_grad[here, :])
    return chunks


def step_kernel(entry, last, table, lengths, one, two, w, out_grad, diagonal, before, *refs):
    outs, (pre, both) = refs[:-2], refs[-2:]
    rows = one.shape[0]
    starts = [table[entry], table[entry + 1]]
    x = jnp.concatenate([one[...], two[...]], axis=0)
    pre[...] = jnp.dot(x, w[...], preferred_element_type=jnp.float32)
    gradients(pre, cotangent_chunks(out_grad, starts, rows), both)
    total = before[...] + sketch_of(starts, rows, lengths, pre, both, diagonal)
    if not last:
        outs[0][...] = total
        return
    kept, sent = outs
    core = table[table.shape[0] - 1]
    half = total.shape[0] // 2
    upper, lower = total[:half, :], total[half:, :]
    kept[...] = jnp.where(core == 0, upper, lower)
    sent[...] = jnp.where(core == 0, lower, upper)


def costs(rows, width, columns):
    return pl.CostEstimate(
        flops=4 * rows * width * columns, bytes_accessed=2 * rows * width, transcendentals=0
    )


def first_step(table, lengths, own, other, w_gate, w_up, out_grad, proj_in, proj_out):
    rows, width = own.shape
    hidden = w_gate.shape[1]
    columns = 2 * hidden + LANES
    chunks = 4 if width % (4 * LANES) == 0 else 1
    own, w_gate, w_up, out_grad, proj_out = [
        pltpu.with_memory_space_constraint(a, pltpu.HBM)
        for a in (own, w_gate, w_up, out_grad, proj_out)
    ]
    return pl.pallas_call(
        first_kernel,
        out_shape=[
            jax.ShapeDtypeStruct((lengths.shape[0] * LANES // 2, LANES), jnp.float32),
            pltpu.VMEM((width, columns), jnp.bfloat16),
            pltpu.VMEM(out_grad.shape, jnp.bfloat16),
            pltpu.VMEM((2 * hidden, LANES), jnp.bfloat16),
        ],
        in_specs=[SMEM, SMEM] + [ANY] * 6 + [VMEM],
        out_specs=[VMEM] * 4,
        scratch_shapes=[
            pltpu.VMEM((2 * rows, width), jnp.bfloat16),
            pltpu.VMEM((2 * rows, columns), jnp.float32),
            pltpu.VMEM((2 * rows, 2 * hidden), jnp.bfloat16),
            pltpu.SemaphoreType.DMA((4,)),
            pltpu.SemaphoreType.DMA((chunks, 2)),
        ],
        compiler_params=pltpu.CompilerParams(vmem_limit_bytes=16 * 2**20),
        cost_estimate=costs(2 * rows, width, columns),
    )(table, lengths, own, other, w_gate, w_up, out_grad, proj_out, proj_in)


def next_step(blocks, entry, total, table, lengths, weights, last=False):
    rows, width = blocks[0].shape
    w, _, diagonal = weights
    shape = total.shape
    out_shape = [jax.ShapeDtypeStruct(shape, jnp.float32)]
    if last:
        out_shape = [jax.ShapeDtypeStruct((shape[0] // 2, LANES), jnp.float32)] * 2
    outs = pl.pallas_call(
        functools.partial(step_kernel, entry, last),
        out_shape=out_shape,
        in_specs=[SMEM, SMEM] + [VMEM] * 6,
        out_specs=[VMEM] * len(out_shape),
        scratch_shapes=[
            pltpu.VMEM((2 * rows, w.shape[1]), jnp.float32),
            pltpu.VMEM((2 * rows, diagonal.shape[0]), jnp.bfloat16),
        ],
        compiler_params=pltpu.CompilerParams(vmem_limit_bytes=16 * 2**20),
        cost_estimate=costs(2 * rows, width, w.shape[1]),
    )(table, lengths, *blocks, *weights, total)
    return outs if last else outs[0]


def score_kernel(table, mine, theirs, val_own, val_other, scores, sketch):
    core = table[table.shape[0] - 1]
    sketch[...] = mine[...] + theirs[...].astype(jnp.float32)
    own, rank = scores.shape[0], sketch.shape[0] // scores.shape[0]
    half = rank // 2
    left = lax.broadcasted_iota(jnp.int32, (own, LANES), 1) < LANES // 2
    squares = jnp.zeros((own, LANES), jnp.float32)
    found = jnp.zeros((4 * own, scores.shape[1]), jnp.float32)
    for side, val in ((core, val_own), (1 - core, val_other)):
        gates, ups = [], []
        for a in range(half):
            slab = sketch[pl.ds(side * half + a, own, stride=rank), :]
            squares += slab * slab
            gates.append(jnp.where(left, slab, 0.0))
            ups.append(jnp.where(left, 0.0, slab))
        gate_high, gate_low = split(jnp.concatenate(gates, axis=1))
        up_high, up_low = split(jnp.concatenate(ups, axis=1))
        found += lax.dot_general(
            jnp.concatenate([gate_high, gate_low, up_high, up_low], axis=0),
            val[...],
            (((1,), (1,)), ((), ())),
            preferred_element_type=jnp.float32,
        )
    count = rank * LANES // 2
    gate_mean = jnp.sum(jnp.where(left, squares, 0.0), axis=1, keepdims=True) / count
    up_mean = jnp.sum(jnp.where(left, 0.0, squares), axis=1, keepdims=True) / count
    gate_part = found[:own] + found[own : 2 * own]
    up_part = found[2 * own : 3 * own] + found[3 * own :]
    scores[...] = gate_part / jnp.sqrt(gate_mean + eps_scale) + up_part / jnp.sqrt(
        up_mean + eps_scale
    )


def score(table, mine, theirs, val_own, val_other, own):
    return pl.pallas_call(
        score_kernel,
        out_shape=jax.ShapeDtypeStruct((own, val_own.shape[0]), jnp.float32),
        in_specs=[SMEM, VMEM, VMEM, VMEM, VMEM],
        out_specs=VMEM,
        scratch_shapes=[pltpu.VMEM(mine.shape, jnp.float32)],
        compiler_params=pltpu.CompilerParams(vmem_limit_bytes=16 * 2**20),
    )(table, mine, theirs, val_own, val_other)


def fast(order, tokens_in, out_grad, w_gate, w_up, proj_in, proj_out, lengths, val_sketch):
    n = len(order)
    rows = tokens_in.shape[0]
    seq_count = lengths.shape[0]
    table = ring_table(order, rows)
    device = lax.axis_index("seq") * n + lax.axis_index("mp")
    table = lax.dynamic_index_in_dim(jnp.asarray(table), device, 0, keepdims=False)
    ahead = [(order[i], order[(i + 1) % n]) for i in range(n)]
    one = ahead + [(n + b, n + a) for a, b in ahead]
    send_one = functools.partial(lax.ppermute, axis_name=("seq", "mp"), perm=one)
    send_two = functools.partial(
        lax.ppermute, axis_name=("seq", "mp"), perm=[(b, a) for a, b in one]
    )
    swap = functools.partial(lax.ppermute, axis_name="seq", perm=[(0, 1), (1, 0)])

    after = lax.optimization_barrier
    one_way = send_one(tokens_in)
    other, other_val = swap(tokens_in), swap(val_sketch)
    later_tokens, table = after((tokens_in, table))
    two_way = send_two(later_tokens)
    total, *weights = first_step(
        table, lengths, tokens_in, other, w_gate, w_up, out_grad, proj_in, proj_out
    )
    add = functools.partial(next_step, table=table, lengths=lengths, weights=weights)

    entry = 2
    for k in range(1, n // 2):
        one_way, total = after((one_way, total))
        next_one, swapped = send_one(one_way), swap(one_way)
        total = add([one_way, swapped], entry, total)
        two_way, total, other_val = after((two_way, total, other_val))
        next_two = send_two(two_way) if k + 1 < n // 2 else None
        total = add([two_way, swap(two_way)], entry + 2, total)
        entry += 4
        one_way, two_way = next_one, next_two
    one_way, total = after((one_way, total))
    kept, sent = add([one_way, swap(one_way)], entry, total, last=True)

    mine, theirs = kept, swap(sent)
    bit = 1
    while bit < n:
        mine = mine + theirs
        sent = mine.astype(jnp.bfloat16)
        exchange = [bit]
        if bit == 1 and n >= 8:
            exchange = [1, 2, 3]
        got = [
            lax.ppermute(sent, "mp", [(i, i ^ flip) for i in range(n)]) for flip in exchange
        ]
        for part in got[:-1]:
            mine = mine + part.astype(jnp.float32)
        theirs = got[-1]
        bit = exchange[-1] + 1 if len(exchange) > 1 else 2 * bit
        if bit < n:
            theirs = theirs.astype(jnp.float32)
    return score(table, mine, theirs, val_sketch, other_val, seq_count // 2)


def grad_rows(rows, cotangent, w_gate, w_up, proj_out):
    half_cols = proj_out.shape[1] // 2
    gate_pre = jnp.dot(rows, w_gate, preferred_element_type=jnp.float32)
    up_pre = jnp.dot(rows, w_up, preferred_element_type=jnp.float32)
    cotangent = cotangent.astype(jnp.float32)
    sigmoid_gate = jax.nn.sigmoid(gate_pre)
    grad_up = (cotangent * gate_pre * sigmoid_gate).astype(jnp.bfloat16)
    grad_gate = (
        cotangent * up_pre * sigmoid_gate * (1.0 + gate_pre * (1.0 - sigmoid_gate))
    ).astype(jnp.bfloat16)
    proj_gate = jnp.dot(grad_gate, proj_out[:, :half_cols], preferred_element_type=jnp.float32)
    proj_up = jnp.dot(grad_up, proj_out[:, half_cols:], preferred_element_type=jnp.float32)
    return jnp.concatenate([proj_gate, proj_up], axis=1)


def plain(order, tokens_in, out_grad, w_gate, w_up, proj_in, proj_out, lengths, val_sketch):
    n = len(order)
    rows = tokens_in.shape[0]
    seq_count = lengths.shape[0]
    rank = proj_in.shape[1]
    x = lax.all_gather(tokens_in, ("seq", "mp"), axis=0, tiled=True)
    grads = grad_rows(x, out_grad, w_gate, w_up, proj_out)
    acts = jnp.dot(x, proj_in, preferred_element_type=jnp.float32)
    ends = jnp.cumsum(lengths)
    position = lax.iota(jnp.int32, x.shape[0])[:, None]
    member = ((position >= (ends - lengths)[None, :]) & (position < ends[None, :])).astype(
        jnp.float32
    )
    weighted = (member[:, :, None] * acts[:, None, :]).reshape(x.shape[0], seq_count * rank)
    sketch = lax.dot_general(
        weighted, grads, (((0,), (0,)), ((), ())), precision=lax.Precision.HIGHEST
    )
    sketch = lax.psum(sketch, ("seq", "mp"))
    own = seq_count // lax.axis_size("seq")
    layered = sketch.reshape(seq_count, rank, 2, rank)
    layered = lax.dynamic_slice_in_dim(layered, lax.axis_index("seq") * own, own, 0)
    norm_scale = jnp.sqrt(jnp.mean(layered * layered, axis=(1, 3)) + eps_scale)
    normed = (layered / norm_scale[:, None, :, None]).reshape(own, 2 * rank * rank)
    full_val = lax.all_gather(val_sketch, "seq", axis=1, tiled=True)
    return lax.dot_general(
        normed,
        full_val.astype(jnp.float32),
        (((1,), (1,)), ((), ())),
        precision=lax.Precision.HIGHEST,
    )


def shards(order, tokens_in, out_grad, w_gate, w_up, proj_in, proj_out, lengths, val_sketch):
    n = len(order)
    rows, width = tokens_in.shape
    fits = (
        n >= 2
        and n & (n - 1) == 0
        and lax.axis_size("seq") == 2
        and rows % CHUNK == 0
        and w_gate.shape[1] % LANES == 0
        and width % LANES == 0
        and 2 * proj_in.shape[1] == LANES
        and lengths.shape[0] % 4 == 0
        and val_sketch.shape[1] == proj_in.shape[1] * LANES // 2
    )
    work = fast if fits else plain
    return work(
        order, tokens_in, out_grad, w_gate, w_up, proj_in, proj_out, lengths, val_sketch
    )


def solution(mesh):
    in_specs = (
        P(("groups", "seq", "mp"), None),
        P("groups", ("seq", "mp")),
        P(None, ("seq", "mp")),
        P(None, ("seq", "mp")),
        P(),
        P(("seq", "mp"), None),
        P("groups"),
        P("mp", "seq"),
    )
    out_specs = P(("groups", "seq"), "mp")
    return jax.shard_map(
        functools.partial(shards, ring_order(mesh)),
        mesh=mesh,
        in_specs=in_specs,
        out_specs=out_specs,
        check_vma=False,
    )
```

```python
import functools

import jax
import jax.numpy as jnp
import numpy as np
from jax import lax
from jax.experimental import pallas as pl
from jax.experimental.pallas import tpu as pltpu
from jax.sharding import PartitionSpec as P

eps_scale = 1e-06
LANES = 128
CHUNK = 32
ANY = pl.BlockSpec(memory_space=pl.ANY)
VMEM = pl.BlockSpec(memory_space=pltpu.VMEM)
SMEM = pl.BlockSpec(memory_space=pltpu.SMEM)


def ring_order(mesh):
    n = mesh.shape["mp"]
    line = list(mesh.devices[0, 0, :])
    natural = list(range(n))
    if n < 4 or not hasattr(line[0], "coords"):
        return natural
    first, third = line[0].coords, line[2].coords
    if sum(abs(a - b) for a, b in zip(first, third)) == 1:
        return natural[0::2] + natural[1::2][::-1]
    return natural


def ring_table(order, rows):
    n = len(order)
    table = []
    for core in range(2):
        for m in range(n):
            p, sign = order.index(m), 1 - 2 * core

            def row(c, shift):
                return (c * n + order[(p + shift) % n]) * rows

            line = [row(core, 0), row(1 - core, 0)]
            for k in range(1, n // 2):
                line += [row(core, -sign * k), row(1 - core, sign * k)]
                line += [row(core, sign * k), row(1 - core, -sign * k)]
            line += [row(core, n // 2), row(1 - core, n // 2), core]
            table.append(line)
    return np.array(table, np.int32)


def split(value):
    high = value.astype(jnp.bfloat16)
    return high, (value - high.astype(jnp.float32)).astype(jnp.bfloat16)


def gradients(pre, cotangents, both):
    hidden = both.shape[1] // 2
    for i, cotangent in enumerate(cotangents):
        here = slice(i * CHUNK, (i + 1) * CHUNK)
        gate = pre[here, :hidden]
        up = pre[here, hidden : 2 * hidden]
        sig = 0.5 * (1.0 + jnp.tanh(0.5 * gate))
        scaled = cotangent().astype(jnp.float32) * sig
        both[here, hidden:] = (scaled * gate).astype(jnp.bfloat16)
        both[here, :hidden] = (scaled * up * (1.0 + gate * (1.0 - sig))).astype(jnp.bfloat16)


def sketch_of(starts, rows, lengths, pre, both, diagonal):
    grads = jnp.dot(both[...], diagonal[...], preferred_element_type=jnp.float32)
    grads_high, grads_low = split(grads)
    grads_both = jnp.concatenate([grads_high, grads_low], axis=1)
    seq_count = lengths.shape[0]
    acts = pre[:, both.shape[1] :]
    position = []
    for start in starts:
        position.append(start + lax.broadcasted_iota(jnp.int32, (rows, LANES), 0))
    position = jnp.concatenate(position, axis=0)
    low = lax.broadcasted_iota(jnp.int32, (1, LANES), 1) < LANES // 2
    ends = []
    for s in range(seq_count):
        ends.append(lengths[s] + (ends[-1] if s else 0))
    highs, lows = [], []
    for g in range(seq_count // 2):
        begin = jnp.where(low, ends[2 * g - 1] if g else 0, ends[2 * g])
        end = jnp.where(low, ends[2 * g], ends[2 * g + 1])
        weighted = jnp.where((position >= begin) & (position < end), acts, 0.0)
        high, rest = split(weighted)
        highs.append(high)
        lows.append(rest)
    over_rows = (((0,), (0,)), ((), ()))
    main = lax.dot_general(
        jnp.concatenate(highs, axis=1),
        grads_both,
        over_rows,
        preferred_element_type=jnp.float32,
    )
    rest = lax.dot_general(
        jnp.concatenate(lows, axis=1), grads_high, over_rows, preferred_element_type=jnp.float32
    )
    return main[:, :LANES] + main[:, LANES:] + rest


def first_kernel(
    table, lengths, own, other, gate_hbm, up_hbm, out_grad_hbm, proj_out_hbm, proj_in,
    total, w, out_grad, diagonal, x, pre, both, sems, w_sems,
):
    rows = own.shape[0]
    width, hidden = gate_hbm.shape
    depth = width // w_sems.shape[0]
    parts = []
    for k in range(w_sems.shape[0]):
        here = pl.ds(k * depth, depth)
        parts.append(
            (
                pltpu.make_async_copy(
                    gate_hbm.at[here], w.at[here, pl.ds(0, hidden)], w_sems.at[k, 0]
                ),
                pltpu.make_async_copy(
                    up_hbm.at[here], w.at[here, pl.ds(hidden, hidden)], w_sems.at[k, 1]
                ),
            )
        )
    blocks = [
        pltpu.make_async_copy(own, x.at[pl.ds(0, rows)], sems.at[0]),
        pltpu.make_async_copy(other, x.at[pl.ds(rows, rows)], sems.at[1]),
    ]
    upper = pltpu.make_async_copy(proj_out_hbm, diagonal.at[pl.ds(0, hidden)], sems.at[2])
    whole = pltpu.make_async_copy(out_grad_hbm, out_grad, sems.at[3])
    for copy in blocks + [upper]:
        copy.start()
    for pair in parts:
        for copy in pair:
            copy.start()
    whole.start()

    w[:, 2 * hidden :] = jnp.concatenate([proj_in[...], proj_in[...]], axis=1)
    upper.wait()
    values = diagonal[:hidden, :]
    left = lax.broadcasted_iota(jnp.int32, values.shape, 1) < LANES // 2
    none = jnp.zeros_like(values)
    diagonal[hidden:, :] = jnp.where(left, none, values)
    diagonal[:hidden, :] = jnp.where(left, values, none)
    for copy in blocks:
        copy.wait()
    for k, pair in enumerate(parts):
        for copy in pair:
            copy.wait()
        here = slice(k * depth, (k + 1) * depth)
        product = jnp.dot(x[:, here], w[here, :], preferred_element_type=jnp.float32)
        pre[...] = product if k == 0 else pre[...] + product
    whole.wait()
    starts = [table[0], table[1]]
    gradients(pre, cotangent_chunks(out_grad, starts, rows), both)
    total[...] = sketch_of(starts, rows, lengths, pre, both, diagonal)


def cotangent_chunks(out_grad, starts, rows):
    chunks = []
    for start in starts:
        for row in range(0, rows, CHUNK):
            here = pl.ds(pl.multiple_of(start + row, CHUNK), CHUNK)
            chunks.append(lambda here=here: out_grad[here, :])
    return chunks


def step_kernel(entry, last, table, lengths, one, two, w, out_grad, diagonal, before, *refs):
    outs, (pre, both) = refs[:-2], refs[-2:]
    rows = one.shape[0]
    starts = [table[entry], table[entry + 1]]
    x = jnp.concatenate([one[...], two[...]], axis=0)
    pre[...] = jnp.dot(x, w[...], preferred_element_type=jnp.float32)
    gradients(pre, cotangent_chunks(out_grad, starts, rows), both)
    total = before[...] + sketch_of(starts, rows, lengths, pre, both, diagonal)
    if not last:
        outs[0][...] = total
        return
    kept, sent = outs
    core = table[table.shape[0] - 1]
    half = total.shape[0] // 2
    upper, lower = total[:half, :], total[half:, :]
    kept[...] = jnp.where(core == 0, upper, lower)
    sent[...] = jnp.where(core == 0, lower, upper)


def costs(rows, width, columns):
    return pl.CostEstimate(
        flops=4 * rows * width * columns, bytes_accessed=2 * rows * width, transcendentals=0
    )


def first_step(table, lengths, own, other, w_gate, w_up, out_grad, proj_in, proj_out):
    rows, width = own.shape
    hidden = w_gate.shape[1]
    columns = 2 * hidden + LANES
    chunks = 4 if width % (4 * LANES) == 0 else 1
    own, w_gate, w_up, out_grad, proj_out = [
        pltpu.with_memory_space_constraint(a, pltpu.HBM)
        for a in (own, w_gate, w_up, out_grad, proj_out)
    ]
    return pl.pallas_call(
        first_kernel,
        out_shape=[
            jax.ShapeDtypeStruct((lengths.shape[0] * LANES // 2, LANES), jnp.float32),
            pltpu.VMEM((width, columns), jnp.bfloat16),
            pltpu.VMEM(out_grad.shape, jnp.bfloat16),
            pltpu.VMEM((2 * hidden, LANES), jnp.bfloat16),
        ],
        in_specs=[SMEM, SMEM] + [ANY] * 6 + [VMEM],
        out_specs=[VMEM] * 4,
        scratch_shapes=[
            pltpu.VMEM((2 * rows, width), jnp.bfloat16),
            pltpu.VMEM((2 * rows, columns), jnp.float32),
            pltpu.VMEM((2 * rows, 2 * hidden), jnp.bfloat16),
            pltpu.SemaphoreType.DMA((4,)),
            pltpu.SemaphoreType.DMA((chunks, 2)),
        ],
        compiler_params=pltpu.CompilerParams(vmem_limit_bytes=16 * 2**20),
        cost_estimate=costs(2 * rows, width, columns),
    )(table, lengths, own, other, w_gate, w_up, out_grad, proj_out, proj_in)


def next_step(blocks, entry, total, table, lengths, weights, last=False):
    rows, width = blocks[0].shape
    w, _, diagonal = weights
    shape = total.shape
    out_shape = [jax.ShapeDtypeStruct(shape, jnp.float32)]
    if last:
        out_shape = [jax.ShapeDtypeStruct((shape[0] // 2, LANES), jnp.float32)] * 2
    outs = pl.pallas_call(
        functools.partial(step_kernel, entry, last),
        out_shape=out_shape,
        in_specs=[SMEM, SMEM] + [VMEM] * 6,
        out_specs=[VMEM] * len(out_shape),
        scratch_shapes=[
            pltpu.VMEM((2 * rows, w.shape[1]), jnp.float32),
            pltpu.VMEM((2 * rows, diagonal.shape[0]), jnp.bfloat16),
        ],
        compiler_params=pltpu.CompilerParams(vmem_limit_bytes=16 * 2**20),
        cost_estimate=costs(2 * rows, width, w.shape[1]),
    )(table, lengths, *blocks, *weights, total)
    return outs if last else outs[0]


def score_kernel(table, given, val_own, val_other, scores, sketch):
    core = table[table.shape[0] - 1]
    sketch[...] = given[...].astype(jnp.float32)
    own, rank = scores.shape[0], sketch.shape[0] // scores.shape[0]
    half = rank // 2
    left = lax.broadcasted_iota(jnp.int32, (own, LANES), 1) < LANES // 2
    squares = jnp.zeros((own, LANES), jnp.float32)
    found = jnp.zeros((4 * own, scores.shape[1]), jnp.float32)
    for side, val in ((core, val_own), (1 - core, val_other)):
        gates, ups = [], []
        for a in range(half):
            slab = sketch[pl.ds(side * half + a, own, stride=rank), :]
            squares += slab * slab
            gates.append(jnp.where(left, slab, 0.0))
            ups.append(jnp.where(left, 0.0, slab))
        gate_high, gate_low = split(jnp.concatenate(gates, axis=1))
        up_high, up_low = split(jnp.concatenate(ups, axis=1))
        found += lax.dot_general(
            jnp.concatenate([gate_high, gate_low, up_high, up_low], axis=0),
            val[...],
            (((1,), (1,)), ((), ())),
            preferred_element_type=jnp.float32,
        )
    count = rank * LANES // 2
    gate_mean = jnp.sum(jnp.where(left, squares, 0.0), axis=1, keepdims=True) / count
    up_mean = jnp.sum(jnp.where(left, 0.0, squares), axis=1, keepdims=True) / count
    gate_part = found[:own] + found[own : 2 * own]
    up_part = found[2 * own : 3 * own] + found[3 * own :]
    scores[...] = gate_part / jnp.sqrt(gate_mean + eps_scale) + up_part / jnp.sqrt(
        up_mean + eps_scale
    )


def score(table, sketch, val_own, val_other, own):
    return pl.pallas_call(
        score_kernel,
        out_shape=jax.ShapeDtypeStruct((own, val_own.shape[0]), jnp.float32),
        in_specs=[SMEM, VMEM, VMEM, VMEM],
        out_specs=VMEM,
        scratch_shapes=[pltpu.VMEM(sketch.shape, jnp.float32)],
        compiler_params=pltpu.CompilerParams(vmem_limit_bytes=16 * 2**20),
    )(table, sketch, val_own, val_other)


def fast(order, tokens_in, out_grad, w_gate, w_up, proj_in, proj_out, lengths, val_sketch):
    n = len(order)
    rows = tokens_in.shape[0]
    seq_count = lengths.shape[0]
    table = ring_table(order, rows)
    device = lax.axis_index("seq") * n + lax.axis_index("mp")
    table = lax.dynamic_index_in_dim(jnp.asarray(table), device, 0, keepdims=False)
    ahead = [(order[i], order[(i + 1) % n]) for i in range(n)]
    one = ahead + [(n + b, n + a) for a, b in ahead]
    send_one = functools.partial(lax.ppermute, axis_name=("seq", "mp"), perm=one)
    send_two = functools.partial(
        lax.ppermute, axis_name=("seq", "mp"), perm=[(b, a) for a, b in one]
    )
    swap = functools.partial(lax.ppermute, axis_name="seq", perm=[(0, 1), (1, 0)])

    after = lax.optimization_barrier
    one_way = send_one(tokens_in)
    other, other_val = swap(tokens_in), swap(val_sketch)
    later_tokens, table = after((tokens_in, table))
    two_way = send_two(later_tokens)
    total, *weights = first_step(
        table, lengths, tokens_in, other, w_gate, w_up, out_grad, proj_in, proj_out
    )
    add = functools.partial(next_step, table=table, lengths=lengths, weights=weights)

    waiting, entry = None, 2
    for k in range(1, n // 2):
        one_way, total = after((one_way, total))
        next_one = send_one(one_way)
        swapped_one = swap(one_way)
        if waiting is not None:
            total = add(waiting, entry, total)
            entry += 2
        two_way, total, other_val = after((two_way, total, other_val))
        next_two = send_two(two_way) if k + 1 < n // 2 else None
        swapped_two = swap(two_way)
        _, swapped_one = after((two_way, swapped_one))
        total = add([one_way, swapped_one], entry, total)
        entry += 2
        waiting = (two_way, swapped_two)
        one_way, two_way = next_one, next_two
    one_way, total = after((one_way, total))
    swapped_one = swap(one_way)
    if waiting is not None:
        total = add(waiting, entry, total)
        entry += 2
    kept, sent = add([one_way, swapped_one], entry, total, last=True)

    part = kept + swap(sent)
    size = part.shape[0] // n
    part = lax.all_to_all(part.reshape(n, size, LANES), "mp", 0, 0)
    part = jnp.sum(part, axis=0).astype(jnp.bfloat16)
    part = jnp.broadcast_to(part[None], (n, size, LANES))
    sketch = lax.all_to_all(part, "mp", 0, 0).reshape(n * size, LANES)
    return score(table, sketch, val_sketch, other_val, seq_count // 2)


def grad_rows(rows, cotangent, w_gate, w_up, proj_out):
    half_cols = proj_out.shape[1] // 2
    gate_pre = jnp.dot(rows, w_gate, preferred_element_type=jnp.float32)
    up_pre = jnp.dot(rows, w_up, preferred_element_type=jnp.float32)
    cotangent = cotangent.astype(jnp.float32)
    sigmoid_gate = jax.nn.sigmoid(gate_pre)
    grad_up = (cotangent * gate_pre * sigmoid_gate).astype(jnp.bfloat16)
    grad_gate = (
        cotangent * up_pre * sigmoid_gate * (1.0 + gate_pre * (1.0 - sigmoid_gate))
    ).astype(jnp.bfloat16)
    proj_gate = jnp.dot(grad_gate, proj_out[:, :half_cols], preferred_element_type=jnp.float32)
    proj_up = jnp.dot(grad_up, proj_out[:, half_cols:], preferred_element_type=jnp.float32)
    return jnp.concatenate([proj_gate, proj_up], axis=1)


def plain(order, tokens_in, out_grad, w_gate, w_up, proj_in, proj_out, lengths, val_sketch):
    n = len(order)
    rows = tokens_in.shape[0]
    seq_count = lengths.shape[0]
    rank = proj_in.shape[1]
    x = lax.all_gather(tokens_in, ("seq", "mp"), axis=0, tiled=True)
    grads = grad_rows(x, out_grad, w_gate, w_up, proj_out)
    acts = jnp.dot(x, proj_in, preferred_element_type=jnp.float32)
    ends = jnp.cumsum(lengths)
    position = lax.iota(jnp.int32, x.shape[0])[:, None]
    member = ((position >= (ends - lengths)[None, :]) & (position < ends[None, :])).astype(
        jnp.float32
    )
    weighted = (member[:, :, None] * acts[:, None, :]).reshape(x.shape[0], seq_count * rank)
    sketch = lax.dot_general(
        weighted, grads, (((0,), (0,)), ((), ())), precision=lax.Precision.HIGHEST
    )
    sketch = lax.psum(sketch, ("seq", "mp"))
    own = seq_count // lax.axis_size("seq")
    layered = sketch.reshape(seq_count, rank, 2, rank)
    layered = lax.dynamic_slice_in_dim(layered, lax.axis_index("seq") * own, own, 0)
    norm_scale = jnp.sqrt(jnp.mean(layered * layered, axis=(1, 3)) + eps_scale)
    normed = (layered / norm_scale[:, None, :, None]).reshape(own, 2 * rank * rank)
    full_val = lax.all_gather(val_sketch, "seq", axis=1, tiled=True)
    return lax.dot_general(
        normed,
        full_val.astype(jnp.float32),
        (((1,), (1,)), ((), ())),
        precision=lax.Precision.HIGHEST,
    )


def shards(order, tokens_in, out_grad, w_gate, w_up, proj_in, proj_out, lengths, val_sketch):
    n = len(order)
    rows, width = tokens_in.shape
    fits = (
        n >= 2
        and n & (n - 1) == 0
        and lax.axis_size("seq") == 2
        and rows % CHUNK == 0
        and w_gate.shape[1] % LANES == 0
        and width % LANES == 0
        and 2 * proj_in.shape[1] == LANES
        and lengths.shape[0] % 4 == 0
        and lengths.shape[0] * LANES // 4 % (8 * n) == 0
        and val_sketch.shape[1] == proj_in.shape[1] * LANES // 2
    )
    work = fast if fits else plain
    return work(
        order, tokens_in, out_grad, w_gate, w_up, proj_in, proj_out, lengths, val_sketch
    )


def solution(mesh):
    in_specs = (
        P(("groups", "seq", "mp"), None),
        P("groups", ("seq", "mp")),
        P(None, ("seq", "mp")),
        P(None, ("seq", "mp")),
        P(),
        P(("seq", "mp"), None),
        P("groups"),
        P("mp", "seq"),
    )
    out_specs = P(("groups", "seq"), "mp")
    return jax.shard_map(
        functools.partial(shards, ring_order(mesh)),
        mesh=mesh,
        in_specs=in_specs,
        out_specs=out_specs,
        check_vma=False,
    )
```

```python
import functools

import jax
import jax.numpy as jnp
import numpy as np
from jax import lax
from jax.experimental import pallas as pl
from jax.experimental.pallas import tpu as pltpu
from jax.sharding import PartitionSpec as P

eps_scale = 1e-06
LANES = 128
CHUNK = 32
ANY = pl.BlockSpec(memory_space=pl.ANY)
VMEM = pl.BlockSpec(memory_space=pltpu.VMEM)
SMEM = pl.BlockSpec(memory_space=pltpu.SMEM)


def ring_order(mesh):
    n = mesh.shape["mp"]
    line = list(mesh.devices[0, 0, :])
    natural = list(range(n))
    if n < 4 or not hasattr(line[0], "coords"):
        return natural
    first, third = line[0].coords, line[2].coords
    if sum(abs(a - b) for a, b in zip(first, third)) == 1:
        return natural[0::2] + natural[1::2][::-1]
    return natural


def ring_table(order, rows):
    n = len(order)
    table = []
    for core in range(2):
        for m in range(n):
            p, sign = order.index(m), 1 - 2 * core

            def row(c, shift):
                return (c * n + order[(p + shift) % n]) * rows

            line = [row(core, 0), row(1 - core, 0)]
            for k in range(1, n // 2):
                line += [row(core, -sign * k), row(1 - core, sign * k)]
                line += [row(core, sign * k), row(1 - core, -sign * k)]
            line += [row(core, n // 2), row(1 - core, n // 2), core]
            table.append(line)
    return np.array(table, np.int32)


def split(value):
    high = value.astype(jnp.bfloat16)
    return high, (value - high.astype(jnp.float32)).astype(jnp.bfloat16)


def gradients(pre, cotangents, both):
    hidden = both.shape[1] // 2
    for i, cotangent in enumerate(cotangents):
        here = slice(i * CHUNK, (i + 1) * CHUNK)
        gate = pre[here, :hidden]
        up = pre[here, hidden : 2 * hidden]
        sig = 0.5 * (1.0 + jnp.tanh(0.5 * gate))
        scaled = cotangent().astype(jnp.float32) * sig
        both[here, hidden:] = (scaled * gate).astype(jnp.bfloat16)
        both[here, :hidden] = (scaled * up * (1.0 + gate * (1.0 - sig))).astype(jnp.bfloat16)


def sketch_of(starts, rows, lengths, pre, both, diagonal):
    grads = jnp.dot(both[...], diagonal[...], preferred_element_type=jnp.float32)
    grads_high, grads_low = split(grads)
    grads_both = jnp.concatenate([grads_high, grads_low], axis=1)
    seq_count = lengths.shape[0]
    acts = pre[:, both.shape[1] :]
    position = []
    for start in starts:
        position.append(start + lax.broadcasted_iota(jnp.int32, (rows, LANES), 0))
    position = jnp.concatenate(position, axis=0)
    low = lax.broadcasted_iota(jnp.int32, (1, LANES), 1) < LANES // 2
    ends = []
    for s in range(seq_count):
        ends.append(lengths[s] + (ends[-1] if s else 0))
    highs, lows = [], []
    for g in range(seq_count // 2):
        begin = jnp.where(low, ends[2 * g - 1] if g else 0, ends[2 * g])
        end = jnp.where(low, ends[2 * g], ends[2 * g + 1])
        weighted = jnp.where((position >= begin) & (position < end), acts, 0.0)
        high, rest = split(weighted)
        highs.append(high)
        lows.append(rest)
    over_rows = (((0,), (0,)), ((), ()))
    main = lax.dot_general(
        jnp.concatenate(highs, axis=1),
        grads_both,
        over_rows,
        preferred_element_type=jnp.float32,
    )
    rest = lax.dot_general(
        jnp.concatenate(lows, axis=1), grads_high, over_rows, preferred_element_type=jnp.float32
    )
    return main[:, :LANES] + main[:, LANES:] + rest


def load_kernel(
    table, lengths, gate_hbm, up_hbm, out_grad_hbm, proj_out_hbm, proj_in,
    w, out_grad, diagonal, sems,
):
    hidden = gate_hbm.shape[1]
    upper = pltpu.make_async_copy(proj_out_hbm, diagonal.at[pl.ds(0, hidden)], sems.at[0])
    copies = [
        pltpu.make_async_copy(gate_hbm, w.at[:, pl.ds(0, hidden)], sems.at[1]),
        pltpu.make_async_copy(up_hbm, w.at[:, pl.ds(hidden, hidden)], sems.at[2]),
        pltpu.make_async_copy(out_grad_hbm, out_grad, sems.at[3]),
    ]
    for copy in [upper] + copies:
        copy.start()
    w[:, 2 * hidden :] = jnp.concatenate([proj_in[...], proj_in[...]], axis=1)
    upper.wait()
    values = diagonal[:hidden, :]
    left = lax.broadcasted_iota(jnp.int32, values.shape, 1) < LANES // 2
    none = jnp.zeros_like(values)
    diagonal[hidden:, :] = jnp.where(left, none, values)
    diagonal[:hidden, :] = jnp.where(left, values, none)
    for copy in copies:
        copy.wait()


def cotangent_chunks(out_grad, starts, rows):
    chunks = []
    for start in starts:
        for row in range(0, rows, CHUNK):
            here = pl.ds(pl.multiple_of(start + row, CHUNK), CHUNK)
            chunks.append(lambda here=here: out_grad[here, :])
    return chunks


def step_kernel(entry, first, last, table, lengths, one, two, w, out_grad, diagonal, *refs):
    outs, (pre, both) = refs[:-2], refs[-2:]
    if not first:
        before, outs = outs[0], outs[1:]
    rows = one.shape[0]
    starts = [table[entry], table[entry + 1]]
    x = jnp.concatenate([one[...], two[...]], axis=0)
    pre[...] = jnp.dot(x, w[...], preferred_element_type=jnp.float32)
    gradients(pre, cotangent_chunks(out_grad, starts, rows), both)
    total = sketch_of(starts, rows, lengths, pre, both, diagonal)
    if not first:
        total += before[...]
    if not last:
        outs[0][...] = total
        return
    kept, sent = outs
    core = table[table.shape[0] - 1]
    half = total.shape[0] // 2
    upper, lower = total[:half, :], total[half:, :]
    kept[...] = jnp.where(core == 0, upper, lower)
    sent[...] = jnp.where(core == 0, lower, upper)


def costs(rows, width, columns):
    return pl.CostEstimate(
        flops=4 * rows * width * columns, bytes_accessed=2 * rows * width, transcendentals=0
    )


def load(table, lengths, w_gate, w_up, out_grad, proj_in, proj_out):
    width, hidden = w_gate.shape
    w_gate, w_up, out_grad, proj_out = [
        pltpu.with_memory_space_constraint(a, pltpu.HBM)
        for a in (w_gate, w_up, out_grad, proj_out)
    ]
    return pl.pallas_call(
        load_kernel,
        out_shape=[
            pltpu.VMEM((width, 2 * hidden + LANES), jnp.bfloat16),
            pltpu.VMEM(out_grad.shape, jnp.bfloat16),
            pltpu.VMEM((2 * hidden, LANES), jnp.bfloat16),
        ],
        in_specs=[SMEM, SMEM] + [ANY] * 4 + [VMEM],
        out_specs=[VMEM] * 3,
        scratch_shapes=[pltpu.SemaphoreType.DMA((4,))],
        compiler_params=pltpu.CompilerParams(vmem_limit_bytes=16 * 2**20),
    )(table, lengths, w_gate, w_up, out_grad, proj_out, proj_in)


def add_step(blocks, entry, total, table, lengths, weights, last=False):
    rows, width = blocks[0].shape
    w, _, diagonal = weights
    first = total is None
    operands = [*blocks, *weights] + ([] if first else [total])
    out_rows = lengths.shape[0] * LANES // 2
    out_shape = [jax.ShapeDtypeStruct((out_rows, LANES), jnp.float32)]
    if last:
        out_shape = [jax.ShapeDtypeStruct((out_rows // 2, LANES), jnp.float32)] * 2
    outs = pl.pallas_call(
        functools.partial(step_kernel, entry, first, last),
        out_shape=out_shape,
        in_specs=[SMEM, SMEM] + [VMEM] * len(operands),
        out_specs=[VMEM] * len(out_shape),
        scratch_shapes=[
            pltpu.VMEM((2 * rows, w.shape[1]), jnp.float32),
            pltpu.VMEM((2 * rows, diagonal.shape[0]), jnp.bfloat16),
        ],
        compiler_params=pltpu.CompilerParams(vmem_limit_bytes=16 * 2**20),
        cost_estimate=costs(2 * rows, width, w.shape[1]),
    )(table, lengths, *operands)
    return outs if last else outs[0]


def score_kernel(table, mine, theirs, val_own, val_other, scores, sketch):
    core = table[table.shape[0] - 1]
    sketch[...] = mine[...] + theirs[...].astype(jnp.float32)
    own, rank = scores.shape[0], sketch.shape[0] // scores.shape[0]
    half = rank // 2
    left = lax.broadcasted_iota(jnp.int32, (own, LANES), 1) < LANES // 2
    squares = jnp.zeros((own, LANES), jnp.float32)
    found = jnp.zeros((4 * own, scores.shape[1]), jnp.float32)
    for side, val in ((core, val_own), (1 - core, val_other)):
        gates, ups = [], []
        for a in range(half):
            slab = sketch[pl.ds(side * half + a, own, stride=rank), :]
            squares += slab * slab
            gates.append(jnp.where(left, slab, 0.0))
            ups.append(jnp.where(left, 0.0, slab))
        gate_high, gate_low = split(jnp.concatenate(gates, axis=1))
        up_high, up_low = split(jnp.concatenate(ups, axis=1))
        found += lax.dot_general(
            jnp.concatenate([gate_high, gate_low, up_high, up_low], axis=0),
            val[...],
            (((1,), (1,)), ((), ())),
            preferred_element_type=jnp.float32,
        )
    count = rank * LANES // 2
    gate_mean = jnp.sum(jnp.where(left, squares, 0.0), axis=1, keepdims=True) / count
    up_mean = jnp.sum(jnp.where(left, 0.0, squares), axis=1, keepdims=True) / count
    gate_part = found[:own] + found[own : 2 * own]
    up_part = found[2 * own : 3 * own] + found[3 * own :]
    scores[...] = gate_part / jnp.sqrt(gate_mean + eps_scale) + up_part / jnp.sqrt(
        up_mean + eps_scale
    )


def score(table, mine, theirs, val_own, val_other, own):
    return pl.pallas_call(
        score_kernel,
        out_shape=jax.ShapeDtypeStruct((own, val_own.shape[0]), jnp.float32),
        in_specs=[SMEM, VMEM, VMEM, VMEM, VMEM],
        out_specs=VMEM,
        scratch_shapes=[pltpu.VMEM(mine.shape, jnp.float32)],
        compiler_params=pltpu.CompilerParams(vmem_limit_bytes=16 * 2**20),
    )(table, mine, theirs, val_own, val_other)


def fast(order, tokens_in, out_grad, w_gate, w_up, proj_in, proj_out, lengths, val_sketch):
    n = len(order)
    rows = tokens_in.shape[0]
    seq_count = lengths.shape[0]
    table = ring_table(order, rows)
    device = lax.axis_index("seq") * n + lax.axis_index("mp")
    table = lax.dynamic_index_in_dim(jnp.asarray(table), device, 0, keepdims=False)
    ahead = [(order[i], order[(i + 1) % n]) for i in range(n)]
    one = ahead + [(n + b, n + a) for a, b in ahead]
    send_one = functools.partial(lax.ppermute, axis_name=("seq", "mp"), perm=one)
    send_two = functools.partial(
        lax.ppermute, axis_name=("seq", "mp"), perm=[(b, a) for a, b in one]
    )
    swap = functools.partial(lax.ppermute, axis_name="seq", perm=[(0, 1), (1, 0)])

    after = lax.optimization_barrier
    one_way = send_one(tokens_in)
    other, other_val = swap(tokens_in), swap(val_sketch)
    w, out_grad, diagonal = load(table, lengths, w_gate, w_up, out_grad, proj_in, proj_out)
    later_tokens, diagonal = after((tokens_in, diagonal))
    two_way = send_two(later_tokens)
    add = functools.partial(
        add_step, table=table, lengths=lengths, weights=[w, out_grad, diagonal]
    )
    total = add([tokens_in, other], 0, None)

    waiting, entry = None, 2
    for k in range(1, n // 2):
        one_way, total = after((one_way, total))
        next_one = send_one(one_way)
        swapped_one = swap(one_way)
        if waiting is not None:
            total = add(waiting, entry, total)
            entry += 2
        two_way, total, other_val = after((two_way, total, other_val))
        next_two = send_two(two_way) if k + 1 < n // 2 else None
        swapped_two = swap(two_way)
        _, swapped_one = after((two_way, swapped_one))
        total = add([one_way, swapped_one], entry, total)
        entry += 2
        waiting = (two_way, swapped_two)
        one_way, two_way = next_one, next_two
    one_way, total = after((one_way, total))
    swapped_one = swap(one_way)
    if waiting is not None:
        total = add(waiting, entry, total)
        entry += 2
    kept, sent = add([one_way, swapped_one], entry, total, last=True)

    mine, theirs = kept, swap(sent)
    bit = 1
    while bit < n:
        mine = mine + theirs
        sent = mine.astype(jnp.bfloat16)
        exchange = [bit]
        if bit == 1 and n >= 8:
            exchange = [1, 2, 3]
        got = [
            lax.ppermute(sent, "mp", [(i, i ^ flip) for i in range(n)]) for flip in exchange
        ]
        for part in got[:-1]:
            mine = mine + part.astype(jnp.float32)
        theirs = got[-1]
        bit = exchange[-1] + 1 if len(exchange) > 1 else 2 * bit
        if bit < n:
            theirs = theirs.astype(jnp.float32)
    return score(table, mine, theirs, val_sketch, other_val, seq_count // 2)


def grad_rows(rows, cotangent, w_gate, w_up, proj_out):
    half_cols = proj_out.shape[1] // 2
    gate_pre = jnp.dot(rows, w_gate, preferred_element_type=jnp.float32)
    up_pre = jnp.dot(rows, w_up, preferred_element_type=jnp.float32)
    cotangent = cotangent.astype(jnp.float32)
    sigmoid_gate = jax.nn.sigmoid(gate_pre)
    grad_up = (cotangent * gate_pre * sigmoid_gate).astype(jnp.bfloat16)
    grad_gate = (
        cotangent * up_pre * sigmoid_gate * (1.0 + gate_pre * (1.0 - sigmoid_gate))
    ).astype(jnp.bfloat16)
    proj_gate = jnp.dot(grad_gate, proj_out[:, :half_cols], preferred_element_type=jnp.float32)
    proj_up = jnp.dot(grad_up, proj_out[:, half_cols:], preferred_element_type=jnp.float32)
    return jnp.concatenate([proj_gate, proj_up], axis=1)


def plain(order, tokens_in, out_grad, w_gate, w_up, proj_in, proj_out, lengths, val_sketch):
    n = len(order)
    rows = tokens_in.shape[0]
    seq_count = lengths.shape[0]
    rank = proj_in.shape[1]
    x = lax.all_gather(tokens_in, ("seq", "mp"), axis=0, tiled=True)
    grads = grad_rows(x, out_grad, w_gate, w_up, proj_out)
    acts = jnp.dot(x, proj_in, preferred_element_type=jnp.float32)
    ends = jnp.cumsum(lengths)
    position = lax.iota(jnp.int32, x.shape[0])[:, None]
    member = ((position >= (ends - lengths)[None, :]) & (position < ends[None, :])).astype(
        jnp.float32
    )
    weighted = (member[:, :, None] * acts[:, None, :]).reshape(x.shape[0], seq_count * rank)
    sketch = lax.dot_general(
        weighted, grads, (((0,), (0,)), ((), ())), precision=lax.Precision.HIGHEST
    )
    sketch = lax.psum(sketch, ("seq", "mp"))
    own = seq_count // lax.axis_size("seq")
    layered = sketch.reshape(seq_count, rank, 2, rank)
    layered = lax.dynamic_slice_in_dim(layered, lax.axis_index("seq") * own, own, 0)
    norm_scale = jnp.sqrt(jnp.mean(layered * layered, axis=(1, 3)) + eps_scale)
    normed = (layered / norm_scale[:, None, :, None]).reshape(own, 2 * rank * rank)
    full_val = lax.all_gather(val_sketch, "seq", axis=1, tiled=True)
    return lax.dot_general(
        normed,
        full_val.astype(jnp.float32),
        (((1,), (1,)), ((), ())),
        precision=lax.Precision.HIGHEST,
    )


def shards(order, tokens_in, out_grad, w_gate, w_up, proj_in, proj_out, lengths, val_sketch):
    n = len(order)
    rows, width = tokens_in.shape
    fits = (
        n >= 2
        and n & (n - 1) == 0
        and lax.axis_size("seq") == 2
        and rows % CHUNK == 0
        and w_gate.shape[1] % LANES == 0
        and width % LANES == 0
        and 2 * proj_in.shape[1] == LANES
        and lengths.shape[0] % 4 == 0
        and val_sketch.shape[1] == proj_in.shape[1] * LANES // 2
    )
    work = fast if fits else plain
    return work(
        order, tokens_in, out_grad, w_gate, w_up, proj_in, proj_out, lengths, val_sketch
    )


def solution(mesh):
    in_specs = (
        P(("groups", "seq", "mp"), None),
        P("groups", ("seq", "mp")),
        P(None, ("seq", "mp")),
        P(None, ("seq", "mp")),
        P(),
        P(("seq", "mp"), None),
        P("groups"),
        P("mp", "seq"),
    )
    out_specs = P(("groups", "seq"), "mp")
    return jax.shard_map(
        functools.partial(shards, ring_order(mesh)),
        mesh=mesh,
        in_specs=in_specs,
        out_specs=out_specs,
        check_vma=False,
    )
```

```python
import functools

import jax
import jax.numpy as jnp
import numpy as np
from jax import lax
from jax.experimental import pallas as pl
from jax.experimental.pallas import tpu as pltpu
from jax.sharding import PartitionSpec as P

eps_scale = 1e-06
LANES = 128
CHUNK = 32
ANY = pl.BlockSpec(memory_space=pl.ANY)
VMEM = pl.BlockSpec(memory_space=pltpu.VMEM)
SMEM = pl.BlockSpec(memory_space=pltpu.SMEM)


def ring_order(mesh):
    n = mesh.shape["mp"]
    line = list(mesh.devices[0, 0, :])
    natural = list(range(n))
    if n < 4 or not hasattr(line[0], "coords"):
        return natural
    first, third = line[0].coords, line[2].coords
    if sum(abs(a - b) for a, b in zip(first, third)) == 1:
        return natural[0::2] + natural[1::2][::-1]
    return natural


def ring_table(order, rows):
    n = len(order)
    table = []
    for core in range(2):
        for m in range(n):
            p, sign = order.index(m), 1 - 2 * core

            def row(c, shift):
                return (c * n + order[(p + shift) % n]) * rows

            line = [row(core, 0), row(1 - core, 0)]
            for k in range(1, n // 2):
                line += [row(core, -sign * k), row(1 - core, sign * k)]
                line += [row(core, sign * k), row(1 - core, -sign * k)]
            line += [row(core, n // 2), row(1 - core, n // 2), core]
            table.append(line)
    return np.array(table, np.int32)


def split(value):
    high = value.astype(jnp.bfloat16)
    return high, (value - high.astype(jnp.float32)).astype(jnp.bfloat16)


def chunks_of(hidden):
    tiles = hidden // LANES
    if tiles < 4:
        return [(0, hidden)]
    size = tiles // 2
    sizes = [size, tiles - 1 - size, 1]
    firsts = [0, size, tiles - 1]
    return [(f * LANES, c * LANES) for f, c in zip(firsts, sizes)]


def columns_of(hidden):
    spans, at = [], 0
    for i, (_, count) in enumerate(chunks_of(hidden)):
        width = 2 * count + (LANES if i == 0 else 0)
        spans.append((at, width))
        at += width
    return spans


def gradients(pre, cotangents, both, first, count):
    hidden = both.shape[1] // 2
    for i, cotangent in enumerate(cotangents):
        here = slice(i * CHUNK, (i + 1) * CHUNK)
        gate = pre[here, :count]
        up = pre[here, count : 2 * count]
        sig = 0.5 * (1.0 + jnp.tanh(0.5 * gate))
        scaled = cotangent(first, count).astype(jnp.float32) * sig
        both[here, hidden + first : hidden + first + count] = (scaled * gate).astype(jnp.bfloat16)
        both[here, first : first + count] = (
            scaled * up * (1.0 + gate * (1.0 - sig))
        ).astype(jnp.bfloat16)


def weighted_acts(starts, rows, lengths, acts):
    seq_count = lengths.shape[0]
    position = []
    for start in starts:
        position.append(start + lax.broadcasted_iota(jnp.int32, (rows, LANES), 0))
    position = jnp.concatenate(position, axis=0)
    low = lax.broadcasted_iota(jnp.int32, (1, LANES), 1) < LANES // 2
    ends = []
    for s in range(seq_count):
        ends.append(lengths[s] + (ends[-1] if s else 0))
    highs, lows = [], []
    for g in range(seq_count // 2):
        begin = jnp.where(low, ends[2 * g - 1] if g else 0, ends[2 * g])
        end = jnp.where(low, ends[2 * g], ends[2 * g + 1])
        weighted = jnp.where((position >= begin) & (position < end), acts, 0.0)
        high, rest = split(weighted)
        highs.append(high)
        lows.append(rest)
    return jnp.concatenate(highs, axis=1), jnp.concatenate(lows, axis=1)


def sketch_of(acts_high, acts_low, both, diagonal):
    grads = jnp.dot(both[...], diagonal[...], preferred_element_type=jnp.float32)
    grads_high, grads_low = split(grads)
    grads_both = jnp.concatenate([grads_high, grads_low], axis=1)
    over_rows = (((0,), (0,)), ((), ()))
    main = lax.dot_general(acts_high, grads_both, over_rows, preferred_element_type=jnp.float32)
    rest = lax.dot_general(acts_low, grads_high, over_rows, preferred_element_type=jnp.float32)
    return main[:, :LANES] + main[:, LANES:] + rest


def small_kernel(table, lengths, out_grad_hbm, proj_out_hbm, out_grad, diagonal, sems):
    hidden = proj_out_hbm.shape[0]
    upper = pltpu.make_async_copy(proj_out_hbm, diagonal.at[pl.ds(0, hidden)], sems.at[0])
    whole = pltpu.make_async_copy(out_grad_hbm, out_grad, sems.at[1])
    upper.start()
    whole.start()
    upper.wait()
    values = diagonal[:hidden, :]
    left = lax.broadcasted_iota(jnp.int32, values.shape, 1) < LANES // 2
    none = jnp.zeros_like(values)
    diagonal[hidden:, :] = jnp.where(left, none, values)
    diagonal[:hidden, :] = jnp.where(left, values, none)
    whole.wait()


def load_kernel(lengths, diagonal, gate_hbm, up_hbm, proj_in, w, sems):
    hidden = gate_hbm.shape[1]
    copies = []
    for i, (first, count) in enumerate(chunks_of(hidden)):
        at = columns_of(hidden)[i][0]
        for j, source in enumerate((gate_hbm, up_hbm)):
            copies.append(
                pltpu.make_async_copy(
                    source.at[:, pl.ds(first, count)],
                    w.at[:, pl.ds(at + j * count, count)],
                    sems.at[i, j],
                )
            )
    for copy in copies:
        copy.start()
    at, width = columns_of(hidden)[0]
    w[:, at + width - LANES : at + width] = jnp.concatenate([proj_in[...], proj_in[...]], axis=1)
    for copy in copies:
        copy.wait()


def cotangent_chunks(out_grad, starts, rows):
    chunks = []
    for start in starts:
        for row in range(0, rows, CHUNK):
            here = pl.ds(pl.multiple_of(start + row, CHUNK), CHUNK)
            chunks.append(
                lambda first, count, here=here: out_grad[here, first : first + count]
            )
    return chunks


def step_kernel(entry, first, last, table, lengths, one, two, w, out_grad, diagonal, *refs):
    hidden = out_grad.shape[1]
    chunks = chunks_of(hidden)
    outs, pres, both = refs[: -1 - len(chunks)], refs[-1 - len(chunks) : -1], refs[-1]
    if not first:
        before, outs = outs[0], outs[1:]
    rows = one.shape[0]
    starts = [table[entry], table[entry + 1]]
    cotangents = cotangent_chunks(out_grad, starts, rows)
    for i, (at, width) in enumerate(columns_of(hidden)):
        x = jnp.concatenate([one[...], two[...]], axis=0)
        pres[i][...] = jnp.dot(x, w[:, at : at + width], preferred_element_type=jnp.float32)
        if i == 0:
            acts = weighted_acts(starts, rows, lengths, pres[0][:, width - LANES :])
        gradients(pres[i], cotangents, both, *chunks[i])
    total = sketch_of(*acts, both, diagonal)
    if not first:
        total += before[...]
    if not last:
        outs[0][...] = total
        return
    kept, sent = outs
    core = table[table.shape[0] - 1]
    half = total.shape[0] // 2
    upper, lower = total[:half, :], total[half:, :]
    kept[...] = jnp.where(core == 0, upper, lower)
    sent[...] = jnp.where(core == 0, lower, upper)


def costs(rows, width, columns):
    return pl.CostEstimate(
        flops=4 * rows * width * columns, bytes_accessed=2 * rows * width, transcendentals=0
    )


def load_small(table, lengths, out_grad, proj_out):
    out_grad, proj_out = [
        pltpu.with_memory_space_constraint(a, pltpu.HBM) for a in (out_grad, proj_out)
    ]
    hidden = out_grad.shape[1]
    return pl.pallas_call(
        small_kernel,
        out_shape=[
            pltpu.VMEM(out_grad.shape, jnp.bfloat16),
            pltpu.VMEM((2 * hidden, LANES), jnp.bfloat16),
        ],
        in_specs=[SMEM, SMEM, ANY, ANY],
        out_specs=[VMEM] * 2,
        scratch_shapes=[pltpu.SemaphoreType.DMA((2,))],
        compiler_params=pltpu.CompilerParams(vmem_limit_bytes=16 * 2**20),
    )(table, lengths, out_grad, proj_out)


def load(lengths, diagonal, w_gate, w_up, proj_in):
    width, hidden = w_gate.shape
    w_gate, w_up = [pltpu.with_memory_space_constraint(a, pltpu.HBM) for a in (w_gate, w_up)]
    return pl.pallas_call(
        load_kernel,
        out_shape=pltpu.VMEM((width, 2 * hidden + LANES), jnp.bfloat16),
        in_specs=[SMEM, VMEM, ANY, ANY, VMEM],
        out_specs=VMEM,
        scratch_shapes=[pltpu.SemaphoreType.DMA((len(chunks_of(hidden)), 2))],
        compiler_params=pltpu.CompilerParams(vmem_limit_bytes=16 * 2**20),
    )(lengths, diagonal, w_gate, w_up, proj_in)


def add_step(blocks, entry, total, table, lengths, weights, last=False):
    rows, width = blocks[0].shape
    w, _, diagonal = weights
    first = total is None
    operands = [*blocks, *weights] + ([] if first else [total])
    out_rows = lengths.shape[0] * LANES // 2
    out_shape = [jax.ShapeDtypeStruct((out_rows, LANES), jnp.float32)]
    if last:
        out_shape = [jax.ShapeDtypeStruct((out_rows // 2, LANES), jnp.float32)] * 2
    outs = pl.pallas_call(
        functools.partial(step_kernel, entry, first, last),
        out_shape=out_shape,
        in_specs=[SMEM, SMEM] + [VMEM] * len(operands),
        out_specs=[VMEM] * len(out_shape),
        scratch_shapes=[
            *[
                pltpu.VMEM((2 * rows, columns), jnp.float32)
                for _, columns in columns_of(diagonal.shape[0] // 2)
            ],
            pltpu.VMEM((2 * rows, diagonal.shape[0]), jnp.bfloat16),
        ],
        compiler_params=pltpu.CompilerParams(vmem_limit_bytes=16 * 2**20),
        cost_estimate=costs(2 * rows, width, w.shape[1]),
    )(table, lengths, *operands)
    return outs if last else outs[0]


def score_kernel(table, mine, theirs, val_own, val_other, scores, sketch):
    core = table[table.shape[0] - 1]
    sketch[...] = mine[...] + theirs[...].astype(jnp.float32)
    own, rank = scores.shape[0], sketch.shape[0] // scores.shape[0]
    half = rank // 2
    left = lax.broadcasted_iota(jnp.int32, (own, LANES), 1) < LANES // 2
    squares = jnp.zeros((own, LANES), jnp.float32)
    found = jnp.zeros((4 * own, scores.shape[1]), jnp.float32)
    for side, val in ((core, val_own), (1 - core, val_other)):
        gates, ups = [], []
        for a in range(half):
            slab = sketch[pl.ds(side * half + a, own, stride=rank), :]
            squares += slab * slab
            gates.append(jnp.where(left, slab, 0.0))
            ups.append(jnp.where(left, 0.0, slab))
        gate_high, gate_low = split(jnp.concatenate(gates, axis=1))
        up_high, up_low = split(jnp.concatenate(ups, axis=1))
        found += lax.dot_general(
            jnp.concatenate([gate_high, gate_low, up_high, up_low], axis=0),
            val[...],
            (((1,), (1,)), ((), ())),
            preferred_element_type=jnp.float32,
        )
    count = rank * LANES // 2
    gate_mean = jnp.sum(jnp.where(left, squares, 0.0), axis=1, keepdims=True) / count
    up_mean = jnp.sum(jnp.where(left, 0.0, squares), axis=1, keepdims=True) / count
    gate_part = found[:own] + found[own : 2 * own]
    up_part = found[2 * own : 3 * own] + found[3 * own :]
    scores[...] = gate_part / jnp.sqrt(gate_mean + eps_scale) + up_part / jnp.sqrt(
        up_mean + eps_scale
    )


def score(table, mine, theirs, val_own, val_other, own):
    return pl.pallas_call(
        score_kernel,
        out_shape=jax.ShapeDtypeStruct((own, val_own.shape[0]), jnp.float32),
        in_specs=[SMEM, VMEM, VMEM, VMEM, VMEM],
        out_specs=VMEM,
        scratch_shapes=[pltpu.VMEM(mine.shape, jnp.float32)],
        compiler_params=pltpu.CompilerParams(vmem_limit_bytes=16 * 2**20),
    )(table, mine, theirs, val_own, val_other)


def fast(order, tokens_in, out_grad, w_gate, w_up, proj_in, proj_out, lengths, val_sketch):
    n = len(order)
    rows = tokens_in.shape[0]
    seq_count = lengths.shape[0]
    table = ring_table(order, rows)
    device = lax.axis_index("seq") * n + lax.axis_index("mp")
    table = lax.dynamic_index_in_dim(jnp.asarray(table), device, 0, keepdims=False)
    ahead = [(order[i], order[(i + 1) % n]) for i in range(n)]
    one = ahead + [(n + b, n + a) for a, b in ahead]
    send_one = functools.partial(lax.ppermute, axis_name=("seq", "mp"), perm=one)
    send_two = functools.partial(
        lax.ppermute, axis_name=("seq", "mp"), perm=[(b, a) for a, b in one]
    )
    swap = functools.partial(lax.ppermute, axis_name="seq", perm=[(0, 1), (1, 0)])

    after = lax.optimization_barrier
    one_way = send_one(tokens_in)
    other, other_val = swap(tokens_in), swap(val_sketch)
    out_grad, diagonal = load_small(table, lengths, out_grad, proj_out)
    later_tokens, diagonal = after((tokens_in, diagonal))
    two_way = send_two(later_tokens)
    w = load(lengths, diagonal, w_gate, w_up, proj_in)
    add = functools.partial(
        add_step, table=table, lengths=lengths, weights=[w, out_grad, diagonal]
    )
    total = add([tokens_in, other], 0, None)

    waiting, entry = None, 2
    for k in range(1, n // 2):
        one_way, total = after((one_way, total))
        next_one = send_one(one_way)
        swapped_one = swap(one_way)
        if waiting is not None:
            total = add(waiting, entry, total)
            entry += 2
        two_way, total, other_val = after((two_way, total, other_val))
        next_two = send_two(two_way) if k + 1 < n // 2 else None
        swapped_two = swap(two_way)
        _, swapped_one = after((two_way, swapped_one))
        total = add([one_way, swapped_one], entry, total)
        entry += 2
        waiting = (two_way, swapped_two)
        one_way, two_way = next_one, next_two
    one_way, total = after((one_way, total))
    swapped_one = swap(one_way)
    if waiting is not None:
        total = add(waiting, entry, total)
        entry += 2
    kept, sent = add([one_way, swapped_one], entry, total, last=True)

    mine, theirs = kept, swap(sent)
    bit = 1
    while bit < n:
        mine = mine + theirs
        sent = mine.astype(jnp.bfloat16)
        exchange = [bit]
        if bit == 1 and n >= 8:
            exchange = [1, 2, 3]
        got = [
            lax.ppermute(sent, "mp", [(i, i ^ flip) for i in range(n)]) for flip in exchange
        ]
        for part in got[:-1]:
            mine = mine + part.astype(jnp.float32)
        theirs = got[-1]
        bit = exchange[-1] + 1 if len(exchange) > 1 else 2 * bit
        if bit < n:
            theirs = theirs.astype(jnp.float32)
    return score(table, mine, theirs, val_sketch, other_val, seq_count // 2)


def grad_rows(rows, cotangent, w_gate, w_up, proj_out):
    half_cols = proj_out.shape[1] // 2
    gate_pre = jnp.dot(rows, w_gate, preferred_element_type=jnp.float32)
    up_pre = jnp.dot(rows, w_up, preferred_element_type=jnp.float32)
    cotangent = cotangent.astype(jnp.float32)
    sigmoid_gate = jax.nn.sigmoid(gate_pre)
    grad_up = (cotangent * gate_pre * sigmoid_gate).astype(jnp.bfloat16)
    grad_gate = (
        cotangent * up_pre * sigmoid_gate * (1.0 + gate_pre * (1.0 - sigmoid_gate))
    ).astype(jnp.bfloat16)
    proj_gate = jnp.dot(grad_gate, proj_out[:, :half_cols], preferred_element_type=jnp.float32)
    proj_up = jnp.dot(grad_up, proj_out[:, half_cols:], preferred_element_type=jnp.float32)
    return jnp.concatenate([proj_gate, proj_up], axis=1)


def plain(order, tokens_in, out_grad, w_gate, w_up, proj_in, proj_out, lengths, val_sketch):
    n = len(order)
    rows = tokens_in.shape[0]
    seq_count = lengths.shape[0]
    rank = proj_in.shape[1]
    x = lax.all_gather(tokens_in, ("seq", "mp"), axis=0, tiled=True)
    grads = grad_rows(x, out_grad, w_gate, w_up, proj_out)
    acts = jnp.dot(x, proj_in, preferred_element_type=jnp.float32)
    ends = jnp.cumsum(lengths)
    position = lax.iota(jnp.int32, x.shape[0])[:, None]
    member = ((position >= (ends - lengths)[None, :]) & (position < ends[None, :])).astype(
        jnp.float32
    )
    weighted = (member[:, :, None] * acts[:, None, :]).reshape(x.shape[0], seq_count * rank)
    sketch = lax.dot_general(
        weighted, grads, (((0,), (0,)), ((), ())), precision=lax.Precision.HIGHEST
    )
    sketch = lax.psum(sketch, ("seq", "mp"))
    own = seq_count // lax.axis_size("seq")
    layered = sketch.reshape(seq_count, rank, 2, rank)
    layered = lax.dynamic_slice_in_dim(layered, lax.axis_index("seq") * own, own, 0)
    norm_scale = jnp.sqrt(jnp.mean(layered * layered, axis=(1, 3)) + eps_scale)
    normed = (layered / norm_scale[:, None, :, None]).reshape(own, 2 * rank * rank)
    full_val = lax.all_gather(val_sketch, "seq", axis=1, tiled=True)
    return lax.dot_general(
        normed,
        full_val.astype(jnp.float32),
        (((1,), (1,)), ((), ())),
        precision=lax.Precision.HIGHEST,
    )


def shards(order, tokens_in, out_grad, w_gate, w_up, proj_in, proj_out, lengths, val_sketch):
    n = len(order)
    rows, width = tokens_in.shape
    fits = (
        n >= 2
        and n & (n - 1) == 0
        and lax.axis_size("seq") == 2
        and rows % CHUNK == 0
        and w_gate.shape[1] % LANES == 0
        and width % LANES == 0
        and 2 * proj_in.shape[1] == LANES
        and lengths.shape[0] % 4 == 0
        and val_sketch.shape[1] == proj_in.shape[1] * LANES // 2
    )
    work = fast if fits else plain
    return work(
        order, tokens_in, out_grad, w_gate, w_up, proj_in, proj_out, lengths, val_sketch
    )


def solution(mesh):
    in_specs = (
        P(("groups", "seq", "mp"), None),
        P("groups", ("seq", "mp")),
        P(None, ("seq", "mp")),
        P(None, ("seq", "mp")),
        P(),
        P(("seq", "mp"), None),
        P("groups"),
        P("mp", "seq"),
    )
    out_specs = P(("groups", "seq"), "mp")
    return jax.shard_map(
        functools.partial(shards, ring_order(mesh)),
        mesh=mesh,
        in_specs=in_specs,
        out_specs=out_specs,
        check_vma=False,
    )
```

```python
import functools

import jax
import jax.numpy as jnp
import numpy as np
from jax import lax
from jax.experimental import pallas as pl
from jax.experimental.pallas import tpu as pltpu
from jax.sharding import PartitionSpec as P

eps_scale = 1e-06
LANES = 128
CHUNK = 32
ANY = pl.BlockSpec(memory_space=pl.ANY)
VMEM = pl.BlockSpec(memory_space=pltpu.VMEM)
SMEM = pl.BlockSpec(memory_space=pltpu.SMEM)


def ring_order(mesh):
    n = mesh.shape["mp"]
    line = list(mesh.devices[0, 0, :])
    natural = list(range(n))
    if n < 4 or not hasattr(line[0], "coords"):
        return natural
    first, third = line[0].coords, line[2].coords
    if sum(abs(a - b) for a, b in zip(first, third)) == 1:
        return natural[0::2] + natural[1::2][::-1]
    return natural


def ring_table(order, rows):
    n = len(order)
    table = []
    for core in range(2):
        for m in range(n):
            p, sign = order.index(m), 1 - 2 * core

            def row(c, shift):
                return (c * n + order[(p + shift) % n]) * rows

            line = [row(core, 0), row(1 - core, 0)]
            for k in range(1, n // 2):
                line += [row(core, -sign * k), row(1 - core, sign * k)]
                line += [row(core, sign * k), row(1 - core, -sign * k)]
            line += [row(core, n // 2), row(1 - core, n // 2), core]
            table.append(line)
    return np.array(table, np.int32)


def split(value):
    high = value.astype(jnp.bfloat16)
    return high, (value - high.astype(jnp.float32)).astype(jnp.bfloat16)


def gradients(pre, cotangents, both):
    hidden = both.shape[1] // 2
    for i, cotangent in enumerate(cotangents):
        here = slice(i * CHUNK, (i + 1) * CHUNK)
        gate = pre[here, :hidden]
        up = pre[here, hidden : 2 * hidden]
        sig = 0.5 * (1.0 + jnp.tanh(0.5 * gate))
        scaled = cotangent().astype(jnp.float32) * sig
        both[here, hidden:] = (scaled * gate).astype(jnp.bfloat16)
        both[here, :hidden] = (scaled * up * (1.0 + gate * (1.0 - sig))).astype(jnp.bfloat16)


def sketch_of(starts, rows, lengths, pre, both, diagonal):
    grads = jnp.dot(both[...], diagonal[...], preferred_element_type=jnp.float32)
    grads_high, grads_low = split(grads)
    grads_both = jnp.concatenate([grads_high, grads_low], axis=1)
    seq_count = lengths.shape[0]
    acts = pre[:, both.shape[1] :]
    position = []
    for start in starts:
        position.append(start + lax.broadcasted_iota(jnp.int32, (rows, LANES), 0))
    position = jnp.concatenate(position, axis=0)
    low = lax.broadcasted_iota(jnp.int32, (1, LANES), 1) < LANES // 2
    ends = []
    for s in range(seq_count):
        ends.append(lengths[s] + (ends[-1] if s else 0))
    highs, lows = [], []
    for g in range(seq_count // 2):
        begin = jnp.where(low, ends[2 * g - 1] if g else 0, ends[2 * g])
        end = jnp.where(low, ends[2 * g], ends[2 * g + 1])
        weighted = jnp.where((position >= begin) & (position < end), acts, 0.0)
        high, rest = split(weighted)
        highs.append(high)
        lows.append(rest)
    over_rows = (((0,), (0,)), ((), ()))
    main = lax.dot_general(
        jnp.concatenate(highs, axis=1),
        grads_both,
        over_rows,
        preferred_element_type=jnp.float32,
    )
    rest = lax.dot_general(
        jnp.concatenate(lows, axis=1), grads_high, over_rows, preferred_element_type=jnp.float32
    )
    return main[:, :LANES] + main[:, LANES:] + rest


def small_kernel(table, lengths, out_grad_hbm, proj_out_hbm, out_grad, diagonal, sems):
    hidden = proj_out_hbm.shape[0]
    upper = pltpu.make_async_copy(proj_out_hbm, diagonal.at[pl.ds(0, hidden)], sems.at[0])
    whole = pltpu.make_async_copy(out_grad_hbm, out_grad, sems.at[1])
    upper.start()
    whole.start()
    upper.wait()
    values = diagonal[:hidden, :]
    left = lax.broadcasted_iota(jnp.int32, values.shape, 1) < LANES // 2
    none = jnp.zeros_like(values)
    diagonal[hidden:, :] = jnp.where(left, none, values)
    diagonal[:hidden, :] = jnp.where(left, values, none)
    whole.wait()


def load_kernel(lengths, diagonal, gate_hbm, up_hbm, proj_in, w, total, sems):
    hidden = gate_hbm.shape[1]
    copies = [
        pltpu.make_async_copy(gate_hbm, w.at[:, pl.ds(0, hidden)], sems.at[0]),
        pltpu.make_async_copy(up_hbm, w.at[:, pl.ds(hidden, hidden)], sems.at[1]),
    ]
    for copy in copies:
        copy.start()
    w[:, 2 * hidden :] = jnp.concatenate([proj_in[...], proj_in[...]], axis=1)
    total[...] = jnp.zeros_like(total)
    for copy in copies:
        copy.wait()


def cotangent_chunks(out_grad, starts, rows):
    chunks = []
    for start in starts:
        for row in range(0, rows, CHUNK):
            here = pl.ds(pl.multiple_of(start + row, CHUNK), CHUNK)
            chunks.append(lambda here=here: out_grad[here, :])
    return chunks


def step_kernel(entry, last, table, lengths, one, two, w, out_grad, diagonal, before, *refs):
    outs, (pre, both) = refs[:-2], refs[-2:]
    rows = one.shape[0]
    starts = [table[entry], table[entry + 1]]
    x = jnp.concatenate([one[...], two[...]], axis=0)
    pre[...] = jnp.dot(x, w[...], preferred_element_type=jnp.float32)
    gradients(pre, cotangent_chunks(out_grad, starts, rows), both)
    total = before[...] + sketch_of(starts, rows, lengths, pre, both, diagonal)
    if not last:
        outs[0][...] = total
        return
    kept, sent = outs
    core = table[table.shape[0] - 1]
    half = total.shape[0] // 2
    upper, lower = total[:half, :], total[half:, :]
    kept[...] = jnp.where(core == 0, upper, lower)
    sent[...] = jnp.where(core == 0, lower, upper)


def costs(rows, width, columns):
    return pl.CostEstimate(
        flops=4 * rows * width * columns, bytes_accessed=2 * rows * width, transcendentals=0
    )


def load_small(table, lengths, out_grad, proj_out):
    out_grad, proj_out = [
        pltpu.with_memory_space_constraint(a, pltpu.HBM) for a in (out_grad, proj_out)
    ]
    hidden = out_grad.shape[1]
    return pl.pallas_call(
        small_kernel,
        out_shape=[
            pltpu.VMEM(out_grad.shape, jnp.bfloat16),
            pltpu.VMEM((2 * hidden, LANES), jnp.bfloat16),
        ],
        in_specs=[SMEM, SMEM, ANY, ANY],
        out_specs=[VMEM] * 2,
        scratch_shapes=[pltpu.SemaphoreType.DMA((2,))],
        compiler_params=pltpu.CompilerParams(vmem_limit_bytes=16 * 2**20),
    )(table, lengths, out_grad, proj_out)


def load(lengths, diagonal, w_gate, w_up, proj_in):
    width, hidden = w_gate.shape
    w_gate, w_up = [pltpu.with_memory_space_constraint(a, pltpu.HBM) for a in (w_gate, w_up)]
    return pl.pallas_call(
        load_kernel,
        out_shape=[
            pltpu.VMEM((width, 2 * hidden + LANES), jnp.bfloat16),
            jax.ShapeDtypeStruct((lengths.shape[0] * LANES // 2, LANES), jnp.float32),
        ],
        in_specs=[SMEM, VMEM, ANY, ANY, VMEM],
        out_specs=[VMEM] * 2,
        scratch_shapes=[pltpu.SemaphoreType.DMA((2,))],
        compiler_params=pltpu.CompilerParams(vmem_limit_bytes=16 * 2**20),
    )(lengths, diagonal, w_gate, w_up, proj_in)


def add_step(blocks, entry, total, table, lengths, weights, last=False):
    rows, width = blocks[0].shape
    w, _, diagonal = weights
    operands = [*blocks, *weights, total]
    out_rows = lengths.shape[0] * LANES // 2
    out_shape = [jax.ShapeDtypeStruct((out_rows, LANES), jnp.float32)]
    if last:
        out_shape = [jax.ShapeDtypeStruct((out_rows // 2, LANES), jnp.float32)] * 2
    outs = pl.pallas_call(
        functools.partial(step_kernel, entry, last),
        out_shape=out_shape,
        in_specs=[SMEM, SMEM] + [VMEM] * len(operands),
        out_specs=[VMEM] * len(out_shape),
        scratch_shapes=[
            pltpu.VMEM((2 * rows, w.shape[1]), jnp.float32),
            pltpu.VMEM((2 * rows, diagonal.shape[0]), jnp.bfloat16),
        ],
        compiler_params=pltpu.CompilerParams(vmem_limit_bytes=16 * 2**20),
        cost_estimate=costs(2 * rows, width, w.shape[1]),
    )(table, lengths, *operands)
    return outs if last else outs[0]


def score_kernel(table, mine, theirs, val_own, val_other, scores, sketch):
    core = table[table.shape[0] - 1]
    sketch[...] = mine[...] + theirs[...].astype(jnp.float32)
    own, rank = scores.shape[0], sketch.shape[0] // scores.shape[0]
    half = rank // 2
    left = lax.broadcasted_iota(jnp.int32, (own, LANES), 1) < LANES // 2
    squares = jnp.zeros((own, LANES), jnp.float32)
    found = jnp.zeros((4 * own, scores.shape[1]), jnp.float32)
    for side, val in ((core, val_own), (1 - core, val_other)):
        gates, ups = [], []
        for a in range(half):
            slab = sketch[pl.ds(side * half + a, own, stride=rank), :]
            squares += slab * slab
            gates.append(jnp.where(left, slab, 0.0))
            ups.append(jnp.where(left, 0.0, slab))
        gate_high, gate_low = split(jnp.concatenate(gates, axis=1))
        up_high, up_low = split(jnp.concatenate(ups, axis=1))
        found += lax.dot_general(
            jnp.concatenate([gate_high, gate_low, up_high, up_low], axis=0),
            val[...],
            (((1,), (1,)), ((), ())),
            preferred_element_type=jnp.float32,
        )
    count = rank * LANES // 2
    gate_mean = jnp.sum(jnp.where(left, squares, 0.0), axis=1, keepdims=True) / count
    up_mean = jnp.sum(jnp.where(left, 0.0, squares), axis=1, keepdims=True) / count
    gate_part = found[:own] + found[own : 2 * own]
    up_part = found[2 * own : 3 * own] + found[3 * own :]
    scores[...] = gate_part / jnp.sqrt(gate_mean + eps_scale) + up_part / jnp.sqrt(
        up_mean + eps_scale
    )


def score(table, mine, theirs, val_own, val_other, own):
    return pl.pallas_call(
        score_kernel,
        out_shape=jax.ShapeDtypeStruct((own, val_own.shape[0]), jnp.float32),
        in_specs=[SMEM, VMEM, VMEM, VMEM, VMEM],
        out_specs=VMEM,
        scratch_shapes=[pltpu.VMEM(mine.shape, jnp.float32)],
        compiler_params=pltpu.CompilerParams(vmem_limit_bytes=16 * 2**20),
    )(table, mine, theirs, val_own, val_other)


def fast(order, tokens_in, out_grad, w_gate, w_up, proj_in, proj_out, lengths, val_sketch):
    n = len(order)
    rows = tokens_in.shape[0]
    seq_count = lengths.shape[0]
    table = ring_table(order, rows)
    device = lax.axis_index("seq") * n + lax.axis_index("mp")
    table = lax.dynamic_index_in_dim(jnp.asarray(table), device, 0, keepdims=False)
    ahead = [(order[i], order[(i + 1) % n]) for i in range(n)]
    one = ahead + [(n + b, n + a) for a, b in ahead]
    send_one = functools.partial(lax.ppermute, axis_name=("seq", "mp"), perm=one)
    send_two = functools.partial(
        lax.ppermute, axis_name=("seq", "mp"), perm=[(b, a) for a, b in one]
    )
    swap = functools.partial(lax.ppermute, axis_name="seq", perm=[(0, 1), (1, 0)])

    after = lax.optimization_barrier
    one_way = send_one(tokens_in)
    other, other_val = swap(tokens_in), swap(val_sketch)
    out_grad, diagonal = load_small(table, lengths, out_grad, proj_out)
    later_tokens, diagonal = after((tokens_in, diagonal))
    two_way = send_two(later_tokens)
    w, total = load(lengths, diagonal, w_gate, w_up, proj_in)
    add = functools.partial(
        add_step, table=table, lengths=lengths, weights=[w, out_grad, diagonal]
    )

    waiting, entry = (tokens_in, other), 0
    for k in range(1, n // 2):
        one_way, total = after((one_way, total))
        next_one = send_one(one_way)
        swapped_one = swap(one_way)
        total = add(waiting, entry, total)
        two_way, total, other_val = after((two_way, total, other_val))
        next_two = send_two(two_way) if k + 1 < n // 2 else None
        total = add([one_way, swapped_one], entry + 2, total)
        entry += 4
        waiting = (two_way, swap(two_way))
        one_way, two_way = next_one, next_two
    one_way, total = after((one_way, total))
    swapped_one = swap(one_way)
    total = add(waiting, entry, total)
    kept, sent = add([one_way, swapped_one], entry + 2, total, last=True)

    mine, theirs = kept, swap(sent)
    bit = 1
    while bit < n:
        mine = mine + theirs
        sent = mine.astype(jnp.bfloat16)
        exchange = [bit]
        if bit == 1 and n >= 8:
            exchange = [1, 2, 3]
        got = [
            lax.ppermute(sent, "mp", [(i, i ^ flip) for i in range(n)]) for flip in exchange
        ]
        for part in got[:-1]:
            mine = mine + part.astype(jnp.float32)
        theirs = got[-1]
        bit = exchange[-1] + 1 if len(exchange) > 1 else 2 * bit
        if bit < n:
            theirs = theirs.astype(jnp.float32)
    return score(table, mine, theirs, val_sketch, other_val, seq_count // 2)


def grad_rows(rows, cotangent, w_gate, w_up, proj_out):
    half_cols = proj_out.shape[1] // 2
    gate_pre = jnp.dot(rows, w_gate, preferred_element_type=jnp.float32)
    up_pre = jnp.dot(rows, w_up, preferred_element_type=jnp.float32)
    cotangent = cotangent.astype(jnp.float32)
    sigmoid_gate = jax.nn.sigmoid(gate_pre)
    grad_up = (cotangent * gate_pre * sigmoid_gate).astype(jnp.bfloat16)
    grad_gate = (
        cotangent * up_pre * sigmoid_gate * (1.0 + gate_pre * (1.0 - sigmoid_gate))
    ).astype(jnp.bfloat16)
    proj_gate = jnp.dot(grad_gate, proj_out[:, :half_cols], preferred_element_type=jnp.float32)
    proj_up = jnp.dot(grad_up, proj_out[:, half_cols:], preferred_element_type=jnp.float32)
    return jnp.concatenate([proj_gate, proj_up], axis=1)


def plain(order, tokens_in, out_grad, w_gate, w_up, proj_in, proj_out, lengths, val_sketch):
    n = len(order)
    rows = tokens_in.shape[0]
    seq_count = lengths.shape[0]
    rank = proj_in.shape[1]
    x = lax.all_gather(tokens_in, ("seq", "mp"), axis=0, tiled=True)
    grads = grad_rows(x, out_grad, w_gate, w_up, proj_out)
    acts = jnp.dot(x, proj_in, preferred_element_type=jnp.float32)
    ends = jnp.cumsum(lengths)
    position = lax.iota(jnp.int32, x.shape[0])[:, None]
    member = ((position >= (ends - lengths)[None, :]) & (position < ends[None, :])).astype(
        jnp.float32
    )
    weighted = (member[:, :, None] * acts[:, None, :]).reshape(x.shape[0], seq_count * rank)
    sketch = lax.dot_general(
        weighted, grads, (((0,), (0,)), ((), ())), precision=lax.Precision.HIGHEST
    )
    sketch = lax.psum(sketch, ("seq", "mp"))
    own = seq_count // lax.axis_size("seq")
    layered = sketch.reshape(seq_count, rank, 2, rank)
    layered = lax.dynamic_slice_in_dim(layered, lax.axis_index("seq") * own, own, 0)
    norm_scale = jnp.sqrt(jnp.mean(layered * layered, axis=(1, 3)) + eps_scale)
    normed = (layered / norm_scale[:, None, :, None]).reshape(own, 2 * rank * rank)
    full_val = lax.all_gather(val_sketch, "seq", axis=1, tiled=True)
    return lax.dot_general(
        normed,
        full_val.astype(jnp.float32),
        (((1,), (1,)), ((), ())),
        precision=lax.Precision.HIGHEST,
    )


def shards(order, tokens_in, out_grad, w_gate, w_up, proj_in, proj_out, lengths, val_sketch):
    n = len(order)
    rows, width = tokens_in.shape
    fits = (
        n >= 2
        and n & (n - 1) == 0
        and lax.axis_size("seq") == 2
        and rows % CHUNK == 0
        and w_gate.shape[1] % LANES == 0
        and width % LANES == 0
        and 2 * proj_in.shape[1] == LANES
        and lengths.shape[0] % 4 == 0
        and val_sketch.shape[1] == proj_in.shape[1] * LANES // 2
    )
    work = fast if fits else plain
    return work(
        order, tokens_in, out_grad, w_gate, w_up, proj_in, proj_out, lengths, val_sketch
    )


def solution(mesh):
    in_specs = (
        P(("groups", "seq", "mp"), None),
        P("groups", ("seq", "mp")),
        P(None, ("seq", "mp")),
        P(None, ("seq", "mp")),
        P(),
        P(("seq", "mp"), None),
        P("groups"),
        P("mp", "seq"),
    )
    out_specs = P(("groups", "seq"), "mp")
    return jax.shard_map(
        functools.partial(shards, ring_order(mesh)),
        mesh=mesh,
        in_specs=in_specs,
        out_specs=out_specs,
        check_vma=False,
    )
```

```python
import functools

import jax
import jax.numpy as jnp
import numpy as np
from jax import lax
from jax.experimental import pallas as pl
from jax.experimental.pallas import tpu as pltpu
from jax.sharding import PartitionSpec as P

eps_scale = 1e-06
LANES = 128
CHUNK = 32
ANY = pl.BlockSpec(memory_space=pl.ANY)
VMEM = pl.BlockSpec(memory_space=pltpu.VMEM)
SMEM = pl.BlockSpec(memory_space=pltpu.SMEM)


def ring_order(mesh):
    n = mesh.shape["mp"]
    line = list(mesh.devices[0, 0, :])
    natural = list(range(n))
    if n < 4 or not hasattr(line[0], "coords"):
        return natural
    first, third = line[0].coords, line[2].coords
    if sum(abs(a - b) for a, b in zip(first, third)) == 1:
        return natural[0::2] + natural[1::2][::-1]
    return natural


def ring_table(order, rows):
    n = len(order)
    table = []
    for core in range(2):
        for m in range(n):
            p, sign = order.index(m), 1 - 2 * core

            def row(c, shift):
                return (c * n + order[(p + shift) % n]) * rows

            line = [row(core, 0), row(1 - core, 0)]
            for k in range(1, n // 2):
                line += [row(core, -sign * k), row(1 - core, sign * k)]
                line += [row(core, sign * k), row(1 - core, -sign * k)]
            line += [row(core, n // 2), row(1 - core, n // 2), core]
            table.append(line)
    return np.array(table, np.int32)


def split(value):
    high = value.astype(jnp.bfloat16)
    return high, (value - high.astype(jnp.float32)).astype(jnp.bfloat16)


def gradients(pre, cotangents, both):
    hidden = both.shape[1] // 2
    for i, cotangent in enumerate(cotangents):
        here = slice(i * CHUNK, (i + 1) * CHUNK)
        gate = pre[here, :hidden]
        up = pre[here, hidden : 2 * hidden]
        sig = 0.5 * (1.0 + jnp.tanh(0.5 * gate))
        scaled = cotangent().astype(jnp.float32) * sig
        both[here, hidden:] = (scaled * gate).astype(jnp.bfloat16)
        both[here, :hidden] = (scaled * up * (1.0 + gate * (1.0 - sig))).astype(jnp.bfloat16)


def sketch_of(starts, rows, lengths, pre, both, diagonal):
    grads = jnp.dot(both[...], diagonal[...], preferred_element_type=jnp.float32)
    grads_high, grads_low = split(grads)
    grads_both = jnp.concatenate([grads_high, grads_low], axis=1)
    seq_count = lengths.shape[0]
    acts = pre[:, both.shape[1] :]
    position = []
    for start in starts:
        position.append(start + lax.broadcasted_iota(jnp.int32, (rows, LANES), 0))
    position = jnp.concatenate(position, axis=0)
    low = lax.broadcasted_iota(jnp.int32, (1, LANES), 1) < LANES // 2
    ends = []
    for s in range(seq_count):
        ends.append(lengths[s] + (ends[-1] if s else 0))
    highs, lows = [], []
    for g in range(seq_count // 2):
        begin = jnp.where(low, ends[2 * g - 1] if g else 0, ends[2 * g])
        end = jnp.where(low, ends[2 * g], ends[2 * g + 1])
        weighted = jnp.where((position >= begin) & (position < end), acts, 0.0)
        high, rest = split(weighted)
        highs.append(high)
        lows.append(rest)
    over_rows = (((0,), (0,)), ((), ()))
    main = lax.dot_general(
        grads_both,
        jnp.concatenate(highs, axis=1),
        over_rows,
        preferred_element_type=jnp.float32,
    )
    rest = lax.dot_general(
        grads_high, jnp.concatenate(lows, axis=1), over_rows, preferred_element_type=jnp.float32
    )
    return main[:LANES, :] + main[LANES:, :] + rest


def small_kernel(table, lengths, out_grad_hbm, proj_out_hbm, out_grad, diagonal, sems):
    hidden = proj_out_hbm.shape[0]
    upper = pltpu.make_async_copy(proj_out_hbm, diagonal.at[pl.ds(0, hidden)], sems.at[0])
    whole = pltpu.make_async_copy(out_grad_hbm, out_grad, sems.at[1])
    upper.start()
    whole.start()
    upper.wait()
    values = diagonal[:hidden, :]
    left = lax.broadcasted_iota(jnp.int32, values.shape, 1) < LANES // 2
    none = jnp.zeros_like(values)
    diagonal[hidden:, :] = jnp.where(left, none, values)
    diagonal[:hidden, :] = jnp.where(left, values, none)
    whole.wait()


def load_kernel(lengths, diagonal, gate_hbm, up_hbm, proj_in, w, total, sems):
    hidden = gate_hbm.shape[1]
    copies = [
        pltpu.make_async_copy(gate_hbm, w.at[:, pl.ds(0, hidden)], sems.at[0]),
        pltpu.make_async_copy(up_hbm, w.at[:, pl.ds(hidden, hidden)], sems.at[1]),
    ]
    for copy in copies:
        copy.start()
    w[:, 2 * hidden :] = jnp.concatenate([proj_in[...], proj_in[...]], axis=1)
    total[...] = jnp.zeros_like(total)
    for copy in copies:
        copy.wait()


def cotangent_chunks(out_grad, starts, rows):
    chunks = []
    for start in starts:
        for row in range(0, rows, CHUNK):
            here = pl.ds(pl.multiple_of(start + row, CHUNK), CHUNK)
            chunks.append(lambda here=here: out_grad[here, :])
    return chunks


def step_kernel(count, entry, last, table, lengths, *refs):
    blocks, (w, out_grad, diagonal, before) = refs[:count], refs[count : count + 4]
    outs, (pre, both) = refs[count + 4 : -2], refs[-2:]
    rows = blocks[0].shape[0]
    starts = [table[entry + i] for i in range(count)]
    x = jnp.concatenate([block[...] for block in blocks], axis=0)
    pre[...] = jnp.dot(x, w[...], preferred_element_type=jnp.float32)
    gradients(pre, cotangent_chunks(out_grad, starts, rows), both)
    total = before[...] + sketch_of(starts, rows, lengths, pre, both, diagonal)
    if not last:
        outs[0][...] = total
        return
    kept, sent = outs
    core = table[table.shape[0] - 1]
    half = total.shape[1] // 2
    upper, lower = total[:, :half], total[:, half:]
    kept[...] = jnp.where(core == 0, upper, lower)
    sent[...] = jnp.where(core == 0, lower, upper)


def costs(rows, width, columns):
    return pl.CostEstimate(
        flops=40 * rows * width * columns, bytes_accessed=2 * rows * width, transcendentals=0
    )


def load_small(table, lengths, out_grad, proj_out):
    out_grad, proj_out = [
        pltpu.with_memory_space_constraint(a, pltpu.HBM) for a in (out_grad, proj_out)
    ]
    hidden = out_grad.shape[1]
    return pl.pallas_call(
        small_kernel,
        out_shape=[
            pltpu.VMEM(out_grad.shape, jnp.bfloat16),
            pltpu.VMEM((2 * hidden, LANES), jnp.bfloat16),
        ],
        in_specs=[SMEM, SMEM, ANY, ANY],
        out_specs=[VMEM] * 2,
        scratch_shapes=[pltpu.SemaphoreType.DMA((2,))],
        compiler_params=pltpu.CompilerParams(vmem_limit_bytes=16 * 2**20),
    )(table, lengths, out_grad, proj_out)


def load(lengths, diagonal, w_gate, w_up, proj_in):
    width, hidden = w_gate.shape
    w_gate, w_up = [pltpu.with_memory_space_constraint(a, pltpu.HBM) for a in (w_gate, w_up)]
    return pl.pallas_call(
        load_kernel,
        out_shape=[
            pltpu.VMEM((width, 2 * hidden + LANES), jnp.bfloat16),
            jax.ShapeDtypeStruct((LANES, lengths.shape[0] * LANES // 2), jnp.float32),
        ],
        in_specs=[SMEM, VMEM, ANY, ANY, VMEM],
        out_specs=[VMEM] * 2,
        scratch_shapes=[pltpu.SemaphoreType.DMA((2,))],
        compiler_params=pltpu.CompilerParams(vmem_limit_bytes=16 * 2**20),
    )(lengths, diagonal, w_gate, w_up, proj_in)


def add_step(blocks, entry, total, table, lengths, weights, last=False):
    count, (rows, width) = len(blocks), blocks[0].shape
    w, _, diagonal = weights
    operands = [*blocks, *weights, total]
    out_shape = [jax.ShapeDtypeStruct(total.shape, jnp.float32)]
    if last:
        out_shape = [jax.ShapeDtypeStruct((LANES, total.shape[1] // 2), jnp.float32)] * 2
    outs = pl.pallas_call(
        functools.partial(step_kernel, count, entry, last),
        out_shape=out_shape,
        in_specs=[SMEM, SMEM] + [VMEM] * len(operands),
        out_specs=[VMEM] * len(out_shape),
        scratch_shapes=[
            pltpu.VMEM((count * rows, w.shape[1]), jnp.float32),
            pltpu.VMEM((count * rows, diagonal.shape[0]), jnp.bfloat16),
        ],
        compiler_params=pltpu.CompilerParams(vmem_limit_bytes=16 * 2**20),
        cost_estimate=costs(count * rows, width, w.shape[1]),
    )(table, lengths, *operands)
    return outs if last else outs[0]


def score_kernel(table, mine, theirs, val_own, val_other, scores, sketch):
    core = table[table.shape[0] - 1]
    sketch[...] = (mine[...] + theirs[...].astype(jnp.float32)).T
    own, rank = scores.shape[0], sketch.shape[0] // scores.shape[0]
    half = rank // 2
    left = lax.broadcasted_iota(jnp.int32, (own, LANES), 1) < LANES // 2
    squares = jnp.zeros((own, LANES), jnp.float32)
    found = jnp.zeros((4 * own, scores.shape[1]), jnp.float32)
    for side, val in ((core, val_own), (1 - core, val_other)):
        gates, ups = [], []
        for a in range(half):
            slab = sketch[pl.ds(side * half + a, own, stride=rank), :]
            squares += slab * slab
            gates.append(jnp.where(left, slab, 0.0))
            ups.append(jnp.where(left, 0.0, slab))
        gate_high, gate_low = split(jnp.concatenate(gates, axis=1))
        up_high, up_low = split(jnp.concatenate(ups, axis=1))
        found += lax.dot_general(
            jnp.concatenate([gate_high, gate_low, up_high, up_low], axis=0),
            val[...],
            (((1,), (1,)), ((), ())),
            preferred_element_type=jnp.float32,
        )
    count = rank * LANES // 2
    gate_mean = jnp.sum(jnp.where(left, squares, 0.0), axis=1, keepdims=True) / count
    up_mean = jnp.sum(jnp.where(left, 0.0, squares), axis=1, keepdims=True) / count
    gate_part = found[:own] + found[own : 2 * own]
    up_part = found[2 * own : 3 * own] + found[3 * own :]
    scores[...] = gate_part / jnp.sqrt(gate_mean + eps_scale) + up_part / jnp.sqrt(
        up_mean + eps_scale
    )


def score(table, mine, theirs, val_own, val_other, own):
    return pl.pallas_call(
        score_kernel,
        out_shape=jax.ShapeDtypeStruct((own, val_own.shape[0]), jnp.float32),
        in_specs=[SMEM, VMEM, VMEM, VMEM, VMEM],
        out_specs=VMEM,
        scratch_shapes=[pltpu.VMEM(mine.shape[::-1], jnp.float32)],
        compiler_params=pltpu.CompilerParams(vmem_limit_bytes=16 * 2**20),
    )(table, mine, theirs, val_own, val_other)


def fast(order, tokens_in, out_grad, w_gate, w_up, proj_in, proj_out, lengths, val_sketch):
    n = len(order)
    rows = tokens_in.shape[0]
    seq_count = lengths.shape[0]
    table = ring_table(order, rows)
    device = lax.axis_index("seq") * n + lax.axis_index("mp")
    table = lax.dynamic_index_in_dim(jnp.asarray(table), device, 0, keepdims=False)
    ahead = [(order[i], order[(i + 1) % n]) for i in range(n)]
    one = ahead + [(n + b, n + a) for a, b in ahead]
    send_one = functools.partial(lax.ppermute, axis_name=("seq", "mp"), perm=one)
    send_two = functools.partial(
        lax.ppermute, axis_name=("seq", "mp"), perm=[(b, a) for a, b in one]
    )
    swap = functools.partial(lax.ppermute, axis_name="seq", perm=[(0, 1), (1, 0)])

    after = lax.optimization_barrier
    one_way = send_one(tokens_in)
    other, other_val = swap(tokens_in), swap(val_sketch)
    out_grad, diagonal = load_small(table, lengths, out_grad, proj_out)
    later_tokens, diagonal = after((tokens_in, diagonal))
    two_way = send_two(later_tokens)
    w, total = load(lengths, diagonal, w_gate, w_up, proj_in)
    add = functools.partial(
        add_step, table=table, lengths=lengths, weights=[w, out_grad, diagonal]
    )

    streams = [(one_way, send_one), (two_way, send_two)]
    waiting, entry = [[tokens_in, other]], 0
    arrivals = n - 1
    for i in range(arrivals):
        block, send = streams[i % 2]
        if i == 1:
            block, total, other_val = after((block, total, other_val))
        else:
            block, total = after((block, total))
        streams[i % 2] = (send(block) if i + 2 < arrivals else None, send)
        if i == arrivals - 1:
            total = add([block], entry, total)
            kept, sent = add([swap(block)], entry + 1, total, last=True)
            break
        waiting.append([block, swap(block)])
        while waiting and (len(waiting) > 1 or i >= arrivals - 2):
            total = add(waiting.pop(0), entry, total)
            entry += 2

    mine, theirs = kept, swap(sent)
    bit = 1
    while bit < n:
        mine = mine + theirs
        sent = mine.astype(jnp.bfloat16)
        exchange = [bit]
        if bit == 1 and n >= 8:
            exchange = [1, 2, 3]
        got = [
            lax.ppermute(sent, "mp", [(i, i ^ flip) for i in range(n)]) for flip in exchange
        ]
        for part in got[:-1]:
            mine = mine + part.astype(jnp.float32)
        theirs = got[-1]
        bit = exchange[-1] + 1 if len(exchange) > 1 else 2 * bit
        if bit < n:
            theirs = theirs.astype(jnp.float32)
    return score(table, mine, theirs, val_sketch, other_val, seq_count // 2)


def grad_rows(rows, cotangent, w_gate, w_up, proj_out):
    half_cols = proj_out.shape[1] // 2
    gate_pre = jnp.dot(rows, w_gate, preferred_element_type=jnp.float32)
    up_pre = jnp.dot(rows, w_up, preferred_element_type=jnp.float32)
    cotangent = cotangent.astype(jnp.float32)
    sigmoid_gate = jax.nn.sigmoid(gate_pre)
    grad_up = (cotangent * gate_pre * sigmoid_gate).astype(jnp.bfloat16)
    grad_gate = (
        cotangent * up_pre * sigmoid_gate * (1.0 + gate_pre * (1.0 - sigmoid_gate))
    ).astype(jnp.bfloat16)
    proj_gate = jnp.dot(grad_gate, proj_out[:, :half_cols], preferred_element_type=jnp.float32)
    proj_up = jnp.dot(grad_up, proj_out[:, half_cols:], preferred_element_type=jnp.float32)
    return jnp.concatenate([proj_gate, proj_up], axis=1)


def plain(order, tokens_in, out_grad, w_gate, w_up, proj_in, proj_out, lengths, val_sketch):
    n = len(order)
    rows = tokens_in.shape[0]
    seq_count = lengths.shape[0]
    rank = proj_in.shape[1]
    x = lax.all_gather(tokens_in, ("seq", "mp"), axis=0, tiled=True)
    grads = grad_rows(x, out_grad, w_gate, w_up, proj_out)
    acts = jnp.dot(x, proj_in, preferred_element_type=jnp.float32)
    ends = jnp.cumsum(lengths)
    position = lax.iota(jnp.int32, x.shape[0])[:, None]
    member = ((position >= (ends - lengths)[None, :]) & (position < ends[None, :])).astype(
        jnp.float32
    )
    weighted = (member[:, :, None] * acts[:, None, :]).reshape(x.shape[0], seq_count * rank)
    sketch = lax.dot_general(
        weighted, grads, (((0,), (0,)), ((), ())), precision=lax.Precision.HIGHEST
    )
    sketch = lax.psum(sketch, ("seq", "mp"))
    own = seq_count // lax.axis_size("seq")
    layered = sketch.reshape(seq_count, rank, 2, rank)
    layered = lax.dynamic_slice_in_dim(layered, lax.axis_index("seq") * own, own, 0)
    norm_scale = jnp.sqrt(jnp.mean(layered * layered, axis=(1, 3)) + eps_scale)
    normed = (layered / norm_scale[:, None, :, None]).reshape(own, 2 * rank * rank)
    full_val = lax.all_gather(val_sketch, "seq", axis=1, tiled=True)
    return lax.dot_general(
        normed,
        full_val.astype(jnp.float32),
        (((1,), (1,)), ((), ())),
        precision=lax.Precision.HIGHEST,
    )


def shards(order, tokens_in, out_grad, w_gate, w_up, proj_in, proj_out, lengths, val_sketch):
    n = len(order)
    rows, width = tokens_in.shape
    fits = (
        n >= 2
        and n & (n - 1) == 0
        and lax.axis_size("seq") == 2
        and rows % CHUNK == 0
        and w_gate.shape[1] % LANES == 0
        and width % LANES == 0
        and 2 * proj_in.shape[1] == LANES
        and lengths.shape[0] % 4 == 0
        and val_sketch.shape[1] == proj_in.shape[1] * LANES // 2
    )
    work = fast if fits else plain
    return work(
        order, tokens_in, out_grad, w_gate, w_up, proj_in, proj_out, lengths, val_sketch
    )


def solution(mesh):
    in_specs = (
        P(("groups", "seq", "mp"), None),
        P("groups", ("seq", "mp")),
        P(None, ("seq", "mp")),
        P(None, ("seq", "mp")),
        P(),
        P(("seq", "mp"), None),
        P("groups"),
        P("mp", "seq"),
    )
    out_specs = P(("groups", "seq"), "mp")
    return jax.shard_map(
        functools.partial(shards, ring_order(mesh)),
        mesh=mesh,
        in_specs=in_specs,
        out_specs=out_specs,
        check_vma=False,
    )
```

```python
import functools

import jax
import jax.numpy as jnp
import numpy as np
from jax import lax
from jax.experimental import pallas as pl
from jax.experimental.pallas import tpu as pltpu
from jax.sharding import PartitionSpec as P

eps_scale = 1e-06
LANES = 128
CHUNK = 32
ANY = pl.BlockSpec(memory_space=pl.ANY)
VMEM = pl.BlockSpec(memory_space=pltpu.VMEM)
SMEM = pl.BlockSpec(memory_space=pltpu.SMEM)


def ring_order(mesh):
    n = mesh.shape["mp"]
    line = list(mesh.devices[0, 0, :])
    natural = list(range(n))
    if n < 4 or not hasattr(line[0], "coords"):
        return natural
    first, third = line[0].coords, line[2].coords
    if sum(abs(a - b) for a, b in zip(first, third)) == 1:
        return natural[0::2] + natural[1::2][::-1]
    return natural


def ring_table(order, rows):
    n = len(order)
    table = []
    for core in range(2):
        for m in range(n):
            p, sign = order.index(m), 1 - 2 * core

            def row(c, shift):
                return (c * n + order[(p + shift) % n]) * rows

            line = [row(core, 0), row(1 - core, 0)]
            for k in range(1, n // 2):
                line += [row(core, -sign * k), row(1 - core, sign * k)]
                line += [row(core, sign * k), row(1 - core, -sign * k)]
            line += [row(core, n // 2), row(1 - core, n // 2), core]
            table.append(line)
    return np.array(table, np.int32)


def split(value):
    high = value.astype(jnp.bfloat16)
    return high, (value - high.astype(jnp.float32)).astype(jnp.bfloat16)


def gradients(pre, cotangents, both):
    hidden = both.shape[1] // 2
    for i, cotangent in enumerate(cotangents):
        here = slice(i * CHUNK, (i + 1) * CHUNK)
        gate = pre[here, :hidden]
        up = pre[here, hidden : 2 * hidden]
        sig = 0.5 * (1.0 + jnp.tanh(0.5 * gate))
        scaled = cotangent().astype(jnp.float32) * sig
        both[here, hidden:] = (scaled * gate).astype(jnp.bfloat16)
        both[here, :hidden] = (scaled * up * (1.0 + gate * (1.0 - sig))).astype(jnp.bfloat16)


def sketch_of(starts, rows, lengths, pre, both, diagonal):
    grads = jnp.dot(both[...], diagonal[...], preferred_element_type=jnp.float32)
    grads_high, grads_low = split(grads)
    grads_both = jnp.concatenate([grads_high, grads_low], axis=1)
    seq_count = lengths.shape[0]
    acts = pre[:, both.shape[1] :]
    position = []
    for start in starts:
        position.append(start + lax.broadcasted_iota(jnp.int32, (rows, LANES), 0))
    position = jnp.concatenate(position, axis=0)
    low = lax.broadcasted_iota(jnp.int32, (1, LANES), 1) < LANES // 2
    ends = []
    for s in range(seq_count):
        ends.append(lengths[s] + (ends[-1] if s else 0))
    highs, lows = [], []
    for g in range(seq_count // 2):
        begin = jnp.where(low, ends[2 * g - 1] if g else 0, ends[2 * g])
        end = jnp.where(low, ends[2 * g], ends[2 * g + 1])
        weighted = jnp.where((position >= begin) & (position < end), acts, 0.0)
        high, rest = split(weighted)
        highs.append(high)
        lows.append(rest)
    over_rows = (((0,), (0,)), ((), ()))
    main = lax.dot_general(
        jnp.concatenate(highs, axis=1),
        grads_both,
        over_rows,
        preferred_element_type=jnp.float32,
    )
    rest = lax.dot_general(
        jnp.concatenate(lows, axis=1), grads_high, over_rows, preferred_element_type=jnp.float32
    )
    return main[:, :LANES] + main[:, LANES:] + rest


def small_kernel(table, lengths, out_grad_hbm, proj_out_hbm, out_grad, diagonal, sems):
    hidden = proj_out_hbm.shape[0]
    upper = pltpu.make_async_copy(proj_out_hbm, diagonal.at[pl.ds(0, hidden)], sems.at[0])
    whole = pltpu.make_async_copy(out_grad_hbm, out_grad, sems.at[1])
    upper.start()
    whole.start()
    upper.wait()
    values = diagonal[:hidden, :]
    left = lax.broadcasted_iota(jnp.int32, values.shape, 1) < LANES // 2
    none = jnp.zeros_like(values)
    diagonal[hidden:, :] = jnp.where(left, none, values)
    diagonal[:hidden, :] = jnp.where(left, values, none)
    whole.wait()


def load_kernel(lengths, diagonal, gate_hbm, up_hbm, proj_in, w, total, sems):
    hidden = gate_hbm.shape[1]
    copies = [
        pltpu.make_async_copy(gate_hbm, w.at[:, pl.ds(0, hidden)], sems.at[0]),
        pltpu.make_async_copy(up_hbm, w.at[:, pl.ds(hidden, hidden)], sems.at[1]),
    ]
    for copy in copies:
        copy.start()
    w[:, 2 * hidden :] = jnp.concatenate([proj_in[...], proj_in[...]], axis=1)
    total[...] = jnp.zeros_like(total)
    for copy in copies:
        copy.wait()


def cotangent_chunks(out_grad, starts, rows):
    chunks = []
    for start in starts:
        for row in range(0, rows, CHUNK):
            here = pl.ds(pl.multiple_of(start + row, CHUNK), CHUNK)
            chunks.append(lambda here=here: out_grad[here, :])
    return chunks


def step_kernel(entry, last, table, lengths, one, two, w, out_grad, diagonal, before, *refs):
    outs, (pre, both) = refs[:-2], refs[-2:]
    rows = one.shape[0]
    starts = [table[entry], table[entry + 1]]
    x = jnp.concatenate([one[...], two[...]], axis=0)
    pre[...] = jnp.dot(x, w[...], preferred_element_type=jnp.float32)
    gradients(pre, cotangent_chunks(out_grad, starts, rows), both)
    total = before[...] + sketch_of(starts, rows, lengths, pre, both, diagonal)
    if not last:
        outs[0][...] = total
        return
    kept, sent = outs
    core = table[table.shape[0] - 1]
    half = total.shape[0] // 2
    upper, lower = total[:half, :], total[half:, :]
    kept[...] = jnp.where(core == 0, upper, lower)
    sent[...] = jnp.where(core == 0, lower, upper)


def costs(rows, width, columns):
    return pl.CostEstimate(
        flops=4 * rows * width * columns, bytes_accessed=2 * rows * width, transcendentals=0
    )


def load_small(table, lengths, out_grad, proj_out):
    out_grad, proj_out = [
        pltpu.with_memory_space_constraint(a, pltpu.HBM) for a in (out_grad, proj_out)
    ]
    hidden = out_grad.shape[1]
    return pl.pallas_call(
        small_kernel,
        out_shape=[
            pltpu.VMEM(out_grad.shape, jnp.bfloat16),
            pltpu.VMEM((2 * hidden, LANES), jnp.bfloat16),
        ],
        in_specs=[SMEM, SMEM, ANY, ANY],
        out_specs=[VMEM] * 2,
        scratch_shapes=[pltpu.SemaphoreType.DMA((2,))],
        compiler_params=pltpu.CompilerParams(vmem_limit_bytes=16 * 2**20),
    )(table, lengths, out_grad, proj_out)


def load(lengths, diagonal, w_gate, w_up, proj_in):
    width, hidden = w_gate.shape
    w_gate, w_up = [pltpu.with_memory_space_constraint(a, pltpu.HBM) for a in (w_gate, w_up)]
    return pl.pallas_call(
        load_kernel,
        out_shape=[
            pltpu.VMEM((width, 2 * hidden + LANES), jnp.bfloat16),
            jax.ShapeDtypeStruct((lengths.shape[0] * LANES // 2, LANES), jnp.float32),
        ],
        in_specs=[SMEM, VMEM, ANY, ANY, VMEM],
        out_specs=[VMEM] * 2,
        scratch_shapes=[pltpu.SemaphoreType.DMA((2,))],
        compiler_params=pltpu.CompilerParams(vmem_limit_bytes=16 * 2**20),
    )(lengths, diagonal, w_gate, w_up, proj_in)


def add_step(blocks, entry, total, table, lengths, weights, last=False):
    rows, width = blocks[0].shape
    w, _, diagonal = weights
    operands = [*blocks, *weights, total]
    out_rows = lengths.shape[0] * LANES // 2
    out_shape = [jax.ShapeDtypeStruct((out_rows, LANES), jnp.float32)]
    if last:
        out_shape = [jax.ShapeDtypeStruct((out_rows // 2, LANES), jnp.float32)] * 2
    outs = pl.pallas_call(
        functools.partial(step_kernel, entry, last),
        out_shape=out_shape,
        in_specs=[SMEM, SMEM] + [VMEM] * len(operands),
        out_specs=[VMEM] * len(out_shape),
        scratch_shapes=[
            pltpu.VMEM((2 * rows, w.shape[1]), jnp.float32),
            pltpu.VMEM((2 * rows, diagonal.shape[0]), jnp.bfloat16),
        ],
        compiler_params=pltpu.CompilerParams(vmem_limit_bytes=16 * 2**20),
        cost_estimate=costs(2 * rows, width, w.shape[1]),
    )(table, lengths, *operands)
    return outs if last else outs[0]


def score_kernel(table, mine, theirs, val_own, val_other, scores, sketch):
    core = table[table.shape[0] - 1]
    sketch[...] = mine[...] + theirs[...].astype(jnp.float32)
    own, rank = scores.shape[0], sketch.shape[0] // scores.shape[0]
    half = rank // 2
    left = lax.broadcasted_iota(jnp.int32, (own, LANES), 1) < LANES // 2
    squares = jnp.zeros((own, LANES), jnp.float32)
    rows = []
    for side in (core, 1 - core):
        gates, ups = [], []
        for a in range(half):
            slab = sketch[pl.ds(side * half + a, own, stride=rank), :]
            squares += slab * slab
            gates.append(jnp.where(left, slab, 0.0))
            ups.append(jnp.where(left, 0.0, slab))
        rows += [*split(jnp.concatenate(gates, axis=1)), *split(jnp.concatenate(ups, axis=1))]
    products = lax.dot_general(
        jnp.concatenate(rows, axis=0),
        jnp.concatenate([val_own[...], val_other[...]], axis=0),
        (((1,), (1,)), ((), ())),
        preferred_element_type=jnp.float32,
    )
    columns = scores.shape[1]
    found = products[: 4 * own, :columns] + products[4 * own :, columns:]
    count = rank * LANES // 2
    gate_mean = jnp.sum(jnp.where(left, squares, 0.0), axis=1, keepdims=True) / count
    up_mean = jnp.sum(jnp.where(left, 0.0, squares), axis=1, keepdims=True) / count
    gate_part = found[:own] + found[own : 2 * own]
    up_part = found[2 * own : 3 * own] + found[3 * own :]
    scores[...] = gate_part / jnp.sqrt(gate_mean + eps_scale) + up_part / jnp.sqrt(
        up_mean + eps_scale
    )


def score(table, mine, theirs, val_own, val_other, own):
    return pl.pallas_call(
        score_kernel,
        out_shape=jax.ShapeDtypeStruct((own, val_own.shape[0]), jnp.float32),
        in_specs=[SMEM, VMEM, VMEM, VMEM, VMEM],
        out_specs=VMEM,
        scratch_shapes=[pltpu.VMEM(mine.shape, jnp.float32)],
        compiler_params=pltpu.CompilerParams(vmem_limit_bytes=16 * 2**20),
    )(table, mine, theirs, val_own, val_other)


def fast(order, tokens_in, out_grad, w_gate, w_up, proj_in, proj_out, lengths, val_sketch):
    n = len(order)
    rows = tokens_in.shape[0]
    seq_count = lengths.shape[0]
    table = ring_table(order, rows)
    device = lax.axis_index("seq") * n + lax.axis_index("mp")
    table = lax.dynamic_index_in_dim(jnp.asarray(table), device, 0, keepdims=False)
    ahead = [(order[i], order[(i + 1) % n]) for i in range(n)]
    one = ahead + [(n + b, n + a) for a, b in ahead]
    send_one = functools.partial(lax.ppermute, axis_name=("seq", "mp"), perm=one)
    send_two = functools.partial(
        lax.ppermute, axis_name=("seq", "mp"), perm=[(b, a) for a, b in one]
    )
    swap = functools.partial(lax.ppermute, axis_name="seq", perm=[(0, 1), (1, 0)])

    after = lax.optimization_barrier
    one_way = send_one(tokens_in)
    other, other_val = swap(tokens_in), swap(val_sketch)
    out_grad, diagonal = load_small(table, lengths, out_grad, proj_out)
    later_tokens, diagonal = after((tokens_in, diagonal))
    two_way = send_two(later_tokens)
    w, total = load(lengths, diagonal, w_gate, w_up, proj_in)
    add = functools.partial(
        add_step, table=table, lengths=lengths, weights=[w, out_grad, diagonal]
    )

    waiting, entry = (tokens_in, other), 0
    for k in range(1, n // 2):
        one_way, total = after((one_way, total))
        next_one = send_one(one_way)
        swapped_one = swap(one_way)
        total = add(waiting, entry, total)
        two_way, total, other_val = after((two_way, total, other_val))
        next_two = send_two(two_way) if k + 1 < n // 2 else None
        total = add([one_way, swapped_one], entry + 2, total)
        entry += 4
        waiting = (two_way, swap(two_way))
        one_way, two_way = next_one, next_two
    one_way, total = after((one_way, total))
    swapped_one = swap(one_way)
    total = add(waiting, entry, total)
    kept, sent = add([one_way, swapped_one], entry + 2, total, last=True)

    mine, theirs = kept, swap(sent)
    bit = 1
    while bit < n:
        mine = mine + theirs
        sent = mine.astype(jnp.bfloat16)
        exchange = [bit]
        if bit == 1 and n >= 8:
            exchange = [3, 2, 1]
        got = [
            lax.ppermute(sent, "mp", [(i, i ^ flip) for i in range(n)]) for flip in exchange
        ]
        for part in got[:-1]:
            mine = mine + part.astype(jnp.float32)
        theirs = got[-1]
        bit = 4 if len(exchange) > 1 else 2 * bit
        if bit < n:
            theirs = theirs.astype(jnp.float32)
    return score(table, mine, theirs, val_sketch, other_val, seq_count // 2)


def grad_rows(rows, cotangent, w_gate, w_up, proj_out):
    half_cols = proj_out.shape[1] // 2
    gate_pre = jnp.dot(rows, w_gate, preferred_element_type=jnp.float32)
    up_pre = jnp.dot(rows, w_up, preferred_element_type=jnp.float32)
    cotangent = cotangent.astype(jnp.float32)
    sigmoid_gate = jax.nn.sigmoid(gate_pre)
    grad_up = (cotangent * gate_pre * sigmoid_gate).astype(jnp.bfloat16)
    grad_gate = (
        cotangent * up_pre * sigmoid_gate * (1.0 + gate_pre * (1.0 - sigmoid_gate))
    ).astype(jnp.bfloat16)
    proj_gate = jnp.dot(grad_gate, proj_out[:, :half_cols], preferred_element_type=jnp.float32)
    proj_up = jnp.dot(grad_up, proj_out[:, half_cols:], preferred_element_type=jnp.float32)
    return jnp.concatenate([proj_gate, proj_up], axis=1)


def plain(order, tokens_in, out_grad, w_gate, w_up, proj_in, proj_out, lengths, val_sketch):
    n = len(order)
    rows = tokens_in.shape[0]
    seq_count = lengths.shape[0]
    rank = proj_in.shape[1]
    x = lax.all_gather(tokens_in, ("seq", "mp"), axis=0, tiled=True)
    grads = grad_rows(x, out_grad, w_gate, w_up, proj_out)
    acts = jnp.dot(x, proj_in, preferred_element_type=jnp.float32)
    ends = jnp.cumsum(lengths)
    position = lax.iota(jnp.int32, x.shape[0])[:, None]
    member = ((position >= (ends - lengths)[None, :]) & (position < ends[None, :])).astype(
        jnp.float32
    )
    weighted = (member[:, :, None] * acts[:, None, :]).reshape(x.shape[0], seq_count * rank)
    sketch = lax.dot_general(
        weighted, grads, (((0,), (0,)), ((), ())), precision=lax.Precision.HIGHEST
    )
    sketch = lax.psum(sketch, ("seq", "mp"))
    own = seq_count // lax.axis_size("seq")
    layered = sketch.reshape(seq_count, rank, 2, rank)
    layered = lax.dynamic_slice_in_dim(layered, lax.axis_index("seq") * own, own, 0)
    norm_scale = jnp.sqrt(jnp.mean(layered * layered, axis=(1, 3)) + eps_scale)
    normed = (layered / norm_scale[:, None, :, None]).reshape(own, 2 * rank * rank)
    full_val = lax.all_gather(val_sketch, "seq", axis=1, tiled=True)
    return lax.dot_general(
        normed,
        full_val.astype(jnp.float32),
        (((1,), (1,)), ((), ())),
        precision=lax.Precision.HIGHEST,
    )


def shards(order, tokens_in, out_grad, w_gate, w_up, proj_in, proj_out, lengths, val_sketch):
    n = len(order)
    rows, width = tokens_in.shape
    fits = (
        n >= 2
        and n & (n - 1) == 0
        and lax.axis_size("seq") == 2
        and rows % CHUNK == 0
        and w_gate.shape[1] % LANES == 0
        and width % LANES == 0
        and 2 * proj_in.shape[1] == LANES
        and lengths.shape[0] % 4 == 0
        and val_sketch.shape[1] == proj_in.shape[1] * LANES // 2
    )
    work = fast if fits else plain
    return work(
        order, tokens_in, out_grad, w_gate, w_up, proj_in, proj_out, lengths, val_sketch
    )


def solution(mesh):
    in_specs = (
        P(("groups", "seq", "mp"), None),
        P("groups", ("seq", "mp")),
        P(None, ("seq", "mp")),
        P(None, ("seq", "mp")),
        P(),
        P(("seq", "mp"), None),
        P("groups"),
        P("mp", "seq"),
    )
    out_specs = P(("groups", "seq"), "mp")
    return jax.shard_map(
        functools.partial(shards, ring_order(mesh)),
        mesh=mesh,
        in_specs=in_specs,
        out_specs=out_specs,
        check_vma=False,
    )
```

```python
import functools

import jax
import jax.numpy as jnp
import numpy as np
from jax import lax
from jax.experimental import pallas as pl
from jax.experimental.pallas import tpu as pltpu
from jax.sharding import PartitionSpec as P

eps_scale = 1e-06
LANES = 128
CHUNK = 32
ANY = pl.BlockSpec(memory_space=pl.ANY)
VMEM = pl.BlockSpec(memory_space=pltpu.VMEM)
SMEM = pl.BlockSpec(memory_space=pltpu.SMEM)


def ring_order(mesh):
    n = mesh.shape["mp"]
    line = list(mesh.devices[0, 0, :])
    natural = list(range(n))
    if n < 4 or not hasattr(line[0], "coords"):
        return natural
    first, third = line[0].coords, line[2].coords
    if sum(abs(a - b) for a, b in zip(first, third)) == 1:
        return natural[0::2] + natural[1::2][::-1]
    return natural


def ring_table(order, rows):
    n = len(order)
    table = []
    for core in range(2):
        for m in range(n):
            p, sign = order.index(m), 1 - 2 * core

            def row(c, shift):
                return (c * n + order[(p + shift) % n]) * rows

            line = [row(core, 0), row(1 - core, 0)]
            for k in range(1, n // 2):
                line += [row(core, -sign * k), row(1 - core, sign * k)]
                line += [row(core, sign * k), row(1 - core, -sign * k)]
            line += [row(core, n // 2), row(1 - core, n // 2), core]
            table.append(line)
    return np.array(table, np.int32)


def split(value):
    high = value.astype(jnp.bfloat16)
    return high, (value - high.astype(jnp.float32)).astype(jnp.bfloat16)


def gradients(pre, cotangents, both):
    hidden = both.shape[1] // 2
    for i, cotangent in enumerate(cotangents):
        here = slice(i * CHUNK, (i + 1) * CHUNK)
        gate = pre[here, :hidden]
        up = pre[here, hidden : 2 * hidden]
        sig = 0.5 * (1.0 + jnp.tanh(0.5 * gate))
        scaled = cotangent().astype(jnp.float32) * sig
        both[here, hidden:] = (scaled * gate).astype(jnp.bfloat16)
        both[here, :hidden] = (scaled * up * (1.0 + gate * (1.0 - sig))).astype(jnp.bfloat16)


def sketch_of(starts, rows, lengths, pre, both, diagonal):
    grads = jnp.dot(both[...], diagonal[...], preferred_element_type=jnp.float32)
    grads_high, grads_low = split(grads)
    grads_both = jnp.concatenate([grads_high, grads_low], axis=1)
    seq_count = lengths.shape[0]
    acts = pre[:, both.shape[1] :]
    position = []
    for start in starts:
        position.append(start + lax.broadcasted_iota(jnp.int32, (rows, LANES), 0))
    position = jnp.concatenate(position, axis=0)
    low = lax.broadcasted_iota(jnp.int32, (1, LANES), 1) < LANES // 2
    ends = []
    for s in range(seq_count):
        ends.append(lengths[s] + (ends[-1] if s else 0))
    highs, lows = [], []
    for g in range(seq_count // 2):
        begin = jnp.where(low, ends[2 * g - 1] if g else 0, ends[2 * g])
        end = jnp.where(low, ends[2 * g], ends[2 * g + 1])
        weighted = jnp.where((position >= begin) & (position < end), acts, 0.0)
        high, rest = split(weighted)
        highs.append(high)
        lows.append(rest)
    over_rows = (((0,), (0,)), ((), ()))
    main = lax.dot_general(
        jnp.concatenate(highs, axis=1),
        grads_both,
        over_rows,
        preferred_element_type=jnp.float32,
    )
    rest = lax.dot_general(
        jnp.concatenate(lows, axis=1), grads_high, over_rows, preferred_element_type=jnp.float32
    )
    return main[:, :LANES] + main[:, LANES:] + rest


def small_kernel(table, lengths, out_grad_hbm, proj_out_hbm, out_grad, diagonal, sems):
    hidden = proj_out_hbm.shape[0]
    upper = pltpu.make_async_copy(proj_out_hbm, diagonal.at[pl.ds(0, hidden)], sems.at[0])
    whole = pltpu.make_async_copy(out_grad_hbm, out_grad, sems.at[1])
    upper.start()
    whole.start()
    upper.wait()
    values = diagonal[:hidden, :]
    left = lax.broadcasted_iota(jnp.int32, values.shape, 1) < LANES // 2
    none = jnp.zeros_like(values)
    diagonal[hidden:, :] = jnp.where(left, none, values)
    diagonal[:hidden, :] = jnp.where(left, values, none)
    whole.wait()


def load_kernel(lengths, diagonal, gate_hbm, up_hbm, proj_in, w, total, sems):
    hidden = gate_hbm.shape[1]
    copies = [
        pltpu.make_async_copy(gate_hbm, w.at[:, pl.ds(0, hidden)], sems.at[0]),
        pltpu.make_async_copy(up_hbm, w.at[:, pl.ds(hidden, hidden)], sems.at[1]),
    ]
    for copy in copies:
        copy.start()
    w[:, 2 * hidden :] = jnp.concatenate([proj_in[...], proj_in[...]], axis=1)
    total[...] = jnp.zeros_like(total)
    for copy in copies:
        copy.wait()


def cotangent_chunks(out_grad, starts, rows):
    chunks = []
    for start in starts:
        for row in range(0, rows, CHUNK):
            here = pl.ds(pl.multiple_of(start + row, CHUNK), CHUNK)
            chunks.append(lambda here=here: out_grad[here, :])
    return chunks


def step_kernel(entry, last, table, lengths, one, two, w, out_grad, diagonal, before, *refs):
    outs, (pre, both) = refs[:-2], refs[-2:]
    rows = one.shape[0]
    starts = [table[entry], table[entry + 1]]
    x = jnp.concatenate([one[...], two[...]], axis=0)
    pre[...] = jnp.dot(x, w[...], preferred_element_type=jnp.float32)
    gradients(pre, cotangent_chunks(out_grad, starts, rows), both)
    total = before[...] + sketch_of(starts, rows, lengths, pre, both, diagonal)
    if not last:
        outs[0][...] = total
        return
    kept, sent = outs
    core = table[table.shape[0] - 1]
    half = total.shape[0] // 2
    upper, lower = total[:half, :], total[half:, :]
    kept[...] = jnp.where(core == 0, upper, lower)
    sent[...] = jnp.where(core == 0, lower, upper)


def costs(rows, width, columns):
    return pl.CostEstimate(
        flops=4 * rows * width * columns, bytes_accessed=2 * rows * width, transcendentals=0
    )


def load_small(table, lengths, out_grad, proj_out):
    out_grad, proj_out = [
        pltpu.with_memory_space_constraint(a, pltpu.HBM) for a in (out_grad, proj_out)
    ]
    hidden = out_grad.shape[1]
    return pl.pallas_call(
        small_kernel,
        out_shape=[
            pltpu.VMEM(out_grad.shape, jnp.bfloat16),
            pltpu.VMEM((2 * hidden, LANES), jnp.bfloat16),
        ],
        in_specs=[SMEM, SMEM, ANY, ANY],
        out_specs=[VMEM] * 2,
        scratch_shapes=[pltpu.SemaphoreType.DMA((2,))],
        compiler_params=pltpu.CompilerParams(vmem_limit_bytes=16 * 2**20),
    )(table, lengths, out_grad, proj_out)


def load(lengths, diagonal, w_gate, w_up, proj_in):
    width, hidden = w_gate.shape
    w_gate, w_up = [pltpu.with_memory_space_constraint(a, pltpu.HBM) for a in (w_gate, w_up)]
    return pl.pallas_call(
        load_kernel,
        out_shape=[
            pltpu.VMEM((width, 2 * hidden + LANES), jnp.bfloat16),
            jax.ShapeDtypeStruct((lengths.shape[0] * LANES // 2, LANES), jnp.float32),
        ],
        in_specs=[SMEM, VMEM, ANY, ANY, VMEM],
        out_specs=[VMEM] * 2,
        scratch_shapes=[pltpu.SemaphoreType.DMA((2,))],
        compiler_params=pltpu.CompilerParams(vmem_limit_bytes=16 * 2**20),
    )(lengths, diagonal, w_gate, w_up, proj_in)


def add_step(blocks, entry, total, table, lengths, weights, last=False):
    rows, width = blocks[0].shape
    w, _, diagonal = weights
    operands = [*blocks, *weights, total]
    out_rows = lengths.shape[0] * LANES // 2
    out_shape = [jax.ShapeDtypeStruct((out_rows, LANES), jnp.float32)]
    if last:
        out_shape = [jax.ShapeDtypeStruct((out_rows // 2, LANES), jnp.float32)] * 2
    outs = pl.pallas_call(
        functools.partial(step_kernel, entry, last),
        out_shape=out_shape,
        in_specs=[SMEM, SMEM] + [VMEM] * len(operands),
        out_specs=[VMEM] * len(out_shape),
        scratch_shapes=[
            pltpu.VMEM((2 * rows, w.shape[1]), jnp.float32),
            pltpu.VMEM((2 * rows, diagonal.shape[0]), jnp.bfloat16),
        ],
        compiler_params=pltpu.CompilerParams(vmem_limit_bytes=16 * 2**20),
        cost_estimate=costs(2 * rows, width, w.shape[1]),
    )(table, lengths, *operands)
    return outs if last else outs[0]


def score_kernel(table, mine, theirs, val_own, val_other, scores, sketch):
    core = table[table.shape[0] - 1]
    sketch[...] = mine[...] + theirs[...].astype(jnp.float32)
    own, rank = scores.shape[0], sketch.shape[0] // scores.shape[0]
    half = rank // 2
    left = lax.broadcasted_iota(jnp.int32, (own, LANES), 1) < LANES // 2
    squares = jnp.zeros((own, LANES), jnp.float32)
    rows = []
    for side in (core, 1 - core):
        gates, ups = [], []
        for a in range(half):
            slab = sketch[pl.ds(side * half + a, own, stride=rank), :]
            squares += slab * slab
            gates.append(jnp.where(left, slab, 0.0))
            ups.append(jnp.where(left, 0.0, slab))
        rows += [*split(jnp.concatenate(gates, axis=1)), *split(jnp.concatenate(ups, axis=1))]
    products = lax.dot_general(
        jnp.concatenate([val_own[...], val_other[...]], axis=0),
        jnp.concatenate(rows, axis=0),
        (((1,), (1,)), ((), ())),
        preferred_element_type=jnp.float32,
    ).T
    columns = scores.shape[1]
    found = products[: 4 * own, :columns] + products[4 * own :, columns:]
    count = rank * LANES // 2
    gate_mean = jnp.sum(jnp.where(left, squares, 0.0), axis=1, keepdims=True) / count
    up_mean = jnp.sum(jnp.where(left, 0.0, squares), axis=1, keepdims=True) / count
    gate_part = found[:own] + found[own : 2 * own]
    up_part = found[2 * own : 3 * own] + found[3 * own :]
    scores[...] = gate_part / jnp.sqrt(gate_mean + eps_scale) + up_part / jnp.sqrt(
        up_mean + eps_scale
    )


def score(table, mine, theirs, val_own, val_other, own):
    return pl.pallas_call(
        score_kernel,
        out_shape=jax.ShapeDtypeStruct((own, val_own.shape[0]), jnp.float32),
        in_specs=[SMEM, VMEM, VMEM, VMEM, VMEM],
        out_specs=VMEM,
        scratch_shapes=[pltpu.VMEM(mine.shape, jnp.float32)],
        compiler_params=pltpu.CompilerParams(vmem_limit_bytes=16 * 2**20),
    )(table, mine, theirs, val_own, val_other)


def fast(order, tokens_in, out_grad, w_gate, w_up, proj_in, proj_out, lengths, val_sketch):
    n = len(order)
    rows = tokens_in.shape[0]
    seq_count = lengths.shape[0]
    table = ring_table(order, rows)
    device = lax.axis_index("seq") * n + lax.axis_index("mp")
    table = lax.dynamic_index_in_dim(jnp.asarray(table), device, 0, keepdims=False)
    ahead = [(order[i], order[(i + 1) % n]) for i in range(n)]
    one = ahead + [(n + b, n + a) for a, b in ahead]
    send_one = functools.partial(lax.ppermute, axis_name=("seq", "mp"), perm=one)
    send_two = functools.partial(
        lax.ppermute, axis_name=("seq", "mp"), perm=[(b, a) for a, b in one]
    )
    swap = functools.partial(lax.ppermute, axis_name="seq", perm=[(0, 1), (1, 0)])

    after = lax.optimization_barrier
    one_way = send_one(tokens_in)
    other, other_val = swap(tokens_in), swap(val_sketch)
    out_grad, diagonal = load_small(table, lengths, out_grad, proj_out)
    later_tokens, diagonal = after((tokens_in, diagonal))
    two_way = send_two(later_tokens)
    w, total = load(lengths, diagonal, w_gate, w_up, proj_in)
    add = functools.partial(
        add_step, table=table, lengths=lengths, weights=[w, out_grad, diagonal]
    )

    waiting, entry = (tokens_in, other), 0
    for k in range(1, n // 2):
        one_way, total = after((one_way, total))
        next_one = send_one(one_way)
        swapped_one = swap(one_way)
        total = add(waiting, entry, total)
        two_way, total, other_val = after((two_way, total, other_val))
        next_two = send_two(two_way) if k + 1 < n // 2 else None
        total = add([one_way, swapped_one], entry + 2, total)
        entry += 4
        waiting = (two_way, swap(two_way))
        one_way, two_way = next_one, next_two
    one_way, total = after((one_way, total))
    swapped_one = swap(one_way)
    total = add(waiting, entry, total)
    kept, sent = add([one_way, swapped_one], entry + 2, total, last=True)

    mine, theirs = kept, swap(sent)
    bit = 1
    while bit < n:
        mine = mine + theirs
        sent = mine.astype(jnp.bfloat16)
        exchange = [bit]
        if bit == 1 and n >= 8:
            exchange = [3, 2, 1]
        got = [
            lax.ppermute(sent, "mp", [(i, i ^ flip) for i in range(n)]) for flip in exchange
        ]
        for part in got[:-1]:
            mine = mine + part.astype(jnp.float32)
        theirs = got[-1]
        bit = 4 if len(exchange) > 1 else 2 * bit
        if bit < n:
            theirs = theirs.astype(jnp.float32)
    return score(table, mine, theirs, val_sketch, other_val, seq_count // 2)


def grad_rows(rows, cotangent, w_gate, w_up, proj_out):
    half_cols = proj_out.shape[1] // 2
    gate_pre = jnp.dot(rows, w_gate, preferred_element_type=jnp.float32)
    up_pre = jnp.dot(rows, w_up, preferred_element_type=jnp.float32)
    cotangent = cotangent.astype(jnp.float32)
    sigmoid_gate = jax.nn.sigmoid(gate_pre)
    grad_up = (cotangent * gate_pre * sigmoid_gate).astype(jnp.bfloat16)
    grad_gate = (
        cotangent * up_pre * sigmoid_gate * (1.0 + gate_pre * (1.0 - sigmoid_gate))
    ).astype(jnp.bfloat16)
    proj_gate = jnp.dot(grad_gate, proj_out[:, :half_cols], preferred_element_type=jnp.float32)
    proj_up = jnp.dot(grad_up, proj_out[:, half_cols:], preferred_element_type=jnp.float32)
    return jnp.concatenate([proj_gate, proj_up], axis=1)


def plain(order, tokens_in, out_grad, w_gate, w_up, proj_in, proj_out, lengths, val_sketch):
    n = len(order)
    rows = tokens_in.shape[0]
    seq_count = lengths.shape[0]
    rank = proj_in.shape[1]
    x = lax.all_gather(tokens_in, ("seq", "mp"), axis=0, tiled=True)
    grads = grad_rows(x, out_grad, w_gate, w_up, proj_out)
    acts = jnp.dot(x, proj_in, preferred_element_type=jnp.float32)
    ends = jnp.cumsum(lengths)
    position = lax.iota(jnp.int32, x.shape[0])[:, None]
    member = ((position >= (ends - lengths)[None, :]) & (position < ends[None, :])).astype(
        jnp.float32
    )
    weighted = (member[:, :, None] * acts[:, None, :]).reshape(x.shape[0], seq_count * rank)
    sketch = lax.dot_general(
        weighted, grads, (((0,), (0,)), ((), ())), precision=lax.Precision.HIGHEST
    )
    sketch = lax.psum(sketch, ("seq", "mp"))
    own = seq_count // lax.axis_size("seq")
    layered = sketch.reshape(seq_count, rank, 2, rank)
    layered = lax.dynamic_slice_in_dim(layered, lax.axis_index("seq") * own, own, 0)
    norm_scale = jnp.sqrt(jnp.mean(layered * layered, axis=(1, 3)) + eps_scale)
    normed = (layered / norm_scale[:, None, :, None]).reshape(own, 2 * rank * rank)
    full_val = lax.all_gather(val_sketch, "seq", axis=1, tiled=True)
    return lax.dot_general(
        normed,
        full_val.astype(jnp.float32),
        (((1,), (1,)), ((), ())),
        precision=lax.Precision.HIGHEST,
    )


def shards(order, tokens_in, out_grad, w_gate, w_up, proj_in, proj_out, lengths, val_sketch):
    n = len(order)
    rows, width = tokens_in.shape
    fits = (
        n >= 2
        and n & (n - 1) == 0
        and lax.axis_size("seq") == 2
        and rows % CHUNK == 0
        and w_gate.shape[1] % LANES == 0
        and width % LANES == 0
        and 2 * proj_in.shape[1] == LANES
        and lengths.shape[0] % 4 == 0
        and val_sketch.shape[1] == proj_in.shape[1] * LANES // 2
    )
    work = fast if fits else plain
    return work(
        order, tokens_in, out_grad, w_gate, w_up, proj_in, proj_out, lengths, val_sketch
    )


def solution(mesh):
    in_specs = (
        P(("groups", "seq", "mp"), None),
        P("groups", ("seq", "mp")),
        P(None, ("seq", "mp")),
        P(None, ("seq", "mp")),
        P(),
        P(("seq", "mp"), None),
        P("groups"),
        P("mp", "seq"),
    )
    out_specs = P(("groups", "seq"), "mp")
    return jax.shard_map(
        functools.partial(shards, ring_order(mesh)),
        mesh=mesh,
        in_specs=in_specs,
        out_specs=out_specs,
        check_vma=False,
    )
```
